32 devices in a mesh: beams: 2 (over y), tm: 4 (over x, core), band: 4 (over z).
Axes of the slice: x: 2, y: 2, z: 4, core: 2. Of those that a mesh axis runs over, the one named last changes fastest.
Arguments:
- signal: float32 [512, 131072], P(('beams', 'band'), 'tm'), parts along dimension 0, may hold values from -6 to 6
- tree_picks: int32 [2, 8, 256], replicated, may hold values from 0 to 63, as said below
- tree_delays: int32 [8, 256], replicated, may hold values from 0 to 4
- template_bank: float32 [2, 201, 64], replicated, may hold values from -0.75 to 0.75
- template_pick: int32 [8, 64, 2], P(('beams', 'band'), 'tm'), parts along dimension 0, may hold values from 0 to 200
Outputs:
- powers: float32 [8, 64, 2, 65536], P(('beams', 'band'), 'tm'), parts along dimension 0
The draws below stay inside these ranges and needn't reach their ends.
There are 2 independent parts, one for each index of `beams`. The reference program is written for one: setup_inputs(seed, part) draws one part's arguments, and reference() takes and returns one part's arrays. A program takes and returns all parts, laid end to end along the dimension named above; an argument that names none is the same for every part. Nothing has to cross between parts.
Inputs may be any that keep to these rules, and one draw needn't show every extreme that they name: `tree_picks`: entries of section j are below the smaller of 2 to the power j and 64.
All inputs are finite; a program needn't handle non-finite values.
Results may differ from the reference program's by a relative error of at most 0.00007.
Values sent between devices are 32-bit elements; how exact they have to be, the bound alone decides.
A program may use at most 192 MiB of HBM per device.

```python
import math
import jax
import jax.numpy as jnp
from jax import lax

CH_DEV = 64
SAMPLES = 131072
MAXD = 4
TAPS = 64
ZBANK = 201
ZSEL = 2
SUBBANDS = 4
CHANNELS = 256
SECTIONS = 8
FREQS = 65536


def draw_tree_picks(key, part):
    sub_key = jax.random.fold_in(key, 11)
    section_iota = jnp.arange(SECTIONS, dtype=jnp.int32)
    upper_bound = jnp.minimum(jnp.left_shift(jnp.int32(1), section_iota), CH_DEV)
    picks = jax.random.randint(sub_key, (2, SECTIONS, CHANNELS), 0, upper_bound[None, :, None], dtype=jnp.int32)
    return picks.at[:, SECTIONS - 1, 0].set(CH_DEV - 1)


def draw_tree_delays(key, part):
    sub_key = jax.random.fold_in(key, 23)
    delays = jax.random.randint(sub_key, (SECTIONS, CHANNELS), 0, MAXD + 1, dtype=jnp.int32)
    return delays.at[:, 0].set(MAXD)


def with_ends(values, stream_key, smallest, high):
    dims = values.shape
    place = [jax.random.randint(jax.random.fold_in(stream_key, axis), (), 0, dims[axis]) for axis in range(len(dims))]
    values = values.at[tuple(place)].set(smallest)
    longest = dims.index(max(dims))
    place[longest] = (place[longest] + 1) % dims[longest]
    return values.at[tuple(place)].set(high)


def block_scale(rng, dims, pieces, smallest, high):
    level = 1.0
    for position, shards_of in pieces:
        draws = jax.random.uniform(jax.random.fold_in(jax.random.fold_in(rng, 6), position), (shards_of,), jnp.float32, smallest / len(pieces), high / len(pieces))
        level = level * jnp.repeat(jnp.exp(draws), dims[position] // shards_of).reshape((-1,) + (1,) * (len(dims) - 1 - position))
    return level


def scatter_about(rng, extent, width, reach, split=(), kind=jnp.bfloat16):
    factor_of = block_scale(rng, extent, split, -0.22, 0.18) if split else 1.0
    result = jax.random.normal(rng, extent, jnp.float32) * width * factor_of
    return jnp.minimum(jnp.maximum(result, -reach), reach).astype(kind)


def setup_inputs(seed: int = 0, part: int = 0) -> dict:
    key_list = jax.random.split(jax.random.key(seed), 6)
    own_keys = jax.random.split(jax.random.fold_in(key_list[5], part), 6)
    return {
        "signal": scatter_about(own_keys[0], (CHANNELS, SAMPLES), 1.0, 6.0, ((0, 4), (1, 4)), jnp.float32),
        "tree_picks": draw_tree_picks(jax.random.fold_in(key_list[5], 71), part),
        "tree_delays": draw_tree_delays(jax.random.fold_in(key_list[5], 71), part),
        "template_bank": scatter_about(key_list[3], (2, ZBANK, TAPS), 0.125, 0.75, (), jnp.float32),
        "template_pick": with_ends(jax.random.randint(own_keys[4], (SUBBANDS, CH_DEV, ZSEL), 0, ZBANK), jax.random.fold_in(own_keys[4], 1), 0, ZBANK - 1).astype(jnp.int32),
    }


def delayed_rows(upper_rows, delays, out_len):
    total = jnp.zeros((upper_rows.shape[0], out_len), upper_rows.dtype)
    for shift_by in range(MAXD + 1):
        total = total + jnp.where(delays[:, None] == shift_by, upper_rows[:, shift_by:shift_by + out_len], 0.0)
    return total

def group_section(block, section_num, first_row, pick_low, pick_high, delays, out_len):
    row_count = block.shape[0]
    half_size = 1 << section_num
    global_row = first_row + jnp.arange(row_count, dtype=jnp.int32)
    base_row = global_row - global_row % (2 * half_size) + global_row % half_size - global_row % min(half_size, CH_DEV) - first_row
    low_rows = jnp.take(block, (base_row + pick_low).astype(jnp.int32), axis=0)
    high_rows = jnp.take(block, (base_row + half_size + pick_high).astype(jnp.int32), axis=0)
    return low_rows[:, :out_len] + delayed_rows(high_rows, delays.astype(jnp.int32), out_len)

def template_powers(spec_re, spec_im, tmpl_re, tmpl_im):
    trials, freq_count = spec_re.shape
    tap_count = tmpl_re.shape[-1]
    block_count = freq_count // 128
    highest = lax.Precision.HIGHEST

    def windows(spectrum):
        padded = jnp.pad(spectrum, ((0, 0), (tap_count // 2, 128 - tap_count // 2)))
        tiles = padded.reshape(trials, block_count + 1, 128)
        return jnp.concatenate([tiles[:, :-1], tiles[:, 1:, :tap_count]], axis=2)
    lag_matrix = jnp.arange(128 + tap_count, dtype=jnp.int32)[:, None] - jnp.arange(128, dtype=jnp.int32)[None, :]
    in_band = (lag_matrix >= 0) & (lag_matrix < tap_count)
    lag_index = jnp.clip(lag_matrix, 0, tap_count - 1)
    band_re = jnp.where(in_band, tmpl_re[..., lag_index], 0.0)
    band_im = jnp.where(in_band, tmpl_im[..., lag_index], 0.0)
    win_re = windows(spec_re)
    win_im = windows(spec_im)
    out_re = jnp.einsum('tbj,tzji->tzbi', win_re, band_re, precision=highest) - jnp.einsum('tbj,tzji->tzbi', win_im, band_im, precision=highest)
    out_im = jnp.einsum('tbj,tzji->tzbi', win_re, band_im, precision=highest) + jnp.einsum('tbj,tzji->tzbi', win_im, band_re, precision=highest)
    return (out_re * out_re + out_im * out_im).reshape(trials, tmpl_re.shape[1], freq_count)

def reference(signal, tree_picks, tree_delays, template_bank, template_pick):
    channels, samples = signal.shape
    rim_depth = SECTIONS * MAXD
    extended = jnp.concatenate([signal, jnp.zeros((channels, rim_depth), signal.dtype)], axis=1)
    length = samples + rim_depth
    for section_num in range(SECTIONS):
        length = length - MAXD
        extended = group_section(extended, section_num, 0, tree_picks[0, section_num], tree_picks[1, section_num], tree_delays[section_num], length)
    norm_scale = 1.0 / math.sqrt(samples * channels)
    spectrum = jnp.fft.rfft(extended, axis=1)[:, :FREQS] * norm_scale
    spec_re = jnp.real(spectrum).astype(jnp.float32)
    spec_im = jnp.imag(spectrum).astype(jnp.float32)
    picked = template_pick.reshape(channels, ZSEL)
    tmpl_re = template_bank[0][picked]
    tmpl_im = template_bank[1][picked]
    group_size = 8
    group_count = channels // group_size

    def one_group(items):
        return template_powers(items[0], items[1], items[2], items[3])
    grouped = lax.map(one_group, (spec_re.reshape(group_count, group_size, FREQS), spec_im.reshape(group_count, group_size, FREQS), tmpl_re.reshape(group_count, group_size, ZSEL, TAPS), tmpl_im.reshape(group_count, group_size, ZSEL, TAPS)))
    return grouped.reshape(SUBBANDS, CH_DEV, ZSEL, FREQS)
```

```python
import functools
import math

import jax
import jax.numpy as jnp
import ml_dtypes
import numpy as np
from jax import lax
from jax.experimental import pallas as pl
from jax.experimental.pallas import tpu as pltpu
from jax.sharding import PartitionSpec as P

CH_DEV = 64
LOGCD = 6
MAXD = 4
LANES = 128
SUBS = 8
RADIX = 256
LIMIT = 56 * 1024 * 1024
FUSED_LIMIT = 62 * 1024 * 1024
GROUP = 2
AHEAD = 3
MESH = pl.DeviceIdType.MESH


def shifted(value, axis, steps):
    count = lax.axis_size(axis)
    first, last = (max(0, -steps), min(count, count - steps))
    return lax.ppermute(value, axis, [(source, source + steps) for source in range(first, last)])


def tree_kernel(sections, sizes, parts, has_rim, *refs):
    low_ref, high_ref, delay_ref, row_ref = refs[:4]
    xs, refs = refs[4 : 4 + len(parts)], refs[4 + len(parts) :]
    if has_rim:
        rim_ref, refs = refs[0], refs[1:]
    buf_a, buf_b = refs[-2:]
    outs = refs[len(refs) - 2 - len(sizes) : -2]
    rows, _, span = buf_a.shape
    tiles = span // LANES - 1
    lane = lax.broadcasted_iota(jnp.int32, (SUBS, LANES), 1)
    sub = lax.broadcasted_iota(jnp.int32, (SUBS, LANES), 0)

    @pl.loop(0, rows, unroll=4)
    def _(r):
        at = 0
        for x_ref, first in zip(xs, parts):
            count = x_ref.shape[2] - first
            buf_a[r, :, at : at + count] = x_ref[r, :, first:]
            at += count
        if has_rim:
            up = pltpu.roll(xs[0][r, :, 0:LANES], SUBS - 1, 0)
            buf_a[r, :, at : at + LANES] = jnp.where(sub == SUBS - 1, rim_ref[r], up)

    def merge(src, section, r, dst, at, count):
        a = low_ref[section, r]
        b = high_ref[section, r]
        d = delay_ref[section, r]
        turn = (LANES - d) & (LANES - 1)
        keep = lane < LANES - d
        turned = [
            pltpu.roll(src[b, :, i * LANES : (i + 1) * LANES], turn, 1) for i in range(tiles + 1)
        ]
        for i in range(count):
            later = turned[min(i + 1, tiles)]
            dst[at, :, i * LANES : (i + 1) * LANES] = src[
                a, :, i * LANES : (i + 1) * LANES
            ] + jnp.where(keep, turned[i], later)

    src, dst = buf_a, buf_b
    for section in range(sections - 1):

        @pl.loop(0, rows, unroll=16)
        def _(r, src=src, dst=dst, section=section):
            merge(src, section, r, dst, r, tiles + 1)

        src, dst = dst, src
    start = 0
    for size, out in zip(sizes, outs):

        @pl.loop(0, size, unroll=16)
        def _(i, start=start, src=src, out=out):
            merge(src, sections - 1, row_ref[start + i], out, i, tiles)

        start += size


def tree(xs, parts, rim, tables_of, sizes, width, span, place, so_far):
    rows = xs[0].shape[0]
    sections = tables_of[0].shape[0]
    smem = pl.BlockSpec(memory_space=pltpu.SMEM)
    vmem = pl.BlockSpec(memory_space=pltpu.VMEM)
    has_rim = rim is not None
    inputs = [*tables_of, *xs] + ([rim] if has_rim else [])
    known = len(inputs)
    return pl.pallas_call(
        functools.partial(tree_kernel, sections, sizes, parts, has_rim),
        grid=(1,),
        out_shape=[jax.ShapeDtypeStruct((size, SUBS, width), jnp.float32) for size in sizes],
        in_specs=[smem] * 4
        + [vmem] * (known - 4)
        + [pl.BlockSpec(memory_space=pl.ANY)] * len(so_far),
        out_specs=[pl.BlockSpec((size, SUBS, span), lambda i: (0, 0, place)) for size in sizes],
        input_output_aliases={known + i: i for i in range(len(so_far))},
        scratch_shapes=[pltpu.VMEM((rows, SUBS, span + LANES), jnp.float32)] * 2,
        compiler_params=pltpu.CompilerParams(vmem_limit_bytes=LIMIT),
        cost_estimate=pl.CostEstimate(
            flops=rows * SUBS * span * sections * 4,
            bytes_accessed=rows * SUBS * span * 8,
            transcendentals=0,
        ),
        name="tree",
    )(*inputs, *so_far)


def split(value):
    high = value.astype(jnp.bfloat16)
    return high, (value - high.astype(jnp.float32)).astype(jnp.bfloat16)


def fill_bands(u, zsel, high_ref, low_ref):
    for z in range(zsel):
        pair = []
        for part in range(2):
            row = u[2 * z + part : 2 * z + part + 1, :]
            wide = jnp.broadcast_to(row, (RADIX, RADIX))
            band = pltpu.roll(wide, 0, 1, stride=1, stride_axis=0)[:, :LANES]
            pair.append(split(band))
        at = 2 * z * LANES
        for ref, real, imag in (
            (high_ref, pair[0][0], pair[1][0]),
            (low_ref, pair[0][1], pair[1][1]),
        ):
            ref[:RADIX, at : at + LANES] = real
            ref[RADIX:, at : at + LANES] = -imag
            ref[:RADIX, at + LANES : at + 2 * LANES] = imag
            ref[RADIX:, at + LANES : at + 2 * LANES] = real


def bands_kernel(zsel, u_ref, high_ref, low_ref):
    fill_bands(u_ref[0], zsel, high_ref.at[0], low_ref.at[0])


def reversed_taps(picks, template_bank):
    trials, zsel = picks.shape
    taps = template_bank.shape[2]
    onehot = (picks[:, :, None] == jnp.arange(template_bank.shape[1], dtype=jnp.int32)).astype(
        jnp.float32
    )
    reversed_bank = jnp.concatenate(
        [
            template_bank[:, :, :1],
            jnp.zeros(template_bank.shape[:2] + (RADIX - taps,), jnp.float32),
            template_bank[:, :, :0:-1],
        ],
        axis=2,
    )
    u = jnp.einsum("tzk,ckm->tzcm", onehot, reversed_bank, precision=lax.Precision.HIGHEST)
    return u.reshape(trials, 2 * zsel, RADIX)


def bands(picks, template_bank):
    trials, zsel = picks.shape
    u = reversed_taps(picks, template_bank)
    wide = 2 * zsel * LANES
    shape = jax.ShapeDtypeStruct((trials, 2 * RADIX, wide), jnp.bfloat16)
    spec = pl.BlockSpec((1, 2 * RADIX, wide), lambda t: (t, 0, 0))
    return pl.pallas_call(
        functools.partial(bands_kernel, zsel),
        grid=(trials,),
        out_shape=[shape, shape],
        in_specs=[pl.BlockSpec((1, 2 * zsel, RADIX), lambda t: (t, 0, 0))],
        out_specs=[spec, spec],
        compiler_params=pltpu.CompilerParams(vmem_limit_bytes=LIMIT),
        cost_estimate=pl.CostEstimate(
            flops=trials * RADIX * RADIX * 20,
            bytes_accessed=trials * 2 * RADIX * wide * 4,
            transcendentals=0,
        ),
        name="bands",
    )(u)


def tables(samples, channels, width, taps):
    cols = samples // RADIX
    outs = cols // 2
    split_by = width // cols if width % cols == 0 else 1
    place = np.arange(RADIX)
    row_of = split_by * (place % (RADIX // split_by)) + place // (RADIX // split_by)
    freq = (np.arange(RADIX) - taps // 2) % RADIX
    b = np.arange(cols)
    scale = 1.0 / math.sqrt(samples * channels)
    angle = 2.0 * np.pi / RADIX * (row_of[:, None] * freq[None, :] % RADIX)
    first = np.concatenate([np.cos(angle), -np.sin(angle)], axis=1) * scale
    angle = 2.0 * np.pi / samples * (b[:, None] * freq[None, :] % samples)
    tw_cos, tw_sin = np.cos(angle), np.sin(angle)
    angle = 2.0 * np.pi / cols * (np.arange(outs)[:, None] * b[None, :] % cols)
    second = np.concatenate([np.cos(angle), np.sin(angle)], axis=1)

    def parts(value):
        value = value.astype(np.float32)
        high = value.astype(ml_dtypes.bfloat16)
        return high, (value - high.astype(np.float32)).astype(ml_dtypes.bfloat16)

    return (
        *parts(first),
        tw_cos.astype(np.float32),
        tw_sin.astype(np.float32),
        *parts(second),
    )


def dot3(a_high, a_low, b_high, b_low):
    def dot(a, b):
        return jnp.dot(a, b, preferred_element_type=jnp.float32)

    return dot(a_high, b_high) + (dot(a_high, b_low) + dot(a_low, b_high))


def powers_of(x, band_high, band_low, consts, zsel, half_taps, store):
    fh, fl, tc, ts, sh, sl = consts
    cols = tc.shape[0]
    outs = cols // 2
    x_high, x_low = split(x.T)
    first = dot3(x_high, x_low, fh[...], fl[...])
    re, im = first[:, :RADIX], first[:, RADIX:]
    mid_re = re * tc[...] + im * ts[...]
    mid_im = im * tc[...] - re * ts[...]
    re_high, re_low = split(mid_re)
    im_high, im_low = split(mid_im)

    def block(a, b):
        return jnp.concatenate(
            [jnp.concatenate([a, b], axis=1), jnp.concatenate([b, -a], axis=1)], axis=0
        )

    spec = dot3(sh[...], sl[...], block(re_high, im_high), block(re_low, im_low))
    row = lax.broadcasted_iota(jnp.int32, (outs, RADIX), 0)
    lane = lax.broadcasted_iota(jnp.int32, (outs, RADIX), 1)
    even, odd = [], []
    for part in (spec[:, :RADIX], spec[:, RADIX:]):
        down = jnp.where(row == 0, 0.0, pltpu.roll(part, 1, 0))
        up = jnp.where(row == outs - 1, 0.0, pltpu.roll(part, outs - 1, 0))
        here = jnp.where(lane < half_taps, down, part)
        after = jnp.where(lane < half_taps, part, up)
        even.append(here)
        odd += [here[:, LANES:], after[:, :LANES]]
    window = jnp.concatenate(
        [jnp.concatenate(even, axis=1), jnp.concatenate(odd, axis=1)], axis=0
    )
    w_high, w_low = split(window)
    got = dot3(w_high, w_low, band_high, band_low)
    for z in range(zsel):
        at = 2 * z * LANES
        real, imag = got[:, at : at + LANES], got[:, at + LANES : at + 2 * LANES]
        power = real * real + imag * imag
        for e in range(2):
            store(pl.ds(e * zsel + z, outs, 2 * zsel), power[e * outs : (e + 1) * outs])


def spectra_kernel(zsel, half_taps, aliased, *refs):
    x_ref, bh_ref, bl_ref = refs[:3]
    consts = refs[3:9]
    out_ref, done_ref = refs[10:] if aliased else refs[9:]
    done_ref[...] = jnp.zeros_like(done_ref)
    cols = consts[2].shape[0]
    x = x_ref[...]
    x = x.reshape(-1, x.shape[-1])
    if x.shape[1] != cols:
        x = jnp.concatenate(
            [x[:, i * cols : (i + 1) * cols] for i in range(x.shape[1] // cols)], axis=0
        )

    def store(rows, value):
        out_ref[0, rows, :] = value

    powers_of(x, bh_ref[0], bl_ref[0], consts, zsel, half_taps, store)


def spectra(x, band_high, band_low, consts, zsel, taps, trials, first_trial, so_far):
    cols = consts[2].shape[0]
    outs = cols // 2
    rows = 2 * outs * zsel
    if x.shape[-1] % cols == 0:
        here = x.shape[1]
        x_spec = pl.BlockSpec((x.shape[0], 1, SUBS, x.shape[-1]), lambda t: (0, t, 0, 0))
    else:
        here = x.shape[1]
        x = x.transpose(1, 0, 2, 3).reshape(here, RADIX, cols)
        x_spec = pl.BlockSpec((1, RADIX, cols), lambda t: (t, 0, 0))
    band_spec = pl.BlockSpec(
        (1,) + band_high.shape[1:], lambda t: (first_trial + t, 0, 0)
    )
    whole = [pl.BlockSpec(c.shape, lambda t: (0, 0)) for c in consts]
    aliased = so_far is not None
    more = [so_far] if aliased else []
    macs = here * (cols * RADIX * 2 * RADIX + outs * 2 * cols * 2 * RADIX + 2 * outs * 4 * RADIX * RADIX)
    return pl.pallas_call(
        functools.partial(spectra_kernel, zsel, taps // 2, aliased),
        grid=(here,),
        out_shape=[
            jax.ShapeDtypeStruct((trials, rows, LANES), jnp.float32),
            jax.ShapeDtypeStruct((SUBS, LANES), jnp.float32),
        ],
        in_specs=[x_spec, band_spec, band_spec, *whole]
        + [pl.BlockSpec(memory_space=pl.ANY)] * len(more),
        out_specs=[
            pl.BlockSpec((1, rows, LANES), lambda t: (first_trial + t, 0, 0)),
            pl.BlockSpec((SUBS, LANES), lambda t: (0, 0)),
        ],
        input_output_aliases={9: 0} if aliased else {},
        compiler_params=pltpu.CompilerParams(vmem_limit_bytes=LIMIT),
        cost_estimate=pl.CostEstimate(
            flops=6 * macs, bytes_accessed=here * 2 * 1024 * 1024, transcendentals=0
        ),
        name="spectra",
    )(x, band_high, band_low, *consts, *more)


def after_kernel(value_ref, done_ref, out_ref):
    del value_ref, done_ref, out_ref


def after(value, done):
    anywhere = pl.BlockSpec(memory_space=pl.ANY)
    return pl.pallas_call(
        after_kernel,
        out_shape=jax.ShapeDtypeStruct(value.shape, value.dtype),
        in_specs=[anywhere, anywhere],
        out_specs=anywhere,
        input_output_aliases={0: 0},
        name="after",
    )(value, done)


def finish(out, trials, samples, zsel):
    out = out.reshape(trials, samples // 2 // LANES, zsel, LANES).transpose(0, 2, 1, 3)
    return out.reshape(1, trials, zsel, samples // 2)


def fused_kernel(
    nb, nt, sections, trials, zsel, taps,
    picks_ref, delay_ref, u_ref, sig_ref, *refs
):
    const_refs, refs = refs[:6], refs[6:]
    out_ref, refs = refs[0], refs[1:]
    raw, refs = refs[0], refs[1:]
    rim, buf_a, buf_b = refs[:3]
    sent, got, refs = refs[3:5], refs[5:7], refs[7:]
    band_high, band_low, power, refs = refs[0], refs[1], refs[2], refs[3:]
    consts, refs = refs[:6], refs[6:]
    one_send, one_recv, two_send, two_recv, rim_sems, own_one, own_two, const_sems, out_sems = refs

    everyone = nb * nt
    rows, _, span = buf_a.shape
    span = span - LANES
    blocks = CH_DEV // SUBS
    groups = trials // GROUP
    tiles = span // LANES
    early = range(tiles + 1)
    late = range(tiles + 1, 2 * tiles)
    mt, mb = lax.axis_index("tm"), lax.axis_index("band")
    me = mt * nb + mb

    def device(e):
        return {"tm": e // nb, "band": e % nb}

    barrier = pltpu.get_barrier_semaphore()

    @pl.loop(1, everyone)
    def _(d):
        pl.semaphore_signal(
            barrier, 1, device_id=device((me + d) % everyone), device_id_type=MESH
        )

    pl.semaphore_wait(barrier, everyone - 1)

    def slab(i, k):
        return sig_ref.at[:, k, :, pl.ds(i * LANES, LANES)]

    def first(i, d):
        return pltpu.make_async_remote_copy(
            slab(i, (mb + d) % nb),
            raw.at[pl.ds(mb * blocks, blocks), i],
            one_send.at[i, d - 1],
            one_recv.at[i, d - 1],
            device_id={"band": (mb + d) % nb},
            device_id_type=MESH,
        )

    def first_from(i, d):
        source = (mb + nb - d) % nb
        return pltpu.make_async_remote_copy(
            slab(i, mb),
            raw.at[pl.ds(source * blocks, blocks), i],
            one_send.at[i, d - 1],
            one_recv.at[i, d - 1],
            device_id={"band": source},
            device_id_type=MESH,
        )

    def first_own(i):
        return pltpu.make_async_copy(
            slab(i, mb), raw.at[pl.ds(mb * blocks, blocks), i], own_one.at[i]
        )

    def first_wait(i):
        for d in range(1, nb):
            first_from(i, d).wait_recv()
        first_own(i).wait()

    apart = sorted(range(1, nb), key=lambda d: -min(d, nb - d))
    for i in (*early, *late):
        for d in apart:
            first(i, d).start()
        first_own(i).start()
    loads = [
        pltpu.make_async_copy(a, b, const_sems.at[i])
        for i, (a, b) in enumerate(zip(const_refs, consts))
    ]
    for load in loads:
        load.start()

    lane = lax.broadcasted_iota(jnp.int32, (SUBS, LANES), 1)
    sub = lax.broadcasted_iota(jnp.int32, (SUBS, LANES), 0)

    def merge(src, section, r, dst, at, count):
        half = 1 << section
        base = r - r % (2 * half) + r % half - r % min(half, CH_DEV)
        a = base + picks_ref[0, section, r]
        b = base + half + picks_ref[1, section, r]
        d = delay_ref[section, r]
        turn = (LANES - d) & (LANES - 1)
        keep = lane < LANES - d
        turned = [
            pltpu.roll(src[b, :, i * LANES : (i + 1) * LANES], turn, 1) for i in range(tiles + 1)
        ]
        for i in range(count):
            later = turned[min(i + 1, tiles)]
            dst[at, :, i * LANES : (i + 1) * LANES] = src[
                a, :, i * LANES : (i + 1) * LANES
            ] + jnp.where(keep, turned[i], later)

    def tree_part(c):
        @pl.loop(0, nb * blocks)
        def _(q):
            for ch in range(SUBS):
                r = q * SUBS + ch
                rows_of = pl.ds(ch, SUBS, stride=SUBS)
                for i in range(tiles + 1 - c):
                    buf_a[r, :, i * LANES : (i + 1) * LANES] = raw[q, c * tiles + i, rows_of, :]
                if c == 1:
                    up = pltpu.roll(raw[q, 0, rows_of, :], SUBS - 1, 0)
                    edge = jnp.broadcast_to(rim[q, ch : ch + 1, :], (SUBS, LANES))
                    buf_a[r, :, span:] = jnp.where(sub == SUBS - 1, edge, up)

        src, dst = buf_a, buf_b
        for section in range(sections - 1):

            @pl.loop(0, rows, unroll=16)
            def _(r, src=src, dst=dst, section=section):
                merge(src, section, r, dst, r, tiles + 1)

            src, dst = dst, src

        @pl.loop(0, everyone)
        def _(e):
            start = (e % nb) * CH_DEV + (e // nb) * trials

            @pl.loop(0, trials, unroll=trials)
            def _(i):
                merge(src, sections - 1, start + i, sent[c].at[e], i, tiles)

    def second(c, g, d):
        e = (me + d) % everyone
        which = pl.ds(g * GROUP, GROUP) if c else slice(None)
        at = 1 + g if c else 0
        return pltpu.make_async_remote_copy(
            sent[c].at[e, which],
            got[c].at[me, which],
            two_send.at[at, d - 1],
            two_recv.at[at, d - 1],
            device_id=device(e),
            device_id_type=MESH,
        )

    def second_from(c, g, d):
        e = (me + everyone - d) % everyone
        which = pl.ds(g * GROUP, GROUP) if c else slice(None)
        at = 1 + g if c else 0
        return pltpu.make_async_remote_copy(
            sent[c].at[e, which],
            got[c].at[e, which],
            two_send.at[at, d - 1],
            two_recv.at[at, d - 1],
            device_id=device(e),
            device_id_type=MESH,
        )

    def second_own(c):
        return pltpu.make_async_copy(sent[c].at[me], got[c].at[me], own_two.at[c])

    def send_second(c, g):
        @pl.loop(1, everyone)
        def _(d):
            second(c, g, d).start()

    for i in early:
        first_wait(i)
    rim_copy = pltpu.make_async_remote_copy(
        raw.at[:, 0, pl.ds(0, SUBS)],
        rim,
        rim_sems.at[0],
        rim_sems.at[1],
        device_id=device((me + everyone - 1) % everyone),
        device_id_type=MESH,
    )

    @pl.when(me > 0)
    def _():
        rim_copy.start()

    @pl.when(me == everyone - 1)
    def _():
        rim[...] = jnp.zeros_like(rim)

    tree_part(0)
    send_second(0, 0)
    second_own(0).start()
    for i in late:
        first_wait(i)

    @pl.when(me < everyone - 1)
    def _():
        rim_copy.wait_recv()

    tree_part(1)
    second_own(1).start()
    for g in range(min(AHEAD, groups)):
        send_second(1, g)
    for i in (*early, *late):
        for d in range(1, nb):
            first(i, d).wait_send()

    @pl.when(me > 0)
    def _():
        rim_copy.wait_send()

    for load in loads:
        load.wait()
    second_own(0).wait()
    second_own(1).wait()

    @pl.loop(1, everyone)
    def _(d):
        second_from(0, 0, d).wait_recv()
        second(0, 0, d).wait_send()

    cols = consts[2].shape[0]

    def out_copy(t, j):
        return pltpu.make_async_copy(power.at[j], out_ref.at[t], out_sems.at[j])

    @pl.loop(0, groups)
    def _(g):
        for j in range(GROUP):
            fill_bands(u_ref[g * GROUP + j], zsel, band_high.at[j], band_low.at[j])

        @pl.loop(1, everyone)
        def _(d):
            second_from(1, g, d).wait_recv()
            second(1, g, d).wait_send()

        @pl.when(g + AHEAD < groups)
        def _():
            send_second(1, g + AHEAD)

        for j in range(GROUP):
            t = g * GROUP + j
            parts = [got[c][:, t].reshape(everyone * SUBS, span) for c in range(2)]
            x = jnp.concatenate(
                [part[:, i : i + cols] for part in parts for i in range(0, span, cols)], axis=0
            )

            @pl.when(g > 0)
            def _(j=j, t=t):
                out_copy(t - GROUP, j).wait()

            def store(where, value, j=j):
                power[j, where, :] = value

            powers_of(x, band_high[j], band_low[j], consts, zsel, taps // 2, store)
            out_copy(t, j).start()

    for j in range(GROUP):
        out_copy(trials - GROUP + j, j).wait()


def fused(signal, picks, delays, u, consts, zsel, taps, nb, nt):
    sections = picks.shape[1]
    channels = CH_DEV * nb
    everyone = nb * nt
    trials = CH_DEV // nt
    slab = signal.shape[1] // nb
    width = slab // SUBS
    span = width // 2
    blocks = CH_DEV // SUBS
    cols = consts[2].shape[0]
    outs = cols // 2
    rows = 2 * outs * zsel
    groups = trials // GROUP
    wide = 2 * zsel * LANES
    view = signal.reshape(blocks, SUBS, nb * SUBS, width).transpose(0, 2, 1, 3)
    view = view.reshape(blocks, nb, SUBS * SUBS, width)
    smem = pl.BlockSpec(memory_space=pltpu.SMEM)
    vmem = pl.BlockSpec(memory_space=pltpu.VMEM)
    anywhere = pl.BlockSpec(memory_space=pl.ANY)
    dma = pltpu.SemaphoreType.DMA
    f32 = jnp.float32
    macs = trials * (cols * RADIX * 2 * RADIX + outs * 2 * cols * 2 * RADIX + 2 * outs * 4 * RADIX * RADIX)
    return pl.pallas_call(
        functools.partial(fused_kernel, nb, nt, sections, trials, zsel, taps),
        out_shape=jax.ShapeDtypeStruct((trials, rows, LANES), f32),
        in_specs=[smem, smem, vmem] + [anywhere] * 7,
        out_specs=anywhere,
        scratch_shapes=[
            pltpu.VMEM((nb * blocks, width // LANES, SUBS * SUBS, LANES), f32),
            pltpu.VMEM((nb * blocks, SUBS, LANES), f32),
            pltpu.VMEM((channels, SUBS, span + LANES), f32),
            pltpu.VMEM((channels, SUBS, span + LANES), f32),
            pltpu.VMEM((everyone, trials, SUBS, span), f32),
            pltpu.VMEM((everyone, trials, SUBS, span), f32),
            pltpu.VMEM((everyone, trials, SUBS, span), f32),
            pltpu.VMEM((everyone, trials, SUBS, span), f32),
            pltpu.VMEM((GROUP, 2 * RADIX, wide), jnp.bfloat16),
            pltpu.VMEM((GROUP, 2 * RADIX, wide), jnp.bfloat16),
            pltpu.VMEM((GROUP, rows, LANES), f32),
            *[pltpu.VMEM(c.shape, c.dtype) for c in consts],
            dma((width // LANES, nb - 1)),
            dma((width // LANES, nb - 1)),
            dma((1 + groups, everyone - 1)),
            dma((1 + groups, everyone - 1)),
            dma((2,)),
            dma((width // LANES,)),
            dma((2,)),
            dma((len(consts),)),
            dma((GROUP,)),
        ],
        compiler_params=pltpu.CompilerParams(
            collective_id=0, has_side_effects=True, vmem_limit_bytes=FUSED_LIMIT
        ),
        cost_estimate=pl.CostEstimate(
            flops=6 * macs, bytes_accessed=3 * signal.size * 4, transcendentals=0
        ),
        name="fused",
    )(picks, delays, u, view, *consts)


def on_device(signal, tree_picks, tree_delays, template_bank, template_pick):
    band_count = lax.axis_size("band")
    time_count = lax.axis_size("tm")
    everyone = band_count * time_count
    sections = LOGCD + band_count.bit_length() - 1
    rim_depth = sections * MAXD
    channels = CH_DEV * band_count
    samples = signal.shape[1] * time_count
    slab = signal.shape[1] // band_count
    width = slab // SUBS
    trials = CH_DEV // time_count
    last = max(1, 3 * trials // 16)
    counts = [count for count in (trials - last, last) if count]
    zsel = template_pick.shape[2]
    taps = template_bank.shape[2]
    cols = samples // RADIX
    if width % (2 * cols) == 0 and trials % GROUP == 0:
        u = reversed_taps(template_pick[0], template_bank)
        consts = [jnp.asarray(c) for c in tables(samples, channels, width, taps)]
        out = fused(signal, tree_picks, tree_delays, u, consts, zsel, taps, band_count, time_count)
        return finish(out, trials, samples, zsel)

    band_high, band_low = bands(template_pick[0], template_bank)

    half = (1 << np.arange(sections))[:, None]
    r = np.arange(channels)[None, :]
    base = r - r % (2 * half) + r % half - r % np.minimum(half, CH_DEV)
    low = tree_picks[0] + base.astype(np.int32)
    high = tree_picks[1] + (base + half).astype(np.int32)
    grid = np.arange(channels).reshape(band_count, time_count, trials).transpose(1, 0, 2)
    firsts = [sum(counts[:q]) for q in range(len(counts))]
    order = np.concatenate(
        [grid[:, :, first : first + count].reshape(-1) for first, count in zip(firsts, counts)]
    ).astype(np.int32)
    tables_of = (low, high, tree_delays, jnp.asarray(order))
    sizes = [everyone * count for count in counts]

    folded = signal.reshape(CH_DEV, band_count, SUBS, width)

    def exchanged(value):
        value = lax.all_to_all(value, "band", split_axis=0, concat_axis=0, tiled=True)
        return value.reshape(channels, SUBS, -1)

    def rim_of(x):
        rim = shifted(x[:, 0, :rim_depth], ("tm", "band"), -1)
        rim = jnp.pad(rim, ((0, 0), (0, LANES - rim_depth)))
        return jnp.broadcast_to(rim[:, None, :], (channels, SUBS, LANES))

    if width % (2 * LANES) == 0:
        span = width // 2
        cut = span + LANES
        x_a = exchanged(folded[..., :cut].transpose(1, 0, 2, 3))
        x_b = after(after(folded[..., cut:].transpose(1, 0, 2, 3), x_a), band_low)
        x_b = exchanged(x_b)
        pieces = tree([x_a], [0], None, tables_of, sizes, width, span, 0, [])
        pieces = tree(
            [x_a, x_b], [span, 0], rim_of(x_a), tables_of, sizes, width, span, 1, pieces
        )
    else:
        x = exchanged(folded.transpose(1, 0, 2, 3))
        pieces = tree([x], [0], rim_of(x), tables_of, sizes, width, width, 0, [])

    consts = [jnp.asarray(c) for c in tables(samples, channels, width, taps)]
    out = None
    for first, count, piece in zip(firsts, counts, pieces):
        piece = piece.reshape(everyone, count, SUBS, width)
        if out is not None:
            piece = after(piece, arrived)
        arrived = lax.all_to_all(piece, ("tm", "band"), split_axis=0, concat_axis=0, tiled=True)
        out, _ = spectra(
            arrived, band_high, band_low, consts, zsel, taps, trials, first, out
        )
    return finish(out, trials, samples, zsel)


def solution(mesh):
    in_specs = (P(("beams", "band"), "tm"), P(), P(), P(), P(("beams", "band"), "tm", None))
    out_specs = P(("beams", "band"), "tm", None, None)
    return jax.shard_map(
        on_device, mesh=mesh, in_specs=in_specs, out_specs=out_specs, check_vma=False
    )
```

```python
import functools
import math

import jax
import jax.numpy as jnp
import ml_dtypes
import numpy as np
from jax import lax
from jax.experimental import pallas as pl
from jax.experimental.pallas import tpu as pltpu
from jax.sharding import PartitionSpec as P

CH_DEV = 64
LOGCD = 6
MAXD = 4
LANES = 128
SUBS = 8
RADIX = 256
LIMIT = 56 * 1024 * 1024
FUSED_LIMIT = 62 * 1024 * 1024
AHEAD = 6
MESH = pl.DeviceIdType.MESH


def shifted(value, axis, steps):
    count = lax.axis_size(axis)
    first, last = (max(0, -steps), min(count, count - steps))
    return lax.ppermute(value, axis, [(source, source + steps) for source in range(first, last)])


def tree_kernel(sections, sizes, parts, has_rim, *refs):
    low_ref, high_ref, delay_ref, row_ref = refs[:4]
    xs, refs = refs[4 : 4 + len(parts)], refs[4 + len(parts) :]
    if has_rim:
        rim_ref, refs = refs[0], refs[1:]
    buf_a, buf_b = refs[-2:]
    outs = refs[len(refs) - 2 - len(sizes) : -2]
    rows, _, span = buf_a.shape
    tiles = span // LANES - 1
    lane = lax.broadcasted_iota(jnp.int32, (SUBS, LANES), 1)
    sub = lax.broadcasted_iota(jnp.int32, (SUBS, LANES), 0)

    @pl.loop(0, rows, unroll=4)
    def _(r):
        at = 0
        for x_ref, first in zip(xs, parts):
            count = x_ref.shape[2] - first
            buf_a[r, :, at : at + count] = x_ref[r, :, first:]
            at += count
        if has_rim:
            up = pltpu.roll(xs[0][r, :, 0:LANES], SUBS - 1, 0)
            buf_a[r, :, at : at + LANES] = jnp.where(sub == SUBS - 1, rim_ref[r], up)

    def merge(src, section, r, dst, at, count):
        a = low_ref[section, r]
        b = high_ref[section, r]
        d = delay_ref[section, r]
        turn = (LANES - d) & (LANES - 1)
        keep = lane < LANES - d
        turned = [
            pltpu.roll(src[b, :, i * LANES : (i + 1) * LANES], turn, 1) for i in range(tiles + 1)
        ]
        for i in range(count):
            later = turned[min(i + 1, tiles)]
            dst[at, :, i * LANES : (i + 1) * LANES] = src[
                a, :, i * LANES : (i + 1) * LANES
            ] + jnp.where(keep, turned[i], later)

    src, dst = buf_a, buf_b
    for section in range(sections - 1):

        @pl.loop(0, rows, unroll=16)
        def _(r, src=src, dst=dst, section=section):
            merge(src, section, r, dst, r, tiles + 1)

        src, dst = dst, src
    start = 0
    for size, out in zip(sizes, outs):

        @pl.loop(0, size, unroll=16)
        def _(i, start=start, src=src, out=out):
            merge(src, sections - 1, row_ref[start + i], out, i, tiles)

        start += size


def tree(xs, parts, rim, tables_of, sizes, width, span, place, so_far):
    rows = xs[0].shape[0]
    sections = tables_of[0].shape[0]
    smem = pl.BlockSpec(memory_space=pltpu.SMEM)
    vmem = pl.BlockSpec(memory_space=pltpu.VMEM)
    has_rim = rim is not None
    inputs = [*tables_of, *xs] + ([rim] if has_rim else [])
    known = len(inputs)
    return pl.pallas_call(
        functools.partial(tree_kernel, sections, sizes, parts, has_rim),
        grid=(1,),
        out_shape=[jax.ShapeDtypeStruct((size, SUBS, width), jnp.float32) for size in sizes],
        in_specs=[smem] * 4
        + [vmem] * (known - 4)
        + [pl.BlockSpec(memory_space=pl.ANY)] * len(so_far),
        out_specs=[pl.BlockSpec((size, SUBS, span), lambda i: (0, 0, place)) for size in sizes],
        input_output_aliases={known + i: i for i in range(len(so_far))},
        scratch_shapes=[pltpu.VMEM((rows, SUBS, span + LANES), jnp.float32)] * 2,
        compiler_params=pltpu.CompilerParams(vmem_limit_bytes=LIMIT),
        cost_estimate=pl.CostEstimate(
            flops=rows * SUBS * span * sections * 4,
            bytes_accessed=rows * SUBS * span * 8,
            transcendentals=0,
        ),
        name="tree",
    )(*inputs, *so_far)


def split(value):
    high = value.astype(jnp.bfloat16)
    return high, (value - high.astype(jnp.float32)).astype(jnp.bfloat16)


def fill_bands(row_of, zsel, high_ref, low_ref):
    for z in range(zsel):
        pair = []
        for part in range(2):
            wide = jnp.broadcast_to(row_of(z, part), (RADIX, RADIX))
            band = pltpu.roll(wide, 0, 1, stride=1, stride_axis=0)[:, :LANES]
            pair.append(split(band))
        at = 2 * z * LANES
        for ref, real, imag in (
            (high_ref, pair[0][0], pair[1][0]),
            (low_ref, pair[0][1], pair[1][1]),
        ):
            ref[:RADIX, at : at + LANES] = real
            ref[RADIX:, at : at + LANES] = -imag
            ref[:RADIX, at + LANES : at + 2 * LANES] = imag
            ref[RADIX:, at + LANES : at + 2 * LANES] = real


def bands_kernel(zsel, u_ref, high_ref, low_ref):
    def row_of(z, part):
        return u_ref[0, 2 * z + part : 2 * z + part + 1, :]

    fill_bands(row_of, zsel, high_ref.at[0], low_ref.at[0])


def reversed_taps(picks, template_bank):
    trials, zsel = picks.shape
    taps = template_bank.shape[2]
    onehot = (picks[:, :, None] == jnp.arange(template_bank.shape[1], dtype=jnp.int32)).astype(
        jnp.float32
    )
    reversed_bank = jnp.concatenate(
        [
            template_bank[:, :, :1],
            jnp.zeros(template_bank.shape[:2] + (RADIX - taps,), jnp.float32),
            template_bank[:, :, :0:-1],
        ],
        axis=2,
    )
    u = jnp.einsum("tzk,ckm->tzcm", onehot, reversed_bank, precision=lax.Precision.HIGHEST)
    return u.reshape(trials, 2 * zsel, RADIX)


def bands(picks, template_bank):
    trials, zsel = picks.shape
    u = reversed_taps(picks, template_bank)
    wide = 2 * zsel * LANES
    shape = jax.ShapeDtypeStruct((trials, 2 * RADIX, wide), jnp.bfloat16)
    spec = pl.BlockSpec((1, 2 * RADIX, wide), lambda t: (t, 0, 0))
    return pl.pallas_call(
        functools.partial(bands_kernel, zsel),
        grid=(trials,),
        out_shape=[shape, shape],
        in_specs=[pl.BlockSpec((1, 2 * zsel, RADIX), lambda t: (t, 0, 0))],
        out_specs=[spec, spec],
        compiler_params=pltpu.CompilerParams(vmem_limit_bytes=LIMIT),
        cost_estimate=pl.CostEstimate(
            flops=trials * RADIX * RADIX * 20,
            bytes_accessed=trials * 2 * RADIX * wide * 4,
            transcendentals=0,
        ),
        name="bands",
    )(u)


def tables(samples, channels, width, taps):
    cols = samples // RADIX
    outs = cols // 2
    split_by = width // cols if width % cols == 0 else 1
    place = np.arange(RADIX)
    row_of = split_by * (place % (RADIX // split_by)) + place // (RADIX // split_by)
    freq = (np.arange(RADIX) - taps // 2) % RADIX
    b = np.arange(cols)
    scale = 1.0 / math.sqrt(samples * channels)
    angle = 2.0 * np.pi / RADIX * (row_of[:, None] * freq[None, :] % RADIX)
    first = np.concatenate([np.cos(angle), -np.sin(angle)], axis=1) * scale
    angle = 2.0 * np.pi / samples * (b[:, None] * freq[None, :] % samples)
    tw_cos, tw_sin = np.cos(angle), np.sin(angle)
    angle = 2.0 * np.pi / cols * (np.arange(outs)[:, None] * b[None, :] % cols)
    second = np.concatenate([np.cos(angle), np.sin(angle)], axis=1)

    def parts(value):
        value = value.astype(np.float32)
        high = value.astype(ml_dtypes.bfloat16)
        return high, (value - high.astype(np.float32)).astype(ml_dtypes.bfloat16)

    return (
        *parts(first),
        tw_cos.astype(np.float32),
        tw_sin.astype(np.float32),
        *parts(second),
    )


def dot3(a_high, a_low, b_high, b_low):
    def dot(a, b):
        return jnp.dot(a, b, preferred_element_type=jnp.float32)

    return dot(a_high, b_high) + (dot(a_high, b_low) + dot(a_low, b_high))


def powers_of(x, band_high, band_low, consts, zsel, half_taps, store):
    fh, fl, tc, ts, sh, sl = consts
    cols = tc.shape[0]
    outs = cols // 2
    x_high, x_low = split(x.T)
    first = dot3(x_high, x_low, fh[...], fl[...])
    re, im = first[:, :RADIX], first[:, RADIX:]
    mid_re = re * tc[...] + im * ts[...]
    mid_im = im * tc[...] - re * ts[...]
    re_high, re_low = split(mid_re)
    im_high, im_low = split(mid_im)

    def block(a, b):
        return jnp.concatenate(
            [jnp.concatenate([a, b], axis=1), jnp.concatenate([b, -a], axis=1)], axis=0
        )

    spec = dot3(sh[...], sl[...], block(re_high, im_high), block(re_low, im_low))
    row = lax.broadcasted_iota(jnp.int32, (outs, RADIX), 0)
    lane = lax.broadcasted_iota(jnp.int32, (outs, RADIX), 1)
    even, odd = [], []
    for part in (spec[:, :RADIX], spec[:, RADIX:]):
        down = jnp.where(row == 0, 0.0, pltpu.roll(part, 1, 0))
        up = jnp.where(row == outs - 1, 0.0, pltpu.roll(part, outs - 1, 0))
        here = jnp.where(lane < half_taps, down, part)
        after = jnp.where(lane < half_taps, part, up)
        even.append(here)
        odd += [here[:, LANES:], after[:, :LANES]]
    window = jnp.concatenate(
        [jnp.concatenate(even, axis=1), jnp.concatenate(odd, axis=1)], axis=0
    )
    w_high, w_low = split(window)
    got = dot3(w_high, w_low, band_high, band_low)
    for z in range(zsel):
        at = 2 * z * LANES
        real, imag = got[:, at : at + LANES], got[:, at + LANES : at + 2 * LANES]
        power = real * real + imag * imag
        for e in range(2):
            store(pl.ds(e * zsel + z, outs, 2 * zsel), power[e * outs : (e + 1) * outs])


def spectra_kernel(zsel, half_taps, aliased, *refs):
    x_ref, bh_ref, bl_ref = refs[:3]
    consts = refs[3:9]
    out_ref, done_ref = refs[10:] if aliased else refs[9:]
    done_ref[...] = jnp.zeros_like(done_ref)
    cols = consts[2].shape[0]
    x = x_ref[...]
    x = x.reshape(-1, x.shape[-1])
    if x.shape[1] != cols:
        x = jnp.concatenate(
            [x[:, i * cols : (i + 1) * cols] for i in range(x.shape[1] // cols)], axis=0
        )

    def store(rows, value):
        out_ref[0, rows, :] = value

    powers_of(x, bh_ref[0], bl_ref[0], consts, zsel, half_taps, store)


def spectra(x, band_high, band_low, consts, zsel, taps, trials, first_trial, so_far):
    cols = consts[2].shape[0]
    outs = cols // 2
    rows = 2 * outs * zsel
    if x.shape[-1] % cols == 0:
        here = x.shape[1]
        x_spec = pl.BlockSpec((x.shape[0], 1, SUBS, x.shape[-1]), lambda t: (0, t, 0, 0))
    else:
        here = x.shape[1]
        x = x.transpose(1, 0, 2, 3).reshape(here, RADIX, cols)
        x_spec = pl.BlockSpec((1, RADIX, cols), lambda t: (t, 0, 0))
    band_spec = pl.BlockSpec(
        (1,) + band_high.shape[1:], lambda t: (first_trial + t, 0, 0)
    )
    whole = [pl.BlockSpec(c.shape, lambda t: (0, 0)) for c in consts]
    aliased = so_far is not None
    more = [so_far] if aliased else []
    macs = here * (cols * RADIX * 2 * RADIX + outs * 2 * cols * 2 * RADIX + 2 * outs * 4 * RADIX * RADIX)
    return pl.pallas_call(
        functools.partial(spectra_kernel, zsel, taps // 2, aliased),
        grid=(here,),
        out_shape=[
            jax.ShapeDtypeStruct((trials, rows, LANES), jnp.float32),
            jax.ShapeDtypeStruct((SUBS, LANES), jnp.float32),
        ],
        in_specs=[x_spec, band_spec, band_spec, *whole]
        + [pl.BlockSpec(memory_space=pl.ANY)] * len(more),
        out_specs=[
            pl.BlockSpec((1, rows, LANES), lambda t: (first_trial + t, 0, 0)),
            pl.BlockSpec((SUBS, LANES), lambda t: (0, 0)),
        ],
        input_output_aliases={9: 0} if aliased else {},
        compiler_params=pltpu.CompilerParams(vmem_limit_bytes=LIMIT),
        cost_estimate=pl.CostEstimate(
            flops=6 * macs, bytes_accessed=here * 2 * 1024 * 1024, transcendentals=0
        ),
        name="spectra",
    )(x, band_high, band_low, *consts, *more)


def after_kernel(value_ref, done_ref, out_ref):
    del value_ref, done_ref, out_ref


def after(value, done):
    anywhere = pl.BlockSpec(memory_space=pl.ANY)
    return pl.pallas_call(
        after_kernel,
        out_shape=jax.ShapeDtypeStruct(value.shape, value.dtype),
        in_specs=[anywhere, anywhere],
        out_specs=anywhere,
        input_output_aliases={0: 0},
        name="after",
    )(value, done)


def finish(out, trials, samples, zsel):
    out = out.reshape(trials, samples // 2 // LANES, zsel, LANES).transpose(0, 2, 1, 3)
    return out.reshape(1, trials, zsel, samples // 2)


def fused_kernel(
    nb, nt, sections, trials, zsel, taps,
    picks_ref, delay_ref, wanted_ref, bank_ref, sig_ref, *refs
):
    const_refs, refs = refs[:6], refs[6:]
    out_ref, last_x, last_bands, sent, refs = refs[0], refs[1:3], refs[3:5], refs[5:7], refs[7:]
    raw, rim, buf_a, buf_b, stage, refs = *refs[:5], refs[5:]
    got, refs = refs[:2], refs[2:]
    band_high, band_low, power, bank, reverse, refs = *refs[:5], refs[5:]
    consts, refs = refs[:6], refs[6:]
    (
        one_send, one_recv, two_send, two_recv, rim_sems, own_one, own_two, stage_sem,
        load_sems, out_sems, last_sems,
    ) = refs

    everyone = nb * nt
    rows, _, span = buf_a.shape
    span = span - LANES
    blocks = CH_DEV // SUBS
    tiles = span // LANES
    early = range(tiles + 1)
    late = range(tiles + 1, 2 * tiles)
    mt, mb = lax.axis_index("tm"), lax.axis_index("band")
    me = mt * nb + mb

    def device(e):
        return {"tm": e // nb, "band": e % nb}

    barrier = pltpu.get_barrier_semaphore()

    @pl.loop(1, everyone)
    def _(d):
        pl.semaphore_signal(
            barrier, 1, device_id=device((me + d) % everyone), device_id_type=MESH
        )

    pl.semaphore_wait(barrier, everyone - 1)

    def slab(i, k):
        return sig_ref.at[:, k, :, pl.ds(i * LANES, LANES)]

    def first(i, d):
        return pltpu.make_async_remote_copy(
            slab(i, (mb + d) % nb),
            raw.at[pl.ds(mb * blocks, blocks), i],
            one_send.at[i, d - 1],
            one_recv.at[i, d - 1],
            device_id={"band": (mb + d) % nb},
            device_id_type=MESH,
        )

    def first_from(i, d):
        source = (mb + nb - d) % nb
        return pltpu.make_async_remote_copy(
            slab(i, mb),
            raw.at[pl.ds(source * blocks, blocks), i],
            one_send.at[i, d - 1],
            one_recv.at[i, d - 1],
            device_id={"band": source},
            device_id_type=MESH,
        )

    def first_own(i):
        return pltpu.make_async_copy(
            slab(i, mb), raw.at[pl.ds(mb * blocks, blocks), i], own_one.at[i]
        )

    def first_wait(i):
        for d in range(1, nb):
            first_from(i, d).wait_recv()
        first_own(i).wait()

    apart = sorted(range(1, nb), key=lambda d: -min(d, nb - d))
    for i in (*early, *late):
        for d in apart:
            first(i, d).start()
        first_own(i).start()
    loads = [
        pltpu.make_async_copy(a, b, load_sems.at[i])
        for i, (a, b) in enumerate(zip((bank_ref, *const_refs), (bank, *consts)))
    ]
    for load in loads:
        load.start()

    loads[0].wait()
    turn_row = lax.broadcasted_iota(jnp.int32, (taps, RADIX), 0)
    turn_lane = lax.broadcasted_iota(jnp.int32, (taps, RADIX), 1)
    turned_to = jnp.where((turn_row + turn_lane) % RADIX == 0, 1.0, 0.0).astype(jnp.float32)
    for part in range(2):
        reverse[part] = lax.dot_general(
            bank[part],
            turned_to,
            (((0,), (0,)), ((), ())),
            precision=lax.Precision.HIGHEST,
            preferred_element_type=jnp.float32,
        )

    lane = lax.broadcasted_iota(jnp.int32, (SUBS, LANES), 1)
    sub = lax.broadcasted_iota(jnp.int32, (SUBS, LANES), 0)

    def merge(src, section, r, dst, at, count):
        half = 1 << section
        base = r - r % (2 * half) + r % half - r % min(half, CH_DEV)
        a = base + picks_ref[0, section, r]
        b = base + half + picks_ref[1, section, r]
        d = delay_ref[section, r]
        turn = (LANES - d) & (LANES - 1)
        keep = lane < LANES - d
        turned = [
            pltpu.roll(src[b, :, i * LANES : (i + 1) * LANES], turn, 1) for i in range(tiles + 1)
        ]
        for i in range(count):
            later = turned[min(i + 1, tiles)]
            dst[at, :, i * LANES : (i + 1) * LANES] = src[
                a, :, i * LANES : (i + 1) * LANES
            ] + jnp.where(keep, turned[i], later)

    def tree_part(c):
        @pl.loop(0, nb * blocks)
        def _(q):
            for ch in range(SUBS):
                r = q * SUBS + ch
                rows_of = pl.ds(ch, SUBS, stride=SUBS)
                for i in range(tiles + 1 - c):
                    buf_a[r, :, i * LANES : (i + 1) * LANES] = raw[q, c * tiles + i, rows_of, :]
                if c == 1:
                    up = pltpu.roll(raw[q, 0, rows_of, :], SUBS - 1, 0)
                    edge = jnp.broadcast_to(rim[q, ch : ch + 1, :], (SUBS, LANES))
                    buf_a[r, :, span:] = jnp.where(sub == SUBS - 1, edge, up)

        src, dst = buf_a, buf_b
        for section in range(sections - 1):

            @pl.loop(0, rows, unroll=16)
            def _(r, src=src, dst=dst, section=section):
                merge(src, section, r, dst, r, tiles + 1)

            src, dst = dst, src

        @pl.loop(0, everyone)
        def _(e):
            start = (e % nb) * CH_DEV + (e // nb) * trials

            @pl.loop(0, trials, unroll=trials)
            def _(i):
                merge(src, sections - 1, start + i, stage.at[e], i, tiles)

        copy = pltpu.make_async_copy(stage, sent[c], stage_sem)
        copy.start()
        copy.wait()

    def part_of(c, t):
        return (pl.ds(t, 1), 1 + t) if c else (slice(None), 0)

    def second(c, t, d):
        e = (me + d) % everyone
        which, at = part_of(c, t)
        return pltpu.make_async_remote_copy(
            sent[c].at[e, which],
            got[c].at[me, which],
            two_send.at[at, d - 1],
            two_recv.at[at, d - 1],
            device_id=device(e),
            device_id_type=MESH,
        )

    def second_from(c, t, d):
        e = (me + everyone - d) % everyone
        which, at = part_of(c, t)
        return pltpu.make_async_remote_copy(
            sent[c].at[e, which],
            got[c].at[e, which],
            two_send.at[at, d - 1],
            two_recv.at[at, d - 1],
            device_id=device(e),
            device_id_type=MESH,
        )

    def second_own(c):
        return pltpu.make_async_copy(sent[c].at[me], got[c].at[me], own_two.at[c])

    def send_second(c, t):
        @pl.loop(1, everyone)
        def _(d):
            second(c, t, d).start()

    def wait_second(c, t):
        @pl.loop(1, everyone)
        def _(d):
            second_from(c, t, d).wait_recv()
            second(c, t, d).wait_send()

    for i in early:
        first_wait(i)
    rim_copy = pltpu.make_async_remote_copy(
        raw.at[:, 0, pl.ds(0, SUBS)],
        rim,
        rim_sems.at[0],
        rim_sems.at[1],
        device_id=device((me + everyone - 1) % everyone),
        device_id_type=MESH,
    )

    @pl.when(me > 0)
    def _():
        rim_copy.start()

    @pl.when(me == everyone - 1)
    def _():
        rim[...] = jnp.zeros_like(rim)

    tree_part(0)
    send_second(0, 0)
    second_own(0).start()
    for i in late:
        first_wait(i)

    @pl.when(me < everyone - 1)
    def _():
        rim_copy.wait_recv()

    tree_part(1)
    second_own(1).start()
    for t in range(min(AHEAD, trials)):
        send_second(1, t)
    for i in (*early, *late):
        for d in range(1, nb):
            first(i, d).wait_send()

    @pl.when(me > 0)
    def _():
        rim_copy.wait_send()

    for load in loads[1:]:
        load.wait()
    second_own(0).wait()
    second_own(1).wait()
    wait_second(0, 0)

    def bands_of(t, j):
        def row(z, part):
            return reverse[part, pl.ds(wanted_ref[z, t], 1), :]

        fill_bands(row, zsel, band_high.at[j], band_low.at[j])

    def out_copy(t, j):
        return pltpu.make_async_copy(power.at[j], out_ref.at[t], out_sems.at[j])

    def spectra_of(t, j):
        x = assemble([got[c][:, t] for c in range(2)], consts)

        def store(where, value):
            power[j, where, :] = value

        powers_of(x, band_high[j], band_low[j], consts, zsel, taps // 2, store)
        out_copy(t, j).start()

    @pl.loop(0, trials // 2 - 1)
    def _(g):
        for j in range(2):
            bands_of(2 * g + j, j)
        for j in range(2):
            t = 2 * g + j
            wait_second(1, t)

            @pl.when(t + AHEAD < trials)
            def _(t=t):
                send_second(1, t + AHEAD)

            @pl.when(g > 0)
            def _(j=j, t=t):
                out_copy(t - 2, j).wait()

            spectra_of(t, j)

    last = trials - 1
    for j in range(2):
        bands_of(last - 1 + j, j)
    band_copies = [
        pltpu.make_async_copy(source.at[1], target, last_sems.at[2 + i])
        for i, (source, target) in enumerate(zip((band_high, band_low), last_bands))
    ]
    for copy in band_copies:
        copy.start()
    wait_second(1, last - 1)
    out_copy(last - 3, 0).wait()
    spectra_of(last - 1, 0)
    wait_second(1, last)
    x_copies = [
        pltpu.make_async_copy(got[c].at[:, last], last_x[c], last_sems.at[c]) for c in range(2)
    ]
    for copy in x_copies:
        copy.start()
    out_copy(last - 2, 1).wait()
    out_copy(last - 1, 0).wait()
    for copy in (*band_copies, *x_copies):
        copy.wait()


def assemble(parts, consts):
    cols = consts[2].shape[0]
    parts = [part.reshape(-1, part.shape[-1]) for part in parts]
    return jnp.concatenate(
        [part[:, i : i + cols] for part in parts for i in range(0, part.shape[1], cols)], axis=0
    )


def last_kernel(zsel, half_taps, *refs):
    done_ref, inputs, out_ref, refs = refs[0], refs[1:11], refs[11], refs[12:]
    held, moved, power, sems, move_sems = refs[:10], *refs[10:]
    loads = [
        pltpu.make_async_copy(a, b, sems.at[i]) for i, (a, b) in enumerate(zip(inputs, held))
    ]
    for load in loads:
        load.start()
    count = done_ref.shape[0]
    fetch = [
        pltpu.make_async_copy(done_ref.at[t], moved.at[t], move_sems.at[0, t])
        for t in range(count)
    ]
    store_back = [
        pltpu.make_async_copy(moved.at[t], out_ref.at[t], move_sems.at[1, t])
        for t in range(count)
    ]
    for move in fetch:
        move.start()
    for load in loads:
        load.wait()
    for move, back in zip(fetch, store_back):
        move.wait()
        back.start()
    x = assemble([held[0][...], held[1][...]], held[4:])

    def store(where, value):
        power[where, :] = value

    powers_of(x, held[2][...], held[3][...], held[4:], zsel, half_taps, store)
    final = pltpu.make_async_copy(power, out_ref.at[count], sems.at[len(loads)])
    final.start()
    for back in store_back:
        back.wait()
    final.wait()


def fused(signal, picks, delays, template_bank, wanted, consts, zsel, taps, nb, nt):
    sections = picks.shape[1]
    channels = CH_DEV * nb
    everyone = nb * nt
    trials = CH_DEV // nt
    slab = signal.shape[1] // nb
    width = slab // SUBS
    span = width // 2
    blocks = CH_DEV // SUBS
    cols = consts[2].shape[0]
    outs = cols // 2
    rows = 2 * outs * zsel
    wide = 2 * zsel * LANES
    view = signal.reshape(blocks, SUBS, nb * SUBS, width).transpose(0, 2, 1, 3)
    view = view.reshape(blocks, nb, SUBS * SUBS, width)
    bank = template_bank.transpose(0, 2, 1)
    smem = pl.BlockSpec(memory_space=pltpu.SMEM)
    anywhere = pl.BlockSpec(memory_space=pl.ANY)
    dma = pltpu.SemaphoreType.DMA
    f32, bf16 = jnp.float32, jnp.bfloat16
    macs = cols * RADIX * 2 * RADIX + outs * 2 * cols * 2 * RADIX + 2 * outs * 4 * RADIX * RADIX
    arrays = jax.ShapeDtypeStruct
    exchanged = (everyone, trials, SUBS, span)
    last = [arrays((everyone, SUBS, span), f32)] * 2 + [arrays((2 * RADIX, wide), bf16)] * 2
    scratch_consts = [pltpu.VMEM(c.shape, c.dtype) for c in consts]
    done, *rest = pl.pallas_call(
        functools.partial(fused_kernel, nb, nt, sections, trials, zsel, taps),
        out_shape=[arrays((trials - 1, rows, LANES), f32)] + last + [arrays(exchanged, f32)] * 2,
        in_specs=[smem] * 3 + [anywhere] * 8,
        out_specs=[anywhere] * 7,
        scratch_shapes=[
            pltpu.VMEM((nb * blocks, width // LANES, SUBS * SUBS, LANES), f32),
            pltpu.VMEM((nb * blocks, SUBS, LANES), f32),
            pltpu.VMEM((channels, SUBS, span + LANES), f32),
            pltpu.VMEM((channels, SUBS, span + LANES), f32),
            pltpu.VMEM(exchanged, f32),
            pltpu.VMEM(exchanged, f32),
            pltpu.VMEM(exchanged, f32),
            pltpu.VMEM((2, 2 * RADIX, wide), bf16),
            pltpu.VMEM((2, 2 * RADIX, wide), bf16),
            pltpu.VMEM((2, rows, LANES), f32),
            pltpu.VMEM(bank.shape, f32),
            pltpu.VMEM(template_bank.shape[:2] + (RADIX,), f32),
            *scratch_consts,
            dma((width // LANES, nb - 1)),
            dma((width // LANES, nb - 1)),
            dma((1 + trials, everyone - 1)),
            dma((1 + trials, everyone - 1)),
            dma((2,)),
            dma((width // LANES,)),
            dma((2,)),
            dma,
            dma((1 + len(consts),)),
            dma((2,)),
            dma((4,)),
        ],
        compiler_params=pltpu.CompilerParams(
            collective_id=0, has_side_effects=True, vmem_limit_bytes=FUSED_LIMIT
        ),
        cost_estimate=pl.CostEstimate(
            flops=6 * trials * macs, bytes_accessed=3 * signal.size * 4, transcendentals=0
        ),
        name="fused",
    )(picks, delays, wanted.T, bank, view, *consts)
    return pl.pallas_call(
        functools.partial(last_kernel, zsel, taps // 2),
        out_shape=arrays((trials, rows, LANES), f32),
        in_specs=[anywhere] * 11,
        out_specs=anywhere,
        scratch_shapes=[
            *[pltpu.VMEM(a.shape, a.dtype) for a in last],
            *scratch_consts,
            pltpu.VMEM((trials - 1, rows, LANES), f32),
            pltpu.VMEM((rows, LANES), f32),
            dma((11,)),
            dma((2, trials - 1)),
        ],
        compiler_params=pltpu.CompilerParams(vmem_limit_bytes=LIMIT),
        cost_estimate=pl.CostEstimate(
            flops=6 * macs, bytes_accessed=3 * signal.size * 4, transcendentals=0
        ),
        name="last",
    )(done, *rest[:4], *consts)


def on_device(signal, tree_picks, tree_delays, template_bank, template_pick):
    band_count = lax.axis_size("band")
    time_count = lax.axis_size("tm")
    everyone = band_count * time_count
    sections = LOGCD + band_count.bit_length() - 1
    rim_depth = sections * MAXD
    channels = CH_DEV * band_count
    samples = signal.shape[1] * time_count
    slab = signal.shape[1] // band_count
    width = slab // SUBS
    trials = CH_DEV // time_count
    last = max(1, 3 * trials // 16)
    counts = [count for count in (trials - last, last) if count]
    zsel = template_pick.shape[2]
    taps = template_bank.shape[2]
    cols = samples // RADIX
    if width % (2 * cols) == 0 and trials % 2 == 0 and trials >= 4:
        consts = [jnp.asarray(c) for c in tables(samples, channels, width, taps)]
        out = fused(
            signal, tree_picks, tree_delays, template_bank, template_pick[0], consts, zsel, taps,
            band_count, time_count,
        )
        return finish(out, trials, samples, zsel)

    band_high, band_low = bands(template_pick[0], template_bank)

    half = (1 << np.arange(sections))[:, None]
    r = np.arange(channels)[None, :]
    base = r - r % (2 * half) + r % half - r % np.minimum(half, CH_DEV)
    low = tree_picks[0] + base.astype(np.int32)
    high = tree_picks[1] + (base + half).astype(np.int32)
    grid = np.arange(channels).reshape(band_count, time_count, trials).transpose(1, 0, 2)
    firsts = [sum(counts[:q]) for q in range(len(counts))]
    order = np.concatenate(
        [grid[:, :, first : first + count].reshape(-1) for first, count in zip(firsts, counts)]
    ).astype(np.int32)
    tables_of = (low, high, tree_delays, jnp.asarray(order))
    sizes = [everyone * count for count in counts]

    folded = signal.reshape(CH_DEV, band_count, SUBS, width)

    def exchanged(value):
        value = lax.all_to_all(value, "band", split_axis=0, concat_axis=0, tiled=True)
        return value.reshape(channels, SUBS, -1)

    def rim_of(x):
        rim = shifted(x[:, 0, :rim_depth], ("tm", "band"), -1)
        rim = jnp.pad(rim, ((0, 0), (0, LANES - rim_depth)))
        return jnp.broadcast_to(rim[:, None, :], (channels, SUBS, LANES))

    if width % (2 * LANES) == 0:
        span = width // 2
        cut = span + LANES
        x_a = exchanged(folded[..., :cut].transpose(1, 0, 2, 3))
        x_b = after(after(folded[..., cut:].transpose(1, 0, 2, 3), x_a), band_low)
        x_b = exchanged(x_b)
        pieces = tree([x_a], [0], None, tables_of, sizes, width, span, 0, [])
        pieces = tree(
            [x_a, x_b], [span, 0], rim_of(x_a), tables_of, sizes, width, span, 1, pieces
        )
    else:
        x = exchanged(folded.transpose(1, 0, 2, 3))
        pieces = tree([x], [0], rim_of(x), tables_of, sizes, width, width, 0, [])

    consts = [jnp.asarray(c) for c in tables(samples, channels, width, taps)]
    out = None
    for first, count, piece in zip(firsts, counts, pieces):
        piece = piece.reshape(everyone, count, SUBS, width)
        if out is not None:
            piece = after(piece, arrived)
        arrived = lax.all_to_all(piece, ("tm", "band"), split_axis=0, concat_axis=0, tiled=True)
        out, _ = spectra(
            arrived, band_high, band_low, consts, zsel, taps, trials, first, out
        )
    return finish(out, trials, samples, zsel)


def solution(mesh):
    in_specs = (P(("beams", "band"), "tm"), P(), P(), P(), P(("beams", "band"), "tm", None))
    out_specs = P(("beams", "band"), "tm", None, None)
    return jax.shard_map(
        on_device, mesh=mesh, in_specs=in_specs, out_specs=out_specs, check_vma=False
    )
```

```python
import functools
import math

import jax
import jax.numpy as jnp
import ml_dtypes
import numpy as np
from jax import lax
from jax.experimental import pallas as pl
from jax.experimental.pallas import tpu as pltpu
from jax.sharding import PartitionSpec as P

CH_DEV = 64
LOGCD = 6
MAXD = 4
LANES = 128
SUBS = 8
RADIX = 256
LIMIT = 56 * 1024 * 1024
FUSED_LIMIT = 62 * 1024 * 1024
AHEAD = 6
MESH = pl.DeviceIdType.MESH


def shifted(value, axis, steps):
    count = lax.axis_size(axis)
    first, last = (max(0, -steps), min(count, count - steps))
    return lax.ppermute(value, axis, [(source, source + steps) for source in range(first, last)])


def tree_kernel(sections, sizes, parts, has_rim, *refs):
    low_ref, high_ref, delay_ref, row_ref = refs[:4]
    xs, refs = refs[4 : 4 + len(parts)], refs[4 + len(parts) :]
    if has_rim:
        rim_ref, refs = refs[0], refs[1:]
    buf_a, buf_b = refs[-2:]
    outs = refs[len(refs) - 2 - len(sizes) : -2]
    rows, _, span = buf_a.shape
    tiles = span // LANES - 1
    lane = lax.broadcasted_iota(jnp.int32, (SUBS, LANES), 1)
    sub = lax.broadcasted_iota(jnp.int32, (SUBS, LANES), 0)

    @pl.loop(0, rows, unroll=4)
    def _(r):
        at = 0
        for x_ref, first in zip(xs, parts):
            count = x_ref.shape[2] - first
            buf_a[r, :, at : at + count] = x_ref[r, :, first:]
            at += count
        if has_rim:
            up = pltpu.roll(xs[0][r, :, 0:LANES], SUBS - 1, 0)
            buf_a[r, :, at : at + LANES] = jnp.where(sub == SUBS - 1, rim_ref[r], up)

    def merge(src, section, r, dst, at, count):
        a = low_ref[section, r]
        b = high_ref[section, r]
        d = delay_ref[section, r]
        turn = (LANES - d) & (LANES - 1)
        keep = lane < LANES - d
        turned = [
            pltpu.roll(src[b, :, i * LANES : (i + 1) * LANES], turn, 1) for i in range(tiles + 1)
        ]
        for i in range(count):
            later = turned[min(i + 1, tiles)]
            dst[at, :, i * LANES : (i + 1) * LANES] = src[
                a, :, i * LANES : (i + 1) * LANES
            ] + jnp.where(keep, turned[i], later)

    src, dst = buf_a, buf_b
    for section in range(sections - 1):

        @pl.loop(0, rows, unroll=16)
        def _(r, src=src, dst=dst, section=section):
            merge(src, section, r, dst, r, tiles + 1)

        src, dst = dst, src
    start = 0
    for size, out in zip(sizes, outs):

        @pl.loop(0, size, unroll=16)
        def _(i, start=start, src=src, out=out):
            merge(src, sections - 1, row_ref[start + i], out, i, tiles)

        start += size


def tree(xs, parts, rim, tables_of, sizes, width, span, place, so_far):
    rows = xs[0].shape[0]
    sections = tables_of[0].shape[0]
    smem = pl.BlockSpec(memory_space=pltpu.SMEM)
    vmem = pl.BlockSpec(memory_space=pltpu.VMEM)
    has_rim = rim is not None
    inputs = [*tables_of, *xs] + ([rim] if has_rim else [])
    known = len(inputs)
    return pl.pallas_call(
        functools.partial(tree_kernel, sections, sizes, parts, has_rim),
        grid=(1,),
        out_shape=[jax.ShapeDtypeStruct((size, SUBS, width), jnp.float32) for size in sizes],
        in_specs=[smem] * 4
        + [vmem] * (known - 4)
        + [pl.BlockSpec(memory_space=pl.ANY)] * len(so_far),
        out_specs=[pl.BlockSpec((size, SUBS, span), lambda i: (0, 0, place)) for size in sizes],
        input_output_aliases={known + i: i for i in range(len(so_far))},
        scratch_shapes=[pltpu.VMEM((rows, SUBS, span + LANES), jnp.float32)] * 2,
        compiler_params=pltpu.CompilerParams(vmem_limit_bytes=LIMIT),
        cost_estimate=pl.CostEstimate(
            flops=rows * SUBS * span * sections * 4,
            bytes_accessed=rows * SUBS * span * 8,
            transcendentals=0,
        ),
        name="tree",
    )(*inputs, *so_far)


def split(value):
    high = value.astype(jnp.bfloat16)
    return high, (value - high.astype(jnp.float32)).astype(jnp.bfloat16)


def fill_bands(row_of, zsel, high_ref, low_ref):
    for z in range(zsel):
        pair = []
        for part in range(2):
            wide = jnp.broadcast_to(row_of(z, part), (RADIX, RADIX))
            band = pltpu.roll(wide, 0, 1, stride=1, stride_axis=0)[:, :LANES]
            pair.append(split(band))
        at = 2 * z * LANES
        for ref, real, imag in (
            (high_ref, pair[0][0], pair[1][0]),
            (low_ref, pair[0][1], pair[1][1]),
        ):
            ref[:RADIX, at : at + LANES] = real
            ref[RADIX:, at : at + LANES] = -imag
            ref[:RADIX, at + LANES : at + 2 * LANES] = imag
            ref[RADIX:, at + LANES : at + 2 * LANES] = real


def bands_kernel(zsel, u_ref, high_ref, low_ref):
    def row_of(z, part):
        return u_ref[0, 2 * z + part : 2 * z + part + 1, :]

    fill_bands(row_of, zsel, high_ref.at[0], low_ref.at[0])


def reversed_taps(picks, template_bank):
    trials, zsel = picks.shape
    taps = template_bank.shape[2]
    onehot = (picks[:, :, None] == jnp.arange(template_bank.shape[1], dtype=jnp.int32)).astype(
        jnp.float32
    )
    reversed_bank = jnp.concatenate(
        [
            template_bank[:, :, :1],
            jnp.zeros(template_bank.shape[:2] + (RADIX - taps,), jnp.float32),
            template_bank[:, :, :0:-1],
        ],
        axis=2,
    )
    u = jnp.einsum("tzk,ckm->tzcm", onehot, reversed_bank, precision=lax.Precision.HIGHEST)
    return u.reshape(trials, 2 * zsel, RADIX)


def bands(picks, template_bank):
    trials, zsel = picks.shape
    u = reversed_taps(picks, template_bank)
    wide = 2 * zsel * LANES
    shape = jax.ShapeDtypeStruct((trials, 2 * RADIX, wide), jnp.bfloat16)
    spec = pl.BlockSpec((1, 2 * RADIX, wide), lambda t: (t, 0, 0))
    return pl.pallas_call(
        functools.partial(bands_kernel, zsel),
        grid=(trials,),
        out_shape=[shape, shape],
        in_specs=[pl.BlockSpec((1, 2 * zsel, RADIX), lambda t: (t, 0, 0))],
        out_specs=[spec, spec],
        compiler_params=pltpu.CompilerParams(vmem_limit_bytes=LIMIT),
        cost_estimate=pl.CostEstimate(
            flops=trials * RADIX * RADIX * 20,
            bytes_accessed=trials * 2 * RADIX * wide * 4,
            transcendentals=0,
        ),
        name="bands",
    )(u)


def tables(samples, channels, width, taps):
    cols = samples // RADIX
    outs = cols // 2
    split_by = width // cols if width % cols == 0 else 1
    place = np.arange(RADIX)
    row_of = split_by * (place % (RADIX // split_by)) + place // (RADIX // split_by)
    freq = (np.arange(RADIX) - taps // 2) % RADIX
    b = np.arange(cols)
    scale = 1.0 / math.sqrt(samples * channels)
    angle = 2.0 * np.pi / RADIX * (row_of[:, None] * freq[None, :] % RADIX)
    first = np.concatenate([np.cos(angle), -np.sin(angle)], axis=1) * scale
    angle = 2.0 * np.pi / samples * (b[:, None] * freq[None, :] % samples)
    tw_cos, tw_sin = np.cos(angle), np.sin(angle)
    angle = 2.0 * np.pi / cols * (np.arange(outs)[:, None] * b[None, :] % cols)
    second = np.concatenate([np.cos(angle), np.sin(angle)], axis=1)

    def parts(value):
        value = value.astype(np.float32)
        high = value.astype(ml_dtypes.bfloat16)
        return high, (value - high.astype(np.float32)).astype(ml_dtypes.bfloat16)

    return (
        *parts(first),
        tw_cos.astype(np.float32),
        tw_sin.astype(np.float32),
        *parts(second),
    )


def dot3(a_high, a_low, b_high, b_low):
    def dot(a, b):
        return jnp.dot(a, b, preferred_element_type=jnp.float32)

    return dot(a_high, b_high) + (dot(a_high, b_low) + dot(a_low, b_high))


def powers_of(x, band_high, band_low, consts, zsel, half_taps, store, between=()):
    fh, fl, tc, ts, sh, sl = consts
    cols = tc.shape[0]
    outs = cols // 2
    x_high, x_low = split(x.T)
    first = dot3(x_high, x_low, fh[...], fl[...])
    if between:
        between[0]()
    re, im = first[:, :RADIX], first[:, RADIX:]
    mid_re = re * tc[...] + im * ts[...]
    mid_im = im * tc[...] - re * ts[...]
    re_high, re_low = split(mid_re)
    im_high, im_low = split(mid_im)

    def block(a, b):
        return jnp.concatenate(
            [jnp.concatenate([a, b], axis=1), jnp.concatenate([b, -a], axis=1)], axis=0
        )

    spec = dot3(sh[...], sl[...], block(re_high, im_high), block(re_low, im_low))
    if between:
        between[1]()
    row = lax.broadcasted_iota(jnp.int32, (outs, RADIX), 0)
    lane = lax.broadcasted_iota(jnp.int32, (outs, RADIX), 1)
    even, odd = [], []
    for part in (spec[:, :RADIX], spec[:, RADIX:]):
        down = jnp.where(row == 0, 0.0, pltpu.roll(part, 1, 0))
        up = jnp.where(row == outs - 1, 0.0, pltpu.roll(part, outs - 1, 0))
        here = jnp.where(lane < half_taps, down, part)
        after = jnp.where(lane < half_taps, part, up)
        even.append(here)
        odd += [here[:, LANES:], after[:, :LANES]]
    window = jnp.concatenate(
        [jnp.concatenate(even, axis=1), jnp.concatenate(odd, axis=1)], axis=0
    )
    w_high, w_low = split(window)
    got = dot3(w_high, w_low, band_high, band_low)
    for z in range(zsel):
        at = 2 * z * LANES
        real, imag = got[:, at : at + LANES], got[:, at + LANES : at + 2 * LANES]
        power = real * real + imag * imag
        for e in range(2):
            store(pl.ds(e * zsel + z, outs, 2 * zsel), power[e * outs : (e + 1) * outs])


def spectra_kernel(zsel, half_taps, aliased, *refs):
    x_ref, bh_ref, bl_ref = refs[:3]
    consts = refs[3:9]
    out_ref, done_ref = refs[10:] if aliased else refs[9:]
    done_ref[...] = jnp.zeros_like(done_ref)
    cols = consts[2].shape[0]
    x = x_ref[...]
    x = x.reshape(-1, x.shape[-1])
    if x.shape[1] != cols:
        x = jnp.concatenate(
            [x[:, i * cols : (i + 1) * cols] for i in range(x.shape[1] // cols)], axis=0
        )

    def store(rows, value):
        out_ref[0, rows, :] = value

    powers_of(x, bh_ref[0], bl_ref[0], consts, zsel, half_taps, store)


def spectra(x, band_high, band_low, consts, zsel, taps, trials, first_trial, so_far):
    cols = consts[2].shape[0]
    outs = cols // 2
    rows = 2 * outs * zsel
    if x.shape[-1] % cols == 0:
        here = x.shape[1]
        x_spec = pl.BlockSpec((x.shape[0], 1, SUBS, x.shape[-1]), lambda t: (0, t, 0, 0))
    else:
        here = x.shape[1]
        x = x.transpose(1, 0, 2, 3).reshape(here, RADIX, cols)
        x_spec = pl.BlockSpec((1, RADIX, cols), lambda t: (t, 0, 0))
    band_spec = pl.BlockSpec(
        (1,) + band_high.shape[1:], lambda t: (first_trial + t, 0, 0)
    )
    whole = [pl.BlockSpec(c.shape, lambda t: (0, 0)) for c in consts]
    aliased = so_far is not None
    more = [so_far] if aliased else []
    macs = here * (cols * RADIX * 2 * RADIX + outs * 2 * cols * 2 * RADIX + 2 * outs * 4 * RADIX * RADIX)
    return pl.pallas_call(
        functools.partial(spectra_kernel, zsel, taps // 2, aliased),
        grid=(here,),
        out_shape=[
            jax.ShapeDtypeStruct((trials, rows, LANES), jnp.float32),
            jax.ShapeDtypeStruct((SUBS, LANES), jnp.float32),
        ],
        in_specs=[x_spec, band_spec, band_spec, *whole]
        + [pl.BlockSpec(memory_space=pl.ANY)] * len(more),
        out_specs=[
            pl.BlockSpec((1, rows, LANES), lambda t: (first_trial + t, 0, 0)),
            pl.BlockSpec((SUBS, LANES), lambda t: (0, 0)),
        ],
        input_output_aliases={9: 0} if aliased else {},
        compiler_params=pltpu.CompilerParams(vmem_limit_bytes=LIMIT),
        cost_estimate=pl.CostEstimate(
            flops=6 * macs, bytes_accessed=here * 2 * 1024 * 1024, transcendentals=0
        ),
        name="spectra",
    )(x, band_high, band_low, *consts, *more)


def after_kernel(value_ref, done_ref, out_ref):
    del value_ref, done_ref, out_ref


def after(value, done):
    anywhere = pl.BlockSpec(memory_space=pl.ANY)
    return pl.pallas_call(
        after_kernel,
        out_shape=jax.ShapeDtypeStruct(value.shape, value.dtype),
        in_specs=[anywhere, anywhere],
        out_specs=anywhere,
        input_output_aliases={0: 0},
        name="after",
    )(value, done)


def finish(out, trials, samples, zsel):
    out = out.reshape(trials, samples // 2 // LANES, zsel, LANES).transpose(0, 2, 1, 3)
    return out.reshape(1, trials, zsel, samples // 2)


def fused_kernel(
    nb, nt, sections, trials, zsel, taps,
    picks_hbm, delay_hbm, wanted_hbm, bank_ref, sig_ref, *refs
):
    const_refs, refs = refs[:6], refs[6:]
    out_ref, last_x, last_bands, sent, refs = refs[0], refs[1:3], refs[3:5], refs[5:7], refs[7:]
    raw, rim, buf_a, buf_b, stage, refs = *refs[:5], refs[5:]
    got, refs = refs[:2], refs[2:]
    band_high, band_low, power, bank, reverse, refs = *refs[:5], refs[5:]
    consts, refs = refs[:6], refs[6:]
    picks_ref, delay_ref, wanted_ref, refs = *refs[:3], refs[3:]
    (
        one_send, one_recv, two_send, two_recv, rim_sems, stage_sem, load_sems, out_sems, last_sems,
    ) = refs

    everyone = nb * nt
    rows, _, span = buf_a.shape
    span = span - LANES
    blocks = CH_DEV // SUBS
    tiles = span // LANES
    early = range(tiles + 1)
    late = range(tiles + 1, 2 * tiles)
    mt, mb = lax.axis_index("tm"), lax.axis_index("band")
    me = mt * nb + mb

    def device(e):
        return {"tm": e // nb, "band": e % nb}

    barrier = pltpu.get_barrier_semaphore()

    @pl.loop(1, everyone)
    def _(d):
        pl.semaphore_signal(
            barrier, 1, device_id=device((me + d) % everyone), device_id_type=MESH
        )

    pl.semaphore_wait(barrier, everyone - 1)

    def slab(i, k):
        return sig_ref.at[:, k, :, pl.ds(i * LANES, LANES)]

    def landed(ref, sem):
        pltpu.make_async_copy(ref, ref, sem).wait()

    def first(i, d):
        return pltpu.make_async_remote_copy(
            slab(i, (mb + d) % nb),
            raw.at[pl.ds(mb * blocks, blocks), i],
            one_send,
            one_recv.at[i],
            device_id={"band": (mb + d) % nb},
            device_id_type=MESH,
        )

    def first_own(i):
        return pltpu.make_async_copy(
            slab(i, mb), raw.at[pl.ds(mb * blocks, blocks), i], one_recv.at[i]
        )

    def first_wait(i):
        landed(raw.at[:, i], one_recv.at[i])

    apart = sorted(range(1, nb), key=lambda d: -min(d, nb - d))
    for i in (*early, *late):
        for d in apart:
            first(i, d).start()
        first_own(i).start()
    loads = [
        pltpu.make_async_copy(a, b, load_sems.at[i])
        for i, (a, b) in enumerate(zip(
            (bank_ref, picks_hbm, delay_hbm, wanted_hbm, *const_refs),
            (bank, picks_ref, delay_ref, wanted_ref, *consts),
        ))
    ]
    for load in loads:
        load.start()

    for load in loads[:4]:
        load.wait()
    turn_row = lax.broadcasted_iota(jnp.int32, (taps, RADIX), 0)
    turn_lane = lax.broadcasted_iota(jnp.int32, (taps, RADIX), 1)
    turned_to = jnp.where((turn_row + turn_lane) % RADIX == 0, 1.0, 0.0).astype(jnp.float32)
    for part in range(2):
        reverse[part] = lax.dot_general(
            bank[part],
            turned_to,
            (((0,), (0,)), ((), ())),
            precision=lax.Precision.HIGHEST,
            preferred_element_type=jnp.float32,
        )

    lane = lax.broadcasted_iota(jnp.int32, (SUBS, LANES), 1)
    sub = lax.broadcasted_iota(jnp.int32, (SUBS, LANES), 0)

    def merge(src, section, r, dst, at, count):
        half = 1 << section
        base = r - r % (2 * half) + r % half - r % min(half, CH_DEV)
        a = base + picks_ref[0, section, r]
        b = base + half + picks_ref[1, section, r]
        d = delay_ref[section, r]
        turn = (LANES - d) & (LANES - 1)
        keep = lane < LANES - d
        turned = [
            pltpu.roll(src[b, :, i * LANES : (i + 1) * LANES], turn, 1) for i in range(tiles + 1)
        ]
        for i in range(count):
            later = turned[min(i + 1, tiles)]
            dst[at, :, i * LANES : (i + 1) * LANES] = src[
                a, :, i * LANES : (i + 1) * LANES
            ] + jnp.where(keep, turned[i], later)

    def tree_part(c):
        @pl.loop(0, nb * blocks)
        def _(q):
            for ch in range(SUBS):
                r = q * SUBS + ch
                rows_of = pl.ds(ch, SUBS, stride=SUBS)
                for i in range(tiles + 1 - c):
                    buf_a[r, :, i * LANES : (i + 1) * LANES] = raw[q, c * tiles + i, rows_of, :]
                if c == 1:
                    up = pltpu.roll(raw[q, 0, rows_of, :], SUBS - 1, 0)
                    edge = jnp.broadcast_to(rim[q, ch : ch + 1, :], (SUBS, LANES))
                    buf_a[r, :, span:] = jnp.where(sub == SUBS - 1, edge, up)

        src, dst = buf_a, buf_b
        for section in range(sections - 1):

            @pl.loop(0, rows, unroll=16)
            def _(r, src=src, dst=dst, section=section):
                merge(src, section, r, dst, r, tiles + 1)

            src, dst = dst, src

        @pl.loop(0, everyone)
        def _(e):
            start = (e % nb) * CH_DEV + (e // nb) * trials

            @pl.loop(0, trials, unroll=trials)
            def _(i):
                merge(src, sections - 1, start + i, stage.at[e], i, tiles)

        copy = pltpu.make_async_copy(stage, sent[c], stage_sem)
        copy.start()
        copy.wait()

    def part_of(c, t):
        return (pl.ds(t, 1), 1 + t) if c else (slice(None), 0)

    def second(c, t, d):
        e = (me + d) % everyone
        which, at = part_of(c, t)
        return pltpu.make_async_remote_copy(
            sent[c].at[e, which],
            got[c].at[me, which],
            two_send.at[c],
            two_recv.at[at],
            device_id=device(e),
            device_id_type=MESH,
        )

    def send_second(c, t):
        @pl.loop(1, everyone)
        def _(d):
            second(c, t, d).start()

        which, at = part_of(c, t)
        pltpu.make_async_copy(
            sent[c].at[me, which], got[c].at[me, which], two_recv.at[at]
        ).start()

    def wait_second(c, t):
        which, at = part_of(c, t)
        landed(got[c].at[:, which], two_recv.at[at])

    for i in early:
        first_wait(i)
    rim_copy = pltpu.make_async_remote_copy(
        raw.at[:, 0, pl.ds(0, SUBS)],
        rim,
        rim_sems.at[0],
        rim_sems.at[1],
        device_id=device((me + everyone - 1) % everyone),
        device_id_type=MESH,
    )

    @pl.when(me > 0)
    def _():
        rim_copy.start()

    @pl.when(me == everyone - 1)
    def _():
        rim[...] = jnp.zeros_like(rim)

    tree_part(0)
    send_second(0, 0)
    for i in late:
        first_wait(i)

    @pl.when(me < everyone - 1)
    def _():
        rim_copy.wait_recv()

    tree_part(1)
    for t in range(min(AHEAD, trials)):
        send_second(1, t)
    landed(raw.at[pl.ds(0, (nb - 1) * blocks)], one_send)

    @pl.when(me > 0)
    def _():
        rim_copy.wait_send()

    for load in loads[4:]:
        load.wait()
    wait_second(0, 0)

    def bands_of(t, j):
        def row(z, part):
            return reverse[part, pl.ds(wanted_ref[z, t], 1), :]

        fill_bands(row, zsel, band_high.at[j], band_low.at[j])

    def out_copy(t, j):
        return pltpu.make_async_copy(power.at[j], out_ref.at[t], out_sems.at[j])

    def spectra_of(t, j):
        x = assemble([got[c][:, t] for c in range(2)], consts)

        def store(where, value):
            power[j, where, :] = value

        powers_of(x, band_high[j], band_low[j], consts, zsel, taps // 2, store)
        out_copy(t, j).start()

    @pl.loop(0, trials // 2 - 1)
    def _(g):
        for j in range(2):
            bands_of(2 * g + j, j)
        for j in range(2):
            t = 2 * g + j
            wait_second(1, t)

            @pl.when(t + AHEAD < trials)
            def _(t=t):
                send_second(1, t + AHEAD)

            @pl.when(g > 0)
            def _(j=j, t=t):
                out_copy(t - 2, j).wait()

            spectra_of(t, j)

    last = trials - 1
    for j in range(2):
        bands_of(last - 1 + j, j)
    band_copies = [
        pltpu.make_async_copy(source.at[1], target, last_sems.at[2 + i])
        for i, (source, target) in enumerate(zip((band_high, band_low), last_bands))
    ]
    for copy in band_copies:
        copy.start()
    wait_second(1, last - 1)
    out_copy(last - 3, 0).wait()
    spectra_of(last - 1, 0)
    wait_second(1, last)
    x_copies = [
        pltpu.make_async_copy(got[c].at[:, last], last_x[c], last_sems.at[c]) for c in range(2)
    ]
    for copy in x_copies:
        copy.start()
    out_copy(last - 2, 1).wait()
    out_copy(last - 1, 0).wait()
    for copy in (*band_copies, *x_copies):
        copy.wait()
    for c in range(2):
        landed(sent[c].at[pl.ds(0, everyone - 1)], two_send.at[c])


def assemble(parts, consts):
    cols = consts[2].shape[0]
    parts = [part.reshape(-1, part.shape[-1]) for part in parts]
    return jnp.concatenate(
        [part[:, i : i + cols] for part in parts for i in range(0, part.shape[1], cols)], axis=0
    )


def last_kernel(zsel, half_taps, *refs):
    done_ref, inputs, out_ref, refs = refs[0], refs[1:11], refs[11], refs[12:]
    held, moved, power, sems, move_sems = refs[:10], *refs[10:]
    loads = [
        pltpu.make_async_copy(a, b, sems.at[i]) for i, (a, b) in enumerate(zip(inputs, held))
    ]
    for load in loads:
        load.start()
    count = done_ref.shape[0]
    fetch = [
        pltpu.make_async_copy(done_ref.at[t], moved.at[t], move_sems.at[0, t])
        for t in range(count)
    ]
    store_back = [
        pltpu.make_async_copy(moved.at[t], out_ref.at[t], move_sems.at[1, t])
        for t in range(count)
    ]
    for move in fetch:
        move.start()
    for load in loads:
        load.wait()

    def move_on(begin, end):
        for move, back in zip(fetch[begin:end], store_back[begin:end]):
            move.wait()
            back.start()

    between = (lambda: move_on(0, count // 2), lambda: move_on(count // 2, count))
    x = assemble([held[0][...], held[1][...]], held[4:])

    def store(where, value):
        power[where, :] = value

    powers_of(x, held[2][...], held[3][...], held[4:], zsel, half_taps, store, between)
    final = pltpu.make_async_copy(power, out_ref.at[count], sems.at[len(loads)])
    final.start()
    for back in store_back:
        back.wait()
    final.wait()


def fused(signal, picks, delays, template_bank, wanted, consts, zsel, taps, nb, nt):
    sections = picks.shape[1]
    channels = CH_DEV * nb
    everyone = nb * nt
    trials = CH_DEV // nt
    slab = signal.shape[1] // nb
    width = slab // SUBS
    span = width // 2
    blocks = CH_DEV // SUBS
    cols = consts[2].shape[0]
    outs = cols // 2
    rows = 2 * outs * zsel
    wide = 2 * zsel * LANES
    view = signal.reshape(blocks, SUBS, nb * SUBS, width).transpose(0, 2, 1, 3)
    view = view.reshape(blocks, nb, SUBS * SUBS, width)
    bank = template_bank.transpose(0, 2, 1)
    anywhere = pl.BlockSpec(memory_space=pl.ANY)
    dma = pltpu.SemaphoreType.DMA
    f32, bf16 = jnp.float32, jnp.bfloat16
    macs = cols * RADIX * 2 * RADIX + outs * 2 * cols * 2 * RADIX + 2 * outs * 4 * RADIX * RADIX
    arrays = jax.ShapeDtypeStruct
    exchanged = (everyone, trials, SUBS, span)
    last = [arrays((everyone, SUBS, span), f32)] * 2 + [arrays((2 * RADIX, wide), bf16)] * 2
    scratch_consts = [pltpu.VMEM(c.shape, c.dtype) for c in consts]
    done, *rest = pl.pallas_call(
        functools.partial(fused_kernel, nb, nt, sections, trials, zsel, taps),
        out_shape=[arrays((trials - 1, rows, LANES), f32)] + last + [arrays(exchanged, f32)] * 2,
        in_specs=[anywhere] * 11,
        out_specs=[anywhere] * 7,
        scratch_shapes=[
            pltpu.VMEM((nb * blocks, width // LANES, SUBS * SUBS, LANES), f32),
            pltpu.VMEM((nb * blocks, SUBS, LANES), f32),
            pltpu.VMEM((channels, SUBS, span + LANES), f32),
            pltpu.VMEM((channels, SUBS, span + LANES), f32),
            pltpu.VMEM(exchanged, f32),
            pltpu.VMEM(exchanged, f32),
            pltpu.VMEM(exchanged, f32),
            pltpu.VMEM((2, 2 * RADIX, wide), bf16),
            pltpu.VMEM((2, 2 * RADIX, wide), bf16),
            pltpu.VMEM((2, rows, LANES), f32),
            pltpu.VMEM(bank.shape, f32),
            pltpu.VMEM(template_bank.shape[:2] + (RADIX,), f32),
            *scratch_consts,
            *[pltpu.SMEM(a.shape, jnp.int32) for a in (picks, delays, wanted.T)],
            dma,
            dma((width // LANES,)),
            dma((2,)),
            dma((1 + trials,)),
            dma((2,)),
            dma,
            dma((4 + len(consts),)),
            dma((2,)),
            dma((4,)),
        ],
        compiler_params=pltpu.CompilerParams(
            collective_id=0, has_side_effects=True, vmem_limit_bytes=FUSED_LIMIT
        ),
        cost_estimate=pl.CostEstimate(
            flops=6 * trials * macs, bytes_accessed=3 * signal.size * 4, transcendentals=0
        ),
        name="fused",
    )(picks, delays, wanted.T, bank, view, *consts)
    return pl.pallas_call(
        functools.partial(last_kernel, zsel, taps // 2),
        out_shape=arrays((trials, rows, LANES), f32),
        in_specs=[anywhere] * 11,
        out_specs=anywhere,
        scratch_shapes=[
            *[pltpu.VMEM(a.shape, a.dtype) for a in last],
            *scratch_consts,
            pltpu.VMEM((trials - 1, rows, LANES), f32),
            pltpu.VMEM((rows, LANES), f32),
            dma((11,)),
            dma((2, trials - 1)),
        ],
        compiler_params=pltpu.CompilerParams(vmem_limit_bytes=LIMIT),
        cost_estimate=pl.CostEstimate(
            flops=6 * macs, bytes_accessed=3 * signal.size * 4, transcendentals=0
        ),
        name="last",
    )(done, *rest[:4], *consts)


def on_device(signal, tree_picks, tree_delays, template_bank, template_pick):
    band_count = lax.axis_size("band")
    time_count = lax.axis_size("tm")
    everyone = band_count * time_count
    sections = LOGCD + band_count.bit_length() - 1
    rim_depth = sections * MAXD
    channels = CH_DEV * band_count
    samples = signal.shape[1] * time_count
    slab = signal.shape[1] // band_count
    width = slab // SUBS
    trials = CH_DEV // time_count
    last = max(1, 3 * trials // 16)
    counts = [count for count in (trials - last, last) if count]
    zsel = template_pick.shape[2]
    taps = template_bank.shape[2]
    cols = samples // RADIX
    if width % (2 * cols) == 0 and trials % 2 == 0 and trials >= 4:
        consts = [jnp.asarray(c) for c in tables(samples, channels, width, taps)]
        out = fused(
            signal, tree_picks, tree_delays, template_bank, template_pick[0], consts, zsel, taps,
            band_count, time_count,
        )
        return finish(out, trials, samples, zsel)

    band_high, band_low = bands(template_pick[0], template_bank)

    half = (1 << np.arange(sections))[:, None]
    r = np.arange(channels)[None, :]
    base = r - r % (2 * half) + r % half - r % np.minimum(half, CH_DEV)
    low = tree_picks[0] + base.astype(np.int32)
    high = tree_picks[1] + (base + half).astype(np.int32)
    grid = np.arange(channels).reshape(band_count, time_count, trials).transpose(1, 0, 2)
    firsts = [sum(counts[:q]) for q in range(len(counts))]
    order = np.concatenate(
        [grid[:, :, first : first + count].reshape(-1) for first, count in zip(firsts, counts)]
    ).astype(np.int32)
    tables_of = (low, high, tree_delays, jnp.asarray(order))
    sizes = [everyone * count for count in counts]

    folded = signal.reshape(CH_DEV, band_count, SUBS, width)

    def exchanged(value):
        value = lax.all_to_all(value, "band", split_axis=0, concat_axis=0, tiled=True)
        return value.reshape(channels, SUBS, -1)

    def rim_of(x):
        rim = shifted(x[:, 0, :rim_depth], ("tm", "band"), -1)
        rim = jnp.pad(rim, ((0, 0), (0, LANES - rim_depth)))
        return jnp.broadcast_to(rim[:, None, :], (channels, SUBS, LANES))

    if width % (2 * LANES) == 0:
        span = width // 2
        cut = span + LANES
        x_a = exchanged(folded[..., :cut].transpose(1, 0, 2, 3))
        x_b = after(after(folded[..., cut:].transpose(1, 0, 2, 3), x_a), band_low)
        x_b = exchanged(x_b)
        pieces = tree([x_a], [0], None, tables_of, sizes, width, span, 0, [])
        pieces = tree(
            [x_a, x_b], [span, 0], rim_of(x_a), tables_of, sizes, width, span, 1, pieces
        )
    else:
        x = exchanged(folded.transpose(1, 0, 2, 3))
        pieces = tree([x], [0], rim_of(x), tables_of, sizes, width, width, 0, [])

    consts = [jnp.asarray(c) for c in tables(samples, channels, width, taps)]
    out = None
    for first, count, piece in zip(firsts, counts, pieces):
        piece = piece.reshape(everyone, count, SUBS, width)
        if out is not None:
            piece = after(piece, arrived)
        arrived = lax.all_to_all(piece, ("tm", "band"), split_axis=0, concat_axis=0, tiled=True)
        out, _ = spectra(
            arrived, band_high, band_low, consts, zsel, taps, trials, first, out
        )
    return finish(out, trials, samples, zsel)


def solution(mesh):
    in_specs = (P(("beams", "band"), "tm"), P(), P(), P(), P(("beams", "band"), "tm", None))
    out_specs = P(("beams", "band"), "tm", None, None)
    return jax.shard_map(
        on_device, mesh=mesh, in_specs=in_specs, out_specs=out_specs, check_vma=False
    )
```

```python
import functools
import math

import jax
import jax.numpy as jnp
import ml_dtypes
import numpy as np
from jax import lax
from jax.experimental import pallas as pl
from jax.experimental.pallas import tpu as pltpu
from jax.sharding import PartitionSpec as P

CH_DEV = 64
LOGCD = 6
MAXD = 4
LANES = 128
SUBS = 8
RADIX = 256
LIMIT = 56 * 1024 * 1024
FUSED_LIMIT = 48 * 1024 * 1024
LAST_LIMIT = 14 * 1024 * 1024
AHEAD = 6
MESH = pl.DeviceIdType.MESH


def shifted(value, axis, steps):
    count = lax.axis_size(axis)
    first, last = (max(0, -steps), min(count, count - steps))
    return lax.ppermute(value, axis, [(source, source + steps) for source in range(first, last)])


def tree_kernel(sections, sizes, parts, has_rim, *refs):
    low_ref, high_ref, delay_ref, row_ref = refs[:4]
    xs, refs = refs[4 : 4 + len(parts)], refs[4 + len(parts) :]
    if has_rim:
        rim_ref, refs = refs[0], refs[1:]
    buf_a, buf_b = refs[-2:]
    outs = refs[len(refs) - 2 - len(sizes) : -2]
    rows, _, span = buf_a.shape
    tiles = span // LANES - 1
    lane = lax.broadcasted_iota(jnp.int32, (SUBS, LANES), 1)
    sub = lax.broadcasted_iota(jnp.int32, (SUBS, LANES), 0)

    @pl.loop(0, rows, unroll=4)
    def _(r):
        at = 0
        for x_ref, first in zip(xs, parts):
            count = x_ref.shape[2] - first
            buf_a[r, :, at : at + count] = x_ref[r, :, first:]
            at += count
        if has_rim:
            up = pltpu.roll(xs[0][r, :, 0:LANES], SUBS - 1, 0)
            buf_a[r, :, at : at + LANES] = jnp.where(sub == SUBS - 1, rim_ref[r], up)

    def merge(src, section, r, dst, at, count):
        a = low_ref[section, r]
        b = high_ref[section, r]
        d = delay_ref[section, r]
        turn = (LANES - d) & (LANES - 1)
        keep = lane < LANES - d
        turned = [
            pltpu.roll(src[b, :, i * LANES : (i + 1) * LANES], turn, 1) for i in range(tiles + 1)
        ]
        for i in range(count):
            later = turned[min(i + 1, tiles)]
            dst[at, :, i * LANES : (i + 1) * LANES] = src[
                a, :, i * LANES : (i + 1) * LANES
            ] + jnp.where(keep, turned[i], later)

    src, dst = buf_a, buf_b
    for section in range(sections - 1):

        @pl.loop(0, rows, unroll=16)
        def _(r, src=src, dst=dst, section=section):
            merge(src, section, r, dst, r, tiles + 1)

        src, dst = dst, src
    start = 0
    for size, out in zip(sizes, outs):

        @pl.loop(0, size, unroll=16)
        def _(i, start=start, src=src, out=out):
            merge(src, sections - 1, row_ref[start + i], out, i, tiles)

        start += size


def tree(xs, parts, rim, tables_of, sizes, width, span, place, so_far):
    rows = xs[0].shape[0]
    sections = tables_of[0].shape[0]
    smem = pl.BlockSpec(memory_space=pltpu.SMEM)
    vmem = pl.BlockSpec(memory_space=pltpu.VMEM)
    has_rim = rim is not None
    inputs = [*tables_of, *xs] + ([rim] if has_rim else [])
    known = len(inputs)
    return pl.pallas_call(
        functools.partial(tree_kernel, sections, sizes, parts, has_rim),
        grid=(1,),
        out_shape=[jax.ShapeDtypeStruct((size, SUBS, width), jnp.float32) for size in sizes],
        in_specs=[smem] * 4
        + [vmem] * (known - 4)
        + [pl.BlockSpec(memory_space=pl.ANY)] * len(so_far),
        out_specs=[pl.BlockSpec((size, SUBS, span), lambda i: (0, 0, place)) for size in sizes],
        input_output_aliases={known + i: i for i in range(len(so_far))},
        scratch_shapes=[pltpu.VMEM((rows, SUBS, span + LANES), jnp.float32)] * 2,
        compiler_params=pltpu.CompilerParams(vmem_limit_bytes=LIMIT),
        cost_estimate=pl.CostEstimate(
            flops=rows * SUBS * span * sections * 4,
            bytes_accessed=rows * SUBS * span * 8,
            transcendentals=0,
        ),
        name="tree",
    )(*inputs, *so_far)


def split(value):
    high = value.astype(jnp.bfloat16)
    return high, (value - high.astype(jnp.float32)).astype(jnp.bfloat16)


def fill_bands(row_of, zsel, high_ref, low_ref):
    for z in range(zsel):
        pair = []
        for part in range(2):
            wide = jnp.broadcast_to(row_of(z, part), (RADIX, RADIX))
            band = pltpu.roll(wide, 0, 1, stride=1, stride_axis=0)[:, :LANES]
            pair.append(split(band))
        at = 2 * z * LANES
        for ref, real, imag in (
            (high_ref, pair[0][0], pair[1][0]),
            (low_ref, pair[0][1], pair[1][1]),
        ):
            ref[:RADIX, at : at + LANES] = real
            ref[RADIX:, at : at + LANES] = -imag
            ref[:RADIX, at + LANES : at + 2 * LANES] = imag
            ref[RADIX:, at + LANES : at + 2 * LANES] = real


def bands_kernel(zsel, u_ref, high_ref, low_ref):
    def row_of(z, part):
        return u_ref[0, 2 * z + part : 2 * z + part + 1, :]

    fill_bands(row_of, zsel, high_ref.at[0], low_ref.at[0])


def reversed_taps(picks, template_bank):
    trials, zsel = picks.shape
    taps = template_bank.shape[2]
    onehot = (picks[:, :, None] == jnp.arange(template_bank.shape[1], dtype=jnp.int32)).astype(
        jnp.float32
    )
    reversed_bank = jnp.concatenate(
        [
            template_bank[:, :, :1],
            jnp.zeros(template_bank.shape[:2] + (RADIX - taps,), jnp.float32),
            template_bank[:, :, :0:-1],
        ],
        axis=2,
    )
    u = jnp.einsum("tzk,ckm->tzcm", onehot, reversed_bank, precision=lax.Precision.HIGHEST)
    return u.reshape(trials, 2 * zsel, RADIX)


def bands(picks, template_bank):
    trials, zsel = picks.shape
    u = reversed_taps(picks, template_bank)
    wide = 2 * zsel * LANES
    shape = jax.ShapeDtypeStruct((trials, 2 * RADIX, wide), jnp.bfloat16)
    spec = pl.BlockSpec((1, 2 * RADIX, wide), lambda t: (t, 0, 0))
    return pl.pallas_call(
        functools.partial(bands_kernel, zsel),
        grid=(trials,),
        out_shape=[shape, shape],
        in_specs=[pl.BlockSpec((1, 2 * zsel, RADIX), lambda t: (t, 0, 0))],
        out_specs=[spec, spec],
        compiler_params=pltpu.CompilerParams(vmem_limit_bytes=LIMIT),
        cost_estimate=pl.CostEstimate(
            flops=trials * RADIX * RADIX * 20,
            bytes_accessed=trials * 2 * RADIX * wide * 4,
            transcendentals=0,
        ),
        name="bands",
    )(u)


def tables(samples, channels, width, taps):
    cols = samples // RADIX
    outs = cols // 2
    split_by = width // cols if width % cols == 0 else 1
    place = np.arange(RADIX)
    row_of = split_by * (place % (RADIX // split_by)) + place // (RADIX // split_by)
    freq = (np.arange(RADIX) - taps // 2) % RADIX
    b = np.arange(cols)
    scale = 1.0 / math.sqrt(samples * channels)
    angle = 2.0 * np.pi / RADIX * (row_of[:, None] * freq[None, :] % RADIX)
    first = np.concatenate([np.cos(angle), -np.sin(angle)], axis=1) * scale
    angle = 2.0 * np.pi / samples * (b[:, None] * freq[None, :] % samples)
    tw_cos, tw_sin = np.cos(angle), np.sin(angle)
    angle = 2.0 * np.pi / cols * (np.arange(outs)[:, None] * b[None, :] % cols)
    second = np.concatenate([np.cos(angle), np.sin(angle)], axis=1)

    def parts(value):
        value = value.astype(np.float32)
        high = value.astype(ml_dtypes.bfloat16)
        return high, (value - high.astype(np.float32)).astype(ml_dtypes.bfloat16)

    return (
        *parts(first),
        tw_cos.astype(np.float32),
        tw_sin.astype(np.float32),
        *parts(second),
    )


def dot3(a_high, a_low, b_high, b_low):
    def dot(a, b):
        return jnp.dot(a, b, preferred_element_type=jnp.float32)

    return dot(a_high, b_high) + (dot(a_high, b_low) + dot(a_low, b_high))


def powers_of(x, band_high, band_low, consts, zsel, half_taps, store):
    fh, fl, tc, ts, sh, sl = consts
    cols = tc.shape[0]
    outs = cols // 2
    x_high, x_low = split(x.T)
    first = dot3(x_high, x_low, fh[...], fl[...])
    re, im = first[:, :RADIX], first[:, RADIX:]
    mid_re = re * tc[...] + im * ts[...]
    mid_im = im * tc[...] - re * ts[...]
    re_high, re_low = split(mid_re)
    im_high, im_low = split(mid_im)

    def block(a, b):
        return jnp.concatenate(
            [jnp.concatenate([a, b], axis=1), jnp.concatenate([b, -a], axis=1)], axis=0
        )

    spec = dot3(sh[...], sl[...], block(re_high, im_high), block(re_low, im_low))
    row = lax.broadcasted_iota(jnp.int32, (outs, RADIX), 0)
    lane = lax.broadcasted_iota(jnp.int32, (outs, RADIX), 1)
    even, odd = [], []
    for part in (spec[:, :RADIX], spec[:, RADIX:]):
        down = jnp.where(row == 0, 0.0, pltpu.roll(part, 1, 0))
        up = jnp.where(row == outs - 1, 0.0, pltpu.roll(part, outs - 1, 0))
        here = jnp.where(lane < half_taps, down, part)
        after = jnp.where(lane < half_taps, part, up)
        even.append(here)
        odd += [here[:, LANES:], after[:, :LANES]]
    window = jnp.concatenate(
        [jnp.concatenate(even, axis=1), jnp.concatenate(odd, axis=1)], axis=0
    )
    w_high, w_low = split(window)
    got = dot3(w_high, w_low, band_high, band_low)
    for z in range(zsel):
        at = 2 * z * LANES
        real, imag = got[:, at : at + LANES], got[:, at + LANES : at + 2 * LANES]
        power = real * real + imag * imag
        for e in range(2):
            store(pl.ds(e * zsel + z, outs, 2 * zsel), power[e * outs : (e + 1) * outs])


def spectra_kernel(zsel, half_taps, aliased, *refs):
    x_ref, bh_ref, bl_ref = refs[:3]
    consts = refs[3:9]
    out_ref, done_ref = refs[10:] if aliased else refs[9:]
    done_ref[...] = jnp.zeros_like(done_ref)
    cols = consts[2].shape[0]
    x = x_ref[...]
    x = x.reshape(-1, x.shape[-1])
    if x.shape[1] != cols:
        x = jnp.concatenate(
            [x[:, i * cols : (i + 1) * cols] for i in range(x.shape[1] // cols)], axis=0
        )

    def store(rows, value):
        out_ref[0, rows, :] = value

    powers_of(x, bh_ref[0], bl_ref[0], consts, zsel, half_taps, store)


def spectra(x, band_high, band_low, consts, zsel, taps, trials, first_trial, so_far):
    cols = consts[2].shape[0]
    outs = cols // 2
    rows = 2 * outs * zsel
    if x.shape[-1] % cols == 0:
        here = x.shape[1]
        x_spec = pl.BlockSpec((x.shape[0], 1, SUBS, x.shape[-1]), lambda t: (0, t, 0, 0))
    else:
        here = x.shape[1]
        x = x.transpose(1, 0, 2, 3).reshape(here, RADIX, cols)
        x_spec = pl.BlockSpec((1, RADIX, cols), lambda t: (t, 0, 0))
    band_spec = pl.BlockSpec(
        (1,) + band_high.shape[1:], lambda t: (first_trial + t, 0, 0)
    )
    whole = [pl.BlockSpec(c.shape, lambda t: (0, 0)) for c in consts]
    aliased = so_far is not None
    more = [so_far] if aliased else []
    macs = here * (cols * RADIX * 2 * RADIX + outs * 2 * cols * 2 * RADIX + 2 * outs * 4 * RADIX * RADIX)
    return pl.pallas_call(
        functools.partial(spectra_kernel, zsel, taps // 2, aliased),
        grid=(here,),
        out_shape=[
            jax.ShapeDtypeStruct((trials, rows, LANES), jnp.float32),
            jax.ShapeDtypeStruct((SUBS, LANES), jnp.float32),
        ],
        in_specs=[x_spec, band_spec, band_spec, *whole]
        + [pl.BlockSpec(memory_space=pl.ANY)] * len(more),
        out_specs=[
            pl.BlockSpec((1, rows, LANES), lambda t: (first_trial + t, 0, 0)),
            pl.BlockSpec((SUBS, LANES), lambda t: (0, 0)),
        ],
        input_output_aliases={9: 0} if aliased else {},
        compiler_params=pltpu.CompilerParams(vmem_limit_bytes=LIMIT),
        cost_estimate=pl.CostEstimate(
            flops=6 * macs, bytes_accessed=here * 2 * 1024 * 1024, transcendentals=0
        ),
        name="spectra",
    )(x, band_high, band_low, *consts, *more)


def after_kernel(value_ref, done_ref, out_ref):
    del value_ref, done_ref, out_ref


def after(value, done):
    anywhere = pl.BlockSpec(memory_space=pl.ANY)
    return pl.pallas_call(
        after_kernel,
        out_shape=jax.ShapeDtypeStruct(value.shape, value.dtype),
        in_specs=[anywhere, anywhere],
        out_specs=anywhere,
        input_output_aliases={0: 0},
        name="after",
    )(value, done)


def finish(out, trials, samples, zsel):
    out = out.reshape(trials, samples // 2 // LANES, zsel, LANES).transpose(0, 2, 1, 3)
    return out.reshape(1, trials, zsel, samples // 2)


def fused_kernel(
    nb, nt, sections, trials, zsel, taps,
    picks_hbm, delay_hbm, wanted_hbm, bank_ref, sig_ref, *refs
):
    const_refs, refs = refs[:6], refs[6:]
    power, last_x, band_high, band_low, refs = refs[0], refs[1:3], refs[3], refs[4], refs[5:]
    consts, sent, refs = refs[:6], refs[6:8], refs[8:]
    raw, rim, buf_a, buf_b, stage, refs = *refs[:5], refs[5:]
    got, refs = refs[:2], refs[2:]
    bank, reverse, refs = *refs[:2], refs[2:]
    picks_ref, delay_ref, wanted_ref, refs = *refs[:3], refs[3:]
    (
        one_send, one_recv, two_send, two_recv, rim_sems, stage_sem, load_sems, last_sems,
    ) = refs

    everyone = nb * nt
    rows, _, span = buf_a.shape
    span = span - LANES
    blocks = CH_DEV // SUBS
    tiles = span // LANES
    early = range(tiles + 1)
    late = range(tiles + 1, 2 * tiles)
    mt, mb = lax.axis_index("tm"), lax.axis_index("band")
    me = mt * nb + mb

    def device(e):
        return {"tm": e // nb, "band": e % nb}

    barrier = pltpu.get_barrier_semaphore()

    @pl.loop(1, everyone)
    def _(d):
        pl.semaphore_signal(
            barrier, 1, device_id=device((me + d) % everyone), device_id_type=MESH
        )

    pl.semaphore_wait(barrier, everyone - 1)

    def slab(i, k):
        return sig_ref.at[:, k, :, pl.ds(i * LANES, LANES)]

    def landed(ref, sem):
        pltpu.make_async_copy(ref, ref, sem).wait()

    def first(i, d):
        return pltpu.make_async_remote_copy(
            slab(i, (mb + d) % nb),
            raw.at[pl.ds(mb * blocks, blocks), i],
            one_send,
            one_recv.at[i],
            device_id={"band": (mb + d) % nb},
            device_id_type=MESH,
        )

    def first_own(i):
        return pltpu.make_async_copy(
            slab(i, mb), raw.at[pl.ds(mb * blocks, blocks), i], one_recv.at[i]
        )

    def first_wait(i):
        landed(raw.at[:, i], one_recv.at[i])

    apart = sorted(range(1, nb), key=lambda d: -min(d, nb - d))
    for i in (*early, *late):
        for d in apart:
            first(i, d).start()
        first_own(i).start()
    loads = [
        pltpu.make_async_copy(a, b, load_sems.at[i])
        for i, (a, b) in enumerate(zip(
            (bank_ref, picks_hbm, delay_hbm, wanted_hbm, *const_refs),
            (bank, picks_ref, delay_ref, wanted_ref, *consts),
        ))
    ]
    for load in loads:
        load.start()

    for load in loads[:4]:
        load.wait()
    turn_row = lax.broadcasted_iota(jnp.int32, (taps, RADIX), 0)
    turn_lane = lax.broadcasted_iota(jnp.int32, (taps, RADIX), 1)
    turned_to = jnp.where((turn_row + turn_lane) % RADIX == 0, 1.0, 0.0).astype(jnp.float32)
    for part in range(2):
        reverse[part] = lax.dot_general(
            bank[part],
            turned_to,
            (((0,), (0,)), ((), ())),
            precision=lax.Precision.HIGHEST,
            preferred_element_type=jnp.float32,
        )

    lane = lax.broadcasted_iota(jnp.int32, (SUBS, LANES), 1)
    sub = lax.broadcasted_iota(jnp.int32, (SUBS, LANES), 0)

    def merge(src, section, r, dst, at, count):
        half = 1 << section
        base = r - r % (2 * half) + r % half - r % min(half, CH_DEV)
        a = base + picks_ref[0, section, r]
        b = base + half + picks_ref[1, section, r]
        d = delay_ref[section, r]
        turn = (LANES - d) & (LANES - 1)
        keep = lane < LANES - d
        turned = [
            pltpu.roll(src[b, :, i * LANES : (i + 1) * LANES], turn, 1) for i in range(tiles + 1)
        ]
        for i in range(count):
            later = turned[min(i + 1, tiles)]
            dst[at, :, i * LANES : (i + 1) * LANES] = src[
                a, :, i * LANES : (i + 1) * LANES
            ] + jnp.where(keep, turned[i], later)

    def tree_part(c):
        @pl.loop(0, nb * blocks)
        def _(q):
            for ch in range(SUBS):
                r = q * SUBS + ch
                rows_of = pl.ds(ch, SUBS, stride=SUBS)
                for i in range(tiles + 1 - c):
                    buf_a[r, :, i * LANES : (i + 1) * LANES] = raw[q, c * tiles + i, rows_of, :]
                if c == 1:
                    up = pltpu.roll(raw[q, 0, rows_of, :], SUBS - 1, 0)
                    edge = jnp.broadcast_to(rim[q, ch : ch + 1, :], (SUBS, LANES))
                    buf_a[r, :, span:] = jnp.where(sub == SUBS - 1, edge, up)

        src, dst = buf_a, buf_b
        for section in range(sections - 1):

            @pl.loop(0, rows, unroll=16)
            def _(r, src=src, dst=dst, section=section):
                merge(src, section, r, dst, r, tiles + 1)

            src, dst = dst, src

        @pl.loop(0, everyone)
        def _(e):
            start = (e % nb) * CH_DEV + (e // nb) * trials

            @pl.loop(0, trials, unroll=trials)
            def _(i):
                merge(src, sections - 1, start + i, stage.at[e], i, tiles)

        copy = pltpu.make_async_copy(stage, sent[c], stage_sem)
        copy.start()
        copy.wait()

    def part_of(c, t):
        return (pl.ds(t, 1), 1 + t) if c else (slice(None), 0)

    def second(c, t, d):
        e = (me + d) % everyone
        which, at = part_of(c, t)
        return pltpu.make_async_remote_copy(
            sent[c].at[e, which],
            got[c].at[me, which],
            two_send.at[c],
            two_recv.at[at],
            device_id=device(e),
            device_id_type=MESH,
        )

    def send_second(c, t):
        @pl.loop(1, everyone)
        def _(d):
            second(c, t, d).start()

        which, at = part_of(c, t)
        pltpu.make_async_copy(
            sent[c].at[me, which], got[c].at[me, which], two_recv.at[at]
        ).start()

    def wait_second(c, t):
        which, at = part_of(c, t)
        landed(got[c].at[:, which], two_recv.at[at])

    for i in early:
        first_wait(i)
    rim_copy = pltpu.make_async_remote_copy(
        raw.at[:, 0, pl.ds(0, SUBS)],
        rim,
        rim_sems.at[0],
        rim_sems.at[1],
        device_id=device((me + everyone - 1) % everyone),
        device_id_type=MESH,
    )

    @pl.when(me > 0)
    def _():
        rim_copy.start()

    @pl.when(me == everyone - 1)
    def _():
        rim[...] = jnp.zeros_like(rim)

    tree_part(0)
    send_second(0, 0)
    for i in late:
        first_wait(i)

    @pl.when(me < everyone - 1)
    def _():
        rim_copy.wait_recv()

    tree_part(1)
    for t in range(min(AHEAD, trials)):
        send_second(1, t)
    landed(raw.at[pl.ds(0, (nb - 1) * blocks)], one_send)

    @pl.when(me > 0)
    def _():
        rim_copy.wait_send()

    for load in loads[4:]:
        load.wait()
    wait_second(0, 0)

    def bands_of(t):
        def row(z, part):
            return reverse[part, pl.ds(wanted_ref[z, t], 1), :]

        fill_bands(row, zsel, band_high, band_low)

    last = trials - 1

    @pl.loop(0, last)
    def _(t):
        bands_of(t)
        wait_second(1, t)

        @pl.when(t + AHEAD < trials)
        def _():
            send_second(1, t + AHEAD)

        def store(where, value):
            power[t, where, :] = value

        x = assemble([got[c][:, t] for c in range(2)], consts)
        powers_of(x, band_high[...], band_low[...], consts, zsel, taps // 2, store)

    bands_of(last)
    wait_second(1, last)
    x_copies = [
        pltpu.make_async_copy(got[c].at[:, last], last_x[c], last_sems.at[c]) for c in range(2)
    ]
    for copy in x_copies:
        copy.start()
    for copy in x_copies:
        copy.wait()
    for c in range(2):
        landed(sent[c].at[pl.ds(0, everyone - 1)], two_send.at[c])


def assemble(parts, consts):
    cols = consts[2].shape[0]
    parts = [part.reshape(-1, part.shape[-1]) for part in parts]
    return jnp.concatenate(
        [part[:, i : i + cols] for part in parts for i in range(0, part.shape[1], cols)], axis=0
    )


def last_kernel(zsel, half_taps, *refs):
    done_ref, early_x, late_x, band_high, band_low = refs[:5]
    consts, out_ref, power, move_sem, sem = refs[5:11], *refs[11:]
    count = done_ref.shape[0]
    move = pltpu.make_async_copy(done_ref, out_ref.at[pl.ds(0, count)], move_sem)
    move.start()
    x = assemble([early_x[...], late_x[...]], consts)

    def store(where, value):
        power[where, :] = value

    powers_of(x, band_high[...], band_low[...], consts, zsel, half_taps, store)
    final = pltpu.make_async_copy(power, out_ref.at[count], sem)
    final.start()
    move.wait()
    final.wait()


def fused(signal, picks, delays, template_bank, wanted, consts, zsel, taps, nb, nt):
    sections = picks.shape[1]
    channels = CH_DEV * nb
    everyone = nb * nt
    trials = CH_DEV // nt
    slab = signal.shape[1] // nb
    width = slab // SUBS
    span = width // 2
    blocks = CH_DEV // SUBS
    cols = consts[2].shape[0]
    outs = cols // 2
    rows = 2 * outs * zsel
    wide = 2 * zsel * LANES
    view = signal.reshape(blocks, SUBS, nb * SUBS, width).transpose(0, 2, 1, 3)
    view = view.reshape(blocks, nb, SUBS * SUBS, width)
    bank = template_bank.transpose(0, 2, 1)
    anywhere = pl.BlockSpec(memory_space=pl.ANY)
    dma = pltpu.SemaphoreType.DMA
    f32, bf16 = jnp.float32, jnp.bfloat16
    macs = cols * RADIX * 2 * RADIX + outs * 2 * cols * 2 * RADIX + 2 * outs * 4 * RADIX * RADIX
    exchanged = (everyone, trials, SUBS, span)
    kept = [
        pltpu.VMEM((trials - 1, rows, LANES), f32),
        *[pltpu.VMEM((everyone, SUBS, span), f32)] * 2,
        *[pltpu.VMEM((2 * RADIX, wide), bf16)] * 2,
        *[pltpu.VMEM(c.shape, c.dtype) for c in consts],
    ]
    vmem = pl.BlockSpec(memory_space=pltpu.VMEM)
    *handed, _, _ = pl.pallas_call(
        functools.partial(fused_kernel, nb, nt, sections, trials, zsel, taps),
        out_shape=kept + [jax.ShapeDtypeStruct(exchanged, f32)] * 2,
        in_specs=[anywhere] * 11,
        out_specs=[vmem] * len(kept) + [anywhere] * 2,
        scratch_shapes=[
            pltpu.VMEM((nb * blocks, width // LANES, SUBS * SUBS, LANES), f32),
            pltpu.VMEM((nb * blocks, SUBS, LANES), f32),
            pltpu.VMEM((channels, SUBS, span + LANES), f32),
            pltpu.VMEM((channels, SUBS, span + LANES), f32),
            pltpu.VMEM(exchanged, f32),
            pltpu.VMEM(exchanged, f32),
            pltpu.VMEM(exchanged, f32),
            pltpu.VMEM(bank.shape, f32),
            pltpu.VMEM(template_bank.shape[:2] + (RADIX,), f32),
            *[pltpu.SMEM(a.shape, jnp.int32) for a in (picks, delays, wanted.T)],
            dma,
            dma((width // LANES,)),
            dma((2,)),
            dma((1 + trials,)),
            dma((2,)),
            dma,
            dma((4 + len(consts),)),
            dma((2,)),
        ],
        compiler_params=pltpu.CompilerParams(
            collective_id=0, has_side_effects=True, vmem_limit_bytes=FUSED_LIMIT
        ),
        cost_estimate=pl.CostEstimate(
            flops=6 * trials * macs, bytes_accessed=3 * signal.size * 4, transcendentals=0
        ),
        name="fused",
    )(picks, delays, wanted.T, bank, view, *consts)
    return pl.pallas_call(
        functools.partial(last_kernel, zsel, taps // 2),
        out_shape=jax.ShapeDtypeStruct((trials, rows, LANES), f32),
        in_specs=[vmem] * len(kept),
        out_specs=anywhere,
        scratch_shapes=[pltpu.VMEM((rows, LANES), f32), dma, dma],
        compiler_params=pltpu.CompilerParams(vmem_limit_bytes=LAST_LIMIT),
        cost_estimate=pl.CostEstimate(
            flops=6 * macs, bytes_accessed=signal.size * 4, transcendentals=0
        ),
        name="last",
    )(*handed)


def on_device(signal, tree_picks, tree_delays, template_bank, template_pick):
    band_count = lax.axis_size("band")
    time_count = lax.axis_size("tm")
    everyone = band_count * time_count
    sections = LOGCD + band_count.bit_length() - 1
    rim_depth = sections * MAXD
    channels = CH_DEV * band_count
    samples = signal.shape[1] * time_count
    slab = signal.shape[1] // band_count
    width = slab // SUBS
    trials = CH_DEV // time_count
    last = max(1, 3 * trials // 16)
    counts = [count for count in (trials - last, last) if count]
    zsel = template_pick.shape[2]
    taps = template_bank.shape[2]
    cols = samples // RADIX
    if width % (2 * cols) == 0 and trials % 2 == 0 and trials >= 4:
        consts = [jnp.asarray(c) for c in tables(samples, channels, width, taps)]
        out = fused(
            signal, tree_picks, tree_delays, template_bank, template_pick[0], consts, zsel, taps,
            band_count, time_count,
        )
        return finish(out, trials, samples, zsel)

    band_high, band_low = bands(template_pick[0], template_bank)

    half = (1 << np.arange(sections))[:, None]
    r = np.arange(channels)[None, :]
    base = r - r % (2 * half) + r % half - r % np.minimum(half, CH_DEV)
    low = tree_picks[0] + base.astype(np.int32)
    high = tree_picks[1] + (base + half).astype(np.int32)
    grid = np.arange(channels).reshape(band_count, time_count, trials).transpose(1, 0, 2)
    firsts = [sum(counts[:q]) for q in range(len(counts))]
    order = np.concatenate(
        [grid[:, :, first : first + count].reshape(-1) for first, count in zip(firsts, counts)]
    ).astype(np.int32)
    tables_of = (low, high, tree_delays, jnp.asarray(order))
    sizes = [everyone * count for count in counts]

    folded = signal.reshape(CH_DEV, band_count, SUBS, width)

    def exchanged(value):
        value = lax.all_to_all(value, "band", split_axis=0, concat_axis=0, tiled=True)
        return value.reshape(channels, SUBS, -1)

    def rim_of(x):
        rim = shifted(x[:, 0, :rim_depth], ("tm", "band"), -1)
        rim = jnp.pad(rim, ((0, 0), (0, LANES - rim_depth)))
        return jnp.broadcast_to(rim[:, None, :], (channels, SUBS, LANES))

    if width % (2 * LANES) == 0:
        span = width // 2
        cut = span + LANES
        x_a = exchanged(folded[..., :cut].transpose(1, 0, 2, 3))
        x_b = after(after(folded[..., cut:].transpose(1, 0, 2, 3), x_a), band_low)
        x_b = exchanged(x_b)
        pieces = tree([x_a], [0], None, tables_of, sizes, width, span, 0, [])
        pieces = tree(
            [x_a, x_b], [span, 0], rim_of(x_a), tables_of, sizes, width, span, 1, pieces
        )
    else:
        x = exchanged(folded.transpose(1, 0, 2, 3))
        pieces = tree([x], [0], rim_of(x), tables_of, sizes, width, width, 0, [])

    consts = [jnp.asarray(c) for c in tables(samples, channels, width, taps)]
    out = None
    for first, count, piece in zip(firsts, counts, pieces):
        piece = piece.reshape(everyone, count, SUBS, width)
        if out is not None:
            piece = after(piece, arrived)
        arrived = lax.all_to_all(piece, ("tm", "band"), split_axis=0, concat_axis=0, tiled=True)
        out, _ = spectra(
            arrived, band_high, band_low, consts, zsel, taps, trials, first, out
        )
    return finish(out, trials, samples, zsel)


def solution(mesh):
    in_specs = (P(("beams", "band"), "tm"), P(), P(), P(), P(("beams", "band"), "tm", None))
    out_specs = P(("beams", "band"), "tm", None, None)
    return jax.shard_map(
        on_device, mesh=mesh, in_specs=in_specs, out_specs=out_specs, check_vma=False
    )
```

```python
import functools
import math

import jax
import jax.numpy as jnp
import ml_dtypes
import numpy as np
from jax import lax
from jax.experimental import pallas as pl
from jax.experimental.pallas import tpu as pltpu
from jax.sharding import PartitionSpec as P

CH_DEV = 64
LOGCD = 6
MAXD = 4
LANES = 128
SUBS = 8
RADIX = 256
LIMIT = 56 * 1024 * 1024
FUSED_LIMIT = 38 * 1024 * 1024
LAST_LIMIT = 14 * 1024 * 1024
AHEAD = 6
MESH = pl.DeviceIdType.MESH


def shifted(value, axis, steps):
    count = lax.axis_size(axis)
    first, last = (max(0, -steps), min(count, count - steps))
    return lax.ppermute(value, axis, [(source, source + steps) for source in range(first, last)])


def tree_kernel(sections, sizes, parts, has_rim, *refs):
    low_ref, high_ref, delay_ref, row_ref = refs[:4]
    xs, refs = refs[4 : 4 + len(parts)], refs[4 + len(parts) :]
    if has_rim:
        rim_ref, refs = refs[0], refs[1:]
    buf_a, buf_b = refs[-2:]
    outs = refs[len(refs) - 2 - len(sizes) : -2]
    rows, _, span = buf_a.shape
    tiles = span // LANES - 1
    lane = lax.broadcasted_iota(jnp.int32, (SUBS, LANES), 1)
    sub = lax.broadcasted_iota(jnp.int32, (SUBS, LANES), 0)

    @pl.loop(0, rows, unroll=4)
    def _(r):
        at = 0
        for x_ref, first in zip(xs, parts):
            count = x_ref.shape[2] - first
            buf_a[r, :, at : at + count] = x_ref[r, :, first:]
            at += count
        if has_rim:
            up = pltpu.roll(xs[0][r, :, 0:LANES], SUBS - 1, 0)
            buf_a[r, :, at : at + LANES] = jnp.where(sub == SUBS - 1, rim_ref[r], up)

    def merge(src, section, r, dst, at, count):
        a = low_ref[section, r]
        b = high_ref[section, r]
        d = delay_ref[section, r]
        turn = (LANES - d) & (LANES - 1)
        keep = lane < LANES - d
        turned = [
            pltpu.roll(src[b, :, i * LANES : (i + 1) * LANES], turn, 1) for i in range(tiles + 1)
        ]
        for i in range(count):
            later = turned[min(i + 1, tiles)]
            dst[at, :, i * LANES : (i + 1) * LANES] = src[
                a, :, i * LANES : (i + 1) * LANES
            ] + jnp.where(keep, turned[i], later)

    src, dst = buf_a, buf_b
    for section in range(sections - 1):

        @pl.loop(0, rows, unroll=16)
        def _(r, src=src, dst=dst, section=section):
            merge(src, section, r, dst, r, tiles + 1)

        src, dst = dst, src
    start = 0
    for size, out in zip(sizes, outs):

        @pl.loop(0, size, unroll=16)
        def _(i, start=start, src=src, out=out):
            merge(src, sections - 1, row_ref[start + i], out, i, tiles)

        start += size


def tree(xs, parts, rim, tables_of, sizes, width, span, place, so_far):
    rows = xs[0].shape[0]
    sections = tables_of[0].shape[0]
    smem = pl.BlockSpec(memory_space=pltpu.SMEM)
    vmem = pl.BlockSpec(memory_space=pltpu.VMEM)
    has_rim = rim is not None
    inputs = [*tables_of, *xs] + ([rim] if has_rim else [])
    known = len(inputs)
    return pl.pallas_call(
        functools.partial(tree_kernel, sections, sizes, parts, has_rim),
        grid=(1,),
        out_shape=[jax.ShapeDtypeStruct((size, SUBS, width), jnp.float32) for size in sizes],
        in_specs=[smem] * 4
        + [vmem] * (known - 4)
        + [pl.BlockSpec(memory_space=pl.ANY)] * len(so_far),
        out_specs=[pl.BlockSpec((size, SUBS, span), lambda i: (0, 0, place)) for size in sizes],
        input_output_aliases={known + i: i for i in range(len(so_far))},
        scratch_shapes=[pltpu.VMEM((rows, SUBS, span + LANES), jnp.float32)] * 2,
        compiler_params=pltpu.CompilerParams(vmem_limit_bytes=LIMIT),
        cost_estimate=pl.CostEstimate(
            flops=rows * SUBS * span * sections * 4,
            bytes_accessed=rows * SUBS * span * 8,
            transcendentals=0,
        ),
        name="tree",
    )(*inputs, *so_far)


def split(value):
    high = value.astype(jnp.bfloat16)
    return high, (value - high.astype(jnp.float32)).astype(jnp.bfloat16)


def fill_bands(row_of, zsel, high_ref, low_ref):
    for z in range(zsel):
        pair = []
        for part in range(2):
            wide = jnp.broadcast_to(row_of(z, part), (RADIX, RADIX))
            band = pltpu.roll(wide, 0, 1, stride=1, stride_axis=0)[:, :LANES]
            pair.append(split(band))
        at = 2 * z * LANES
        for ref, real, imag in (
            (high_ref, pair[0][0], pair[1][0]),
            (low_ref, pair[0][1], pair[1][1]),
        ):
            ref[:RADIX, at : at + LANES] = real
            ref[RADIX:, at : at + LANES] = -imag
            ref[:RADIX, at + LANES : at + 2 * LANES] = imag
            ref[RADIX:, at + LANES : at + 2 * LANES] = real


def bands_kernel(zsel, u_ref, high_ref, low_ref):
    def row_of(z, part):
        return u_ref[0, 2 * z + part : 2 * z + part + 1, :]

    fill_bands(row_of, zsel, high_ref.at[0], low_ref.at[0])


def reversed_taps(picks, template_bank):
    trials, zsel = picks.shape
    taps = template_bank.shape[2]
    onehot = (picks[:, :, None] == jnp.arange(template_bank.shape[1], dtype=jnp.int32)).astype(
        jnp.float32
    )
    reversed_bank = jnp.concatenate(
        [
            template_bank[:, :, :1],
            jnp.zeros(template_bank.shape[:2] + (RADIX - taps,), jnp.float32),
            template_bank[:, :, :0:-1],
        ],
        axis=2,
    )
    u = jnp.einsum("tzk,ckm->tzcm", onehot, reversed_bank, precision=lax.Precision.HIGHEST)
    return u.reshape(trials, 2 * zsel, RADIX)


def bands(picks, template_bank):
    trials, zsel = picks.shape
    u = reversed_taps(picks, template_bank)
    wide = 2 * zsel * LANES
    shape = jax.ShapeDtypeStruct((trials, 2 * RADIX, wide), jnp.bfloat16)
    spec = pl.BlockSpec((1, 2 * RADIX, wide), lambda t: (t, 0, 0))
    return pl.pallas_call(
        functools.partial(bands_kernel, zsel),
        grid=(trials,),
        out_shape=[shape, shape],
        in_specs=[pl.BlockSpec((1, 2 * zsel, RADIX), lambda t: (t, 0, 0))],
        out_specs=[spec, spec],
        compiler_params=pltpu.CompilerParams(vmem_limit_bytes=LIMIT),
        cost_estimate=pl.CostEstimate(
            flops=trials * RADIX * RADIX * 20,
            bytes_accessed=trials * 2 * RADIX * wide * 4,
            transcendentals=0,
        ),
        name="bands",
    )(u)


def tables(samples, channels, width, taps):
    cols = samples // RADIX
    outs = cols // 2
    split_by = width // cols if width % cols == 0 else 1
    place = np.arange(RADIX)
    row_of = split_by * (place % (RADIX // split_by)) + place // (RADIX // split_by)
    freq = (np.arange(RADIX) - taps // 2) % RADIX
    b = np.arange(cols)
    scale = 1.0 / math.sqrt(samples * channels)
    angle = 2.0 * np.pi / RADIX * (row_of[:, None] * freq[None, :] % RADIX)
    first = np.concatenate([np.cos(angle), -np.sin(angle)], axis=1) * scale
    angle = 2.0 * np.pi / samples * (b[:, None] * freq[None, :] % samples)
    tw_cos, tw_sin = np.cos(angle), np.sin(angle)
    angle = 2.0 * np.pi / cols * (np.arange(outs)[:, None] * b[None, :] % cols)
    second = np.concatenate([np.cos(angle), np.sin(angle)], axis=1)

    def parts(value):
        value = value.astype(np.float32)
        high = value.astype(ml_dtypes.bfloat16)
        return high, (value - high.astype(np.float32)).astype(ml_dtypes.bfloat16)

    return (
        *parts(first),
        tw_cos.astype(np.float32),
        tw_sin.astype(np.float32),
        *parts(second),
    )


def dot3(a_high, a_low, b_high, b_low):
    def dot(a, b):
        return jnp.dot(a, b, preferred_element_type=jnp.float32)

    return dot(a_high, b_high) + (dot(a_high, b_low) + dot(a_low, b_high))


def powers_of(x, band_high, band_low, consts, zsel, half_taps, store):
    fh, fl, tc, ts, sh, sl = consts
    cols = tc.shape[0]
    outs = cols // 2
    x_high, x_low = split(x.T)
    first = dot3(x_high, x_low, fh[...], fl[...])
    re, im = first[:, :RADIX], first[:, RADIX:]
    mid_re = re * tc[...] + im * ts[...]
    mid_im = im * tc[...] - re * ts[...]
    re_high, re_low = split(mid_re)
    im_high, im_low = split(mid_im)

    def block(a, b):
        return jnp.concatenate(
            [jnp.concatenate([a, b], axis=1), jnp.concatenate([b, -a], axis=1)], axis=0
        )

    spec = dot3(sh[...], sl[...], block(re_high, im_high), block(re_low, im_low))
    row = lax.broadcasted_iota(jnp.int32, (outs, RADIX), 0)
    lane = lax.broadcasted_iota(jnp.int32, (outs, RADIX), 1)
    even, odd = [], []
    for part in (spec[:, :RADIX], spec[:, RADIX:]):
        down = jnp.where(row == 0, 0.0, pltpu.roll(part, 1, 0))
        up = jnp.where(row == outs - 1, 0.0, pltpu.roll(part, outs - 1, 0))
        here = jnp.where(lane < half_taps, down, part)
        after = jnp.where(lane < half_taps, part, up)
        even.append(here)
        odd += [here[:, LANES:], after[:, :LANES]]
    window = jnp.concatenate(
        [jnp.concatenate(even, axis=1), jnp.concatenate(odd, axis=1)], axis=0
    )
    w_high, w_low = split(window)
    got = dot3(w_high, w_low, band_high, band_low)
    for z in range(zsel):
        at = 2 * z * LANES
        real, imag = got[:, at : at + LANES], got[:, at + LANES : at + 2 * LANES]
        power = real * real + imag * imag
        for e in range(2):
            store(pl.ds(e * zsel + z, outs, 2 * zsel), power[e * outs : (e + 1) * outs])


def spectra_kernel(zsel, half_taps, aliased, *refs):
    x_ref, bh_ref, bl_ref = refs[:3]
    consts = refs[3:9]
    out_ref, done_ref = refs[10:] if aliased else refs[9:]
    done_ref[...] = jnp.zeros_like(done_ref)
    cols = consts[2].shape[0]
    x = x_ref[...]
    x = x.reshape(-1, x.shape[-1])
    if x.shape[1] != cols:
        x = jnp.concatenate(
            [x[:, i * cols : (i + 1) * cols] for i in range(x.shape[1] // cols)], axis=0
        )

    def store(rows, value):
        out_ref[0, rows, :] = value

    powers_of(x, bh_ref[0], bl_ref[0], consts, zsel, half_taps, store)


def spectra(x, band_high, band_low, consts, zsel, taps, trials, first_trial, so_far):
    cols = consts[2].shape[0]
    outs = cols // 2
    rows = 2 * outs * zsel
    if x.shape[-1] % cols == 0:
        here = x.shape[1]
        x_spec = pl.BlockSpec((x.shape[0], 1, SUBS, x.shape[-1]), lambda t: (0, t, 0, 0))
    else:
        here = x.shape[1]
        x = x.transpose(1, 0, 2, 3).reshape(here, RADIX, cols)
        x_spec = pl.BlockSpec((1, RADIX, cols), lambda t: (t, 0, 0))
    band_spec = pl.BlockSpec(
        (1,) + band_high.shape[1:], lambda t: (first_trial + t, 0, 0)
    )
    whole = [pl.BlockSpec(c.shape, lambda t: (0, 0)) for c in consts]
    aliased = so_far is not None
    more = [so_far] if aliased else []
    macs = here * (cols * RADIX * 2 * RADIX + outs * 2 * cols * 2 * RADIX + 2 * outs * 4 * RADIX * RADIX)
    return pl.pallas_call(
        functools.partial(spectra_kernel, zsel, taps // 2, aliased),
        grid=(here,),
        out_shape=[
            jax.ShapeDtypeStruct((trials, rows, LANES), jnp.float32),
            jax.ShapeDtypeStruct((SUBS, LANES), jnp.float32),
        ],
        in_specs=[x_spec, band_spec, band_spec, *whole]
        + [pl.BlockSpec(memory_space=pl.ANY)] * len(more),
        out_specs=[
            pl.BlockSpec((1, rows, LANES), lambda t: (first_trial + t, 0, 0)),
            pl.BlockSpec((SUBS, LANES), lambda t: (0, 0)),
        ],
        input_output_aliases={9: 0} if aliased else {},
        compiler_params=pltpu.CompilerParams(vmem_limit_bytes=LIMIT),
        cost_estimate=pl.CostEstimate(
            flops=6 * macs, bytes_accessed=here * 2 * 1024 * 1024, transcendentals=0
        ),
        name="spectra",
    )(x, band_high, band_low, *consts, *more)


def after_kernel(value_ref, done_ref, out_ref):
    del value_ref, done_ref, out_ref


def after(value, done):
    anywhere = pl.BlockSpec(memory_space=pl.ANY)
    return pl.pallas_call(
        after_kernel,
        out_shape=jax.ShapeDtypeStruct(value.shape, value.dtype),
        in_specs=[anywhere, anywhere],
        out_specs=anywhere,
        input_output_aliases={0: 0},
        name="after",
    )(value, done)


def finish(out, trials, samples, zsel):
    out = out.reshape(trials, samples // 2 // LANES, zsel, LANES).transpose(0, 2, 1, 3)
    return out.reshape(1, trials, zsel, samples // 2)


def rim_pack(sections):
    return LANES >> (sections * MAXD - 1).bit_length()


def fused_kernel(
    nb, nt, sections, trials, zsel, taps,
    picks_hbm, delay_hbm, wanted_hbm, bank_ref, sig_ref, *refs
):
    const_refs, refs = refs[:6], refs[6:]
    power, got, band_high, band_low, refs = refs[0], refs[1:3], refs[3], refs[4], refs[5:]
    consts, sent, refs = refs[:6], refs[6:8], refs[8:]
    raw, rim, rim_sent, buf_a, buf_b, stage, refs = *refs[:6], refs[6:]
    bank, reverse, refs = *refs[:2], refs[2:]
    picks_ref, delay_ref, wanted_ref, refs = *refs[:3], refs[3:]
    (
        one_send, one_recv, two_send, two_recv, rim_sems, stage_sem, load_sems,
    ) = refs

    everyone = nb * nt
    rows, _, span = buf_a.shape
    span = span - LANES
    blocks = CH_DEV // SUBS
    tiles = span // LANES
    early = range(tiles + 1)
    late = range(tiles + 1, 2 * tiles)
    pack = rim_pack(sections)
    share = LANES // pack
    mt, mb = lax.axis_index("tm"), lax.axis_index("band")
    me = mt * nb + mb

    def device(e):
        return {"tm": e // nb, "band": e % nb}

    barrier = pltpu.get_barrier_semaphore()

    @pl.loop(1, everyone)
    def _(d):
        pl.semaphore_signal(
            barrier, 1, device_id=device((me + d) % everyone), device_id_type=MESH
        )

    pl.semaphore_wait(barrier, everyone - 1)

    def slab(i, k):
        return sig_ref.at[:, k, :, pl.ds(i * LANES, LANES)]

    def landed(ref, sem):
        pltpu.make_async_copy(ref, ref, sem).wait()

    def first(i, d):
        return pltpu.make_async_remote_copy(
            slab(i, (mb + d) % nb),
            raw.at[pl.ds(mb * blocks, blocks), i],
            one_send,
            one_recv.at[i],
            device_id={"band": (mb + d) % nb},
            device_id_type=MESH,
        )

    def first_own(i):
        return pltpu.make_async_copy(
            slab(i, mb), raw.at[pl.ds(mb * blocks, blocks), i], one_recv.at[i]
        )

    def first_wait(i):
        landed(raw.at[:, i], one_recv.at[i])

    apart = sorted(range(1, nb), key=lambda d: -min(d, nb - d))
    for i in (*early, *late):
        for d in apart:
            first(i, d).start()
        first_own(i).start()
    loads = [
        pltpu.make_async_copy(a, b, load_sems.at[i])
        for i, (a, b) in enumerate(zip(
            (bank_ref, picks_hbm, delay_hbm, wanted_hbm, *const_refs),
            (bank, picks_ref, delay_ref, wanted_ref, *consts),
        ))
    ]
    for load in loads:
        load.start()

    for load in loads[:4]:
        load.wait()
    turn_row = lax.broadcasted_iota(jnp.int32, (taps, RADIX), 0)
    turn_lane = lax.broadcasted_iota(jnp.int32, (taps, RADIX), 1)
    turned_to = jnp.where((turn_row + turn_lane) % RADIX == 0, 1.0, 0.0).astype(jnp.float32)
    for part in range(2):
        reverse[part] = lax.dot_general(
            bank[part],
            turned_to,
            (((0,), (0,)), ((), ())),
            precision=lax.Precision.HIGHEST,
            preferred_element_type=jnp.float32,
        )

    lane = lax.broadcasted_iota(jnp.int32, (SUBS, LANES), 1)
    sub = lax.broadcasted_iota(jnp.int32, (SUBS, LANES), 0)

    def merge(src, section, r, dst, at, count):
        half = 1 << section
        base = r - r % (2 * half) + r % half - r % min(half, CH_DEV)
        a = base + picks_ref[0, section, r]
        b = base + half + picks_ref[1, section, r]
        d = delay_ref[section, r]
        turn = (LANES - d) & (LANES - 1)
        keep = lane < LANES - d
        turned = [
            pltpu.roll(src[b, :, i * LANES : (i + 1) * LANES], turn, 1) for i in range(tiles + 1)
        ]
        for i in range(count):
            later = turned[min(i + 1, tiles)]
            dst[at, :, i * LANES : (i + 1) * LANES] = src[
                a, :, i * LANES : (i + 1) * LANES
            ] + jnp.where(keep, turned[i], later)

    def tree_part(c):
        @pl.loop(0, nb * blocks)
        def _(q):
            for ch in range(SUBS):
                r = q * SUBS + ch
                rows_of = pl.ds(ch, SUBS, stride=SUBS)
                for i in range(tiles + 1 - c):
                    buf_a[r, :, i * LANES : (i + 1) * LANES] = raw[q, c * tiles + i, rows_of, :]
                if c == 1:
                    edges = pltpu.roll(rim[q // pack], (LANES - (q % pack) * share) % LANES, 1)
                    up = pltpu.roll(raw[q, 0, rows_of, :], SUBS - 1, 0)
                    edge = jnp.broadcast_to(edges[ch : ch + 1], (SUBS, LANES))
                    buf_a[r, :, span:] = jnp.where(sub == SUBS - 1, edge, up)

        src, dst = buf_a, buf_b
        for section in range(sections - 1):

            @pl.loop(0, rows, unroll=16)
            def _(r, src=src, dst=dst, section=section):
                merge(src, section, r, dst, r, tiles + 1)

            src, dst = dst, src

        @pl.loop(0, everyone)
        def _(e):
            start = (e % nb) * CH_DEV + (e // nb) * trials

            @pl.loop(0, trials, unroll=trials)
            def _(i):
                merge(src, sections - 1, start + i, stage.at[e], i, tiles)

        copy = pltpu.make_async_copy(stage, sent[c], stage_sem)
        copy.start()
        copy.wait()

    def part_of(c, t):
        return (pl.ds(t, 1), 1 + t) if c else (slice(None), 0)

    def second(c, t, d):
        e = (me + d) % everyone
        which, at = part_of(c, t)
        return pltpu.make_async_remote_copy(
            sent[c].at[e, which],
            got[c].at[me, which],
            two_send.at[c],
            two_recv.at[at],
            device_id=device(e),
            device_id_type=MESH,
        )

    def send_second(c, t):
        @pl.loop(1, everyone)
        def _(d):
            second(c, t, d).start()

        which, at = part_of(c, t)
        pltpu.make_async_copy(
            sent[c].at[me, which], got[c].at[me, which], two_recv.at[at]
        ).start()

    def wait_second(c, t):
        which, at = part_of(c, t)
        landed(got[c].at[:, which], two_recv.at[at])

    for i in early:
        first_wait(i)

    @pl.loop(0, nb * blocks // pack)
    def _(q):
        packed = raw[q * pack, 0, :SUBS, :]
        for p in range(1, pack):
            moved = pltpu.roll(raw[q * pack + p, 0, :SUBS, :], p * share, 1)
            packed = jnp.where(lane < p * share, packed, moved)
        rim_sent[q] = packed

    rim_copy = pltpu.make_async_remote_copy(
        rim_sent,
        rim,
        rim_sems.at[0],
        rim_sems.at[1],
        device_id=device((me + everyone - 1) % everyone),
        device_id_type=MESH,
    )

    @pl.when(me > 0)
    def _():
        rim_copy.start()

    @pl.when(me == everyone - 1)
    def _():
        rim[...] = jnp.zeros_like(rim)

    tree_part(0)
    send_second(0, 0)
    for i in late:
        first_wait(i)

    @pl.when(me < everyone - 1)
    def _():
        rim_copy.wait_recv()

    tree_part(1)
    for t in range(min(AHEAD, trials)):
        send_second(1, t)
    landed(raw.at[pl.ds(0, (nb - 1) * blocks)], one_send)

    @pl.when(me > 0)
    def _():
        rim_copy.wait_send()

    for load in loads[4:]:
        load.wait()
    wait_second(0, 0)

    def bands_of(t):
        def row(z, part):
            return reverse[part, pl.ds(wanted_ref[z, t], 1), :]

        fill_bands(row, zsel, band_high, band_low)

    last = trials - 1

    @pl.loop(0, last)
    def _(t):
        bands_of(t)
        wait_second(1, t)

        @pl.when(t + AHEAD < trials)
        def _():
            send_second(1, t + AHEAD)

        def store(where, value):
            power[t, where, :] = value

        x = assemble([got[c][:, t] for c in range(2)], consts)
        powers_of(x, band_high[...], band_low[...], consts, zsel, taps // 2, store)

    bands_of(last)
    wait_second(1, last)
    for c in range(2):
        landed(sent[c].at[pl.ds(0, everyone - 1)], two_send.at[c])


def assemble(parts, consts):
    cols = consts[2].shape[0]
    parts = [part.reshape(-1, part.shape[-1]) for part in parts]
    return jnp.concatenate(
        [part[:, i : i + cols] for part in parts for i in range(0, part.shape[1], cols)], axis=0
    )


def last_kernel(zsel, half_taps, *refs):
    done_ref, got, (band_high, band_low) = refs[0], refs[1:3], refs[3:5]
    consts, out_ref, power, move_sem, sem = refs[5:11], *refs[11:]
    count = done_ref.shape[0]
    move = pltpu.make_async_copy(done_ref, out_ref.at[pl.ds(0, count)], move_sem)
    move.start()
    x = assemble([ref[:, count] for ref in got], consts)

    def store(where, value):
        power[where, :] = value

    powers_of(x, band_high[...], band_low[...], consts, zsel, half_taps, store)
    final = pltpu.make_async_copy(power, out_ref.at[count], sem)
    final.start()
    move.wait()
    final.wait()


def fused(signal, picks, delays, template_bank, wanted, consts, zsel, taps, nb, nt):
    sections = picks.shape[1]
    channels = CH_DEV * nb
    everyone = nb * nt
    trials = CH_DEV // nt
    slab = signal.shape[1] // nb
    width = slab // SUBS
    span = width // 2
    blocks = CH_DEV // SUBS
    cols = consts[2].shape[0]
    outs = cols // 2
    rows = 2 * outs * zsel
    wide = 2 * zsel * LANES
    view = signal.reshape(blocks, SUBS, nb * SUBS, width).transpose(0, 2, 1, 3)
    view = view.reshape(blocks, nb, SUBS * SUBS, width)
    bank = template_bank.transpose(0, 2, 1)
    anywhere = pl.BlockSpec(memory_space=pl.ANY)
    dma = pltpu.SemaphoreType.DMA
    f32, bf16 = jnp.float32, jnp.bfloat16
    macs = cols * RADIX * 2 * RADIX + outs * 2 * cols * 2 * RADIX + 2 * outs * 4 * RADIX * RADIX
    exchanged = (everyone, trials, SUBS, span)
    kept = [
        pltpu.VMEM((trials - 1, rows, LANES), f32),
        *[pltpu.VMEM(exchanged, f32)] * 2,
        *[pltpu.VMEM((2 * RADIX, wide), bf16)] * 2,
        *[pltpu.VMEM(c.shape, c.dtype) for c in consts],
    ]
    vmem = pl.BlockSpec(memory_space=pltpu.VMEM)
    *handed, _, _ = pl.pallas_call(
        functools.partial(fused_kernel, nb, nt, sections, trials, zsel, taps),
        out_shape=kept + [jax.ShapeDtypeStruct(exchanged, f32)] * 2,
        in_specs=[anywhere] * 11,
        out_specs=[vmem] * len(kept) + [anywhere] * 2,
        scratch_shapes=[
            pltpu.VMEM((nb * blocks, width // LANES, SUBS * SUBS, LANES), f32),
            *[pltpu.VMEM((nb * blocks // rim_pack(sections), SUBS, LANES), f32)] * 2,
            pltpu.VMEM((channels, SUBS, span + LANES), f32),
            pltpu.VMEM((channels, SUBS, span + LANES), f32),
            pltpu.VMEM(exchanged, f32),
            pltpu.VMEM(bank.shape, f32),
            pltpu.VMEM(template_bank.shape[:2] + (RADIX,), f32),
            *[pltpu.SMEM(a.shape, jnp.int32) for a in (picks, delays, wanted.T)],
            dma,
            dma((width // LANES,)),
            dma((2,)),
            dma((1 + trials,)),
            dma((2,)),
            dma,
            dma((4 + len(consts),)),
        ],
        compiler_params=pltpu.CompilerParams(
            collective_id=0, has_side_effects=True, vmem_limit_bytes=FUSED_LIMIT
        ),
        cost_estimate=pl.CostEstimate(
            flops=6 * trials * macs, bytes_accessed=3 * signal.size * 4, transcendentals=0
        ),
        name="fused",
    )(picks, delays, wanted.T, bank, view, *consts)
    return pl.pallas_call(
        functools.partial(last_kernel, zsel, taps // 2),
        out_shape=jax.ShapeDtypeStruct((trials, rows, LANES), f32),
        in_specs=[vmem] * len(kept),
        out_specs=anywhere,
        scratch_shapes=[pltpu.VMEM((rows, LANES), f32), dma, dma],
        compiler_params=pltpu.CompilerParams(vmem_limit_bytes=LAST_LIMIT),
        cost_estimate=pl.CostEstimate(
            flops=6 * macs, bytes_accessed=signal.size * 4, transcendentals=0
        ),
        name="last",
    )(*handed)


def on_device(signal, tree_picks, tree_delays, template_bank, template_pick):
    band_count = lax.axis_size("band")
    time_count = lax.axis_size("tm")
    everyone = band_count * time_count
    sections = LOGCD + band_count.bit_length() - 1
    rim_depth = sections * MAXD
    channels = CH_DEV * band_count
    samples = signal.shape[1] * time_count
    slab = signal.shape[1] // band_count
    width = slab // SUBS
    trials = CH_DEV // time_count
    last = max(1, 3 * trials // 16)
    counts = [count for count in (trials - last, last) if count]
    zsel = template_pick.shape[2]
    taps = template_bank.shape[2]
    cols = samples // RADIX
    if width % (2 * cols) == 0 and trials % 2 == 0 and trials >= 4:
        consts = [jnp.asarray(c) for c in tables(samples, channels, width, taps)]
        out = fused(
            signal, tree_picks, tree_delays, template_bank, template_pick[0], consts, zsel, taps,
            band_count, time_count,
        )
        return finish(out, trials, samples, zsel)

    band_high, band_low = bands(template_pick[0], template_bank)

    half = (1 << np.arange(sections))[:, None]
    r = np.arange(channels)[None, :]
    base = r - r % (2 * half) + r % half - r % np.minimum(half, CH_DEV)
    low = tree_picks[0] + base.astype(np.int32)
    high = tree_picks[1] + (base + half).astype(np.int32)
    grid = np.arange(channels).reshape(band_count, time_count, trials).transpose(1, 0, 2)
    firsts = [sum(counts[:q]) for q in range(len(counts))]
    order = np.concatenate(
        [grid[:, :, first : first + count].reshape(-1) for first, count in zip(firsts, counts)]
    ).astype(np.int32)
    tables_of = (low, high, tree_delays, jnp.asarray(order))
    sizes = [everyone * count for count in counts]

    folded = signal.reshape(CH_DEV, band_count, SUBS, width)

    def exchanged(value):
        value = lax.all_to_all(value, "band", split_axis=0, concat_axis=0, tiled=True)
        return value.reshape(channels, SUBS, -1)

    def rim_of(x):
        rim = shifted(x[:, 0, :rim_depth], ("tm", "band"), -1)
        rim = jnp.pad(rim, ((0, 0), (0, LANES - rim_depth)))
        return jnp.broadcast_to(rim[:, None, :], (channels, SUBS, LANES))

    if width % (2 * LANES) == 0:
        span = width // 2
        cut = span + LANES
        x_a = exchanged(folded[..., :cut].transpose(1, 0, 2, 3))
        x_b = after(after(folded[..., cut:].transpose(1, 0, 2, 3), x_a), band_low)
        x_b = exchanged(x_b)
        pieces = tree([x_a], [0], None, tables_of, sizes, width, span, 0, [])
        pieces = tree(
            [x_a, x_b], [span, 0], rim_of(x_a), tables_of, sizes, width, span, 1, pieces
        )
    else:
        x = exchanged(folded.transpose(1, 0, 2, 3))
        pieces = tree([x], [0], rim_of(x), tables_of, sizes, width, width, 0, [])

    consts = [jnp.asarray(c) for c in tables(samples, channels, width, taps)]
    out = None
    for first, count, piece in zip(firsts, counts, pieces):
        piece = piece.reshape(everyone, count, SUBS, width)
        if out is not None:
            piece = after(piece, arrived)
        arrived = lax.all_to_all(piece, ("tm", "band"), split_axis=0, concat_axis=0, tiled=True)
        out, _ = spectra(
            arrived, band_high, band_low, consts, zsel, taps, trials, first, out
        )
    return finish(out, trials, samples, zsel)


def solution(mesh):
    in_specs = (P(("beams", "band"), "tm"), P(), P(), P(), P(("beams", "band"), "tm", None))
    out_specs = P(("beams", "band"), "tm", None, None)
    return jax.shard_map(
        on_device, mesh=mesh, in_specs=in_specs, out_specs=out_specs, check_vma=False
    )
```

```python
import functools
import math

import jax
import jax.numpy as jnp
import ml_dtypes
import numpy as np
from jax import lax
from jax.experimental import pallas as pl
from jax.experimental.pallas import tpu as pltpu
from jax.sharding import PartitionSpec as P

CH_DEV = 64
LOGCD = 6
MAXD = 4
LANES = 128
SUBS = 8
RADIX = 256
LIMIT = 56 * 1024 * 1024
FUSED_LIMIT = 38 * 1024 * 1024
LAST_LIMIT = 14 * 1024 * 1024
AHEAD = 6
MESH = pl.DeviceIdType.MESH


def shifted(value, axis, steps):
    count = lax.axis_size(axis)
    first, last = (max(0, -steps), min(count, count - steps))
    return lax.ppermute(value, axis, [(source, source + steps) for source in range(first, last)])


def tree_kernel(sections, sizes, parts, has_rim, *refs):
    low_ref, high_ref, delay_ref, row_ref = refs[:4]
    xs, refs = refs[4 : 4 + len(parts)], refs[4 + len(parts) :]
    if has_rim:
        rim_ref, refs = refs[0], refs[1:]
    buf_a, buf_b = refs[-2:]
    outs = refs[len(refs) - 2 - len(sizes) : -2]
    rows, _, span = buf_a.shape
    tiles = span // LANES - 1
    lane = lax.broadcasted_iota(jnp.int32, (SUBS, LANES), 1)
    sub = lax.broadcasted_iota(jnp.int32, (SUBS, LANES), 0)

    @pl.loop(0, rows, unroll=4)
    def _(r):
        at = 0
        for x_ref, first in zip(xs, parts):
            count = x_ref.shape[2] - first
            buf_a[r, :, at : at + count] = x_ref[r, :, first:]
            at += count
        if has_rim:
            up = pltpu.roll(xs[0][r, :, 0:LANES], SUBS - 1, 0)
            buf_a[r, :, at : at + LANES] = jnp.where(sub == SUBS - 1, rim_ref[r], up)

    def merge(src, section, r, dst, at, count):
        a = low_ref[section, r]
        b = high_ref[section, r]
        d = delay_ref[section, r]
        turn = (LANES - d) & (LANES - 1)
        keep = lane < LANES - d
        turned = [
            pltpu.roll(src[b, :, i * LANES : (i + 1) * LANES], turn, 1) for i in range(tiles + 1)
        ]
        for i in range(count):
            later = turned[min(i + 1, tiles)]
            dst[at, :, i * LANES : (i + 1) * LANES] = src[
                a, :, i * LANES : (i + 1) * LANES
            ] + jnp.where(keep, turned[i], later)

    src, dst = buf_a, buf_b
    for section in range(sections - 1):

        @pl.loop(0, rows, unroll=16)
        def _(r, src=src, dst=dst, section=section):
            merge(src, section, r, dst, r, tiles + 1)

        src, dst = dst, src
    start = 0
    for size, out in zip(sizes, outs):

        @pl.loop(0, size, unroll=16)
        def _(i, start=start, src=src, out=out):
            merge(src, sections - 1, row_ref[start + i], out, i, tiles)

        start += size


def tree(xs, parts, rim, tables_of, sizes, width, span, place, so_far):
    rows = xs[0].shape[0]
    sections = tables_of[0].shape[0]
    smem = pl.BlockSpec(memory_space=pltpu.SMEM)
    vmem = pl.BlockSpec(memory_space=pltpu.VMEM)
    has_rim = rim is not None
    inputs = [*tables_of, *xs] + ([rim] if has_rim else [])
    known = len(inputs)
    return pl.pallas_call(
        functools.partial(tree_kernel, sections, sizes, parts, has_rim),
        grid=(1,),
        out_shape=[jax.ShapeDtypeStruct((size, SUBS, width), jnp.float32) for size in sizes],
        in_specs=[smem] * 4
        + [vmem] * (known - 4)
        + [pl.BlockSpec(memory_space=pl.ANY)] * len(so_far),
        out_specs=[pl.BlockSpec((size, SUBS, span), lambda i: (0, 0, place)) for size in sizes],
        input_output_aliases={known + i: i for i in range(len(so_far))},
        scratch_shapes=[pltpu.VMEM((rows, SUBS, span + LANES), jnp.float32)] * 2,
        compiler_params=pltpu.CompilerParams(vmem_limit_bytes=LIMIT),
        cost_estimate=pl.CostEstimate(
            flops=rows * SUBS * span * sections * 4,
            bytes_accessed=rows * SUBS * span * 8,
            transcendentals=0,
        ),
        name="tree",
    )(*inputs, *so_far)


def split(value):
    high = value.astype(jnp.bfloat16)
    return high, (value - high.astype(jnp.float32)).astype(jnp.bfloat16)


def fill_bands(row_of, zsel, high_ref, low_ref):
    for z in range(zsel):
        pair = []
        for part in range(2):
            wide = jnp.broadcast_to(row_of(z, part), (RADIX, RADIX))
            band = pltpu.roll(wide, 0, 1, stride=1, stride_axis=0)[:, :LANES]
            pair.append(split(band))
        at = 2 * z * LANES
        for ref, real, imag in (
            (high_ref, pair[0][0], pair[1][0]),
            (low_ref, pair[0][1], pair[1][1]),
        ):
            ref[:RADIX, at : at + LANES] = real
            ref[RADIX:, at : at + LANES] = -imag
            ref[:RADIX, at + LANES : at + 2 * LANES] = imag
            ref[RADIX:, at + LANES : at + 2 * LANES] = real


def bands_kernel(zsel, u_ref, high_ref, low_ref):
    def row_of(z, part):
        return u_ref[0, 2 * z + part : 2 * z + part + 1, :]

    fill_bands(row_of, zsel, high_ref.at[0], low_ref.at[0])


def reversed_taps(picks, template_bank):
    trials, zsel = picks.shape
    taps = template_bank.shape[2]
    onehot = (picks[:, :, None] == jnp.arange(template_bank.shape[1], dtype=jnp.int32)).astype(
        jnp.float32
    )
    reversed_bank = jnp.concatenate(
        [
            template_bank[:, :, :1],
            jnp.zeros(template_bank.shape[:2] + (RADIX - taps,), jnp.float32),
            template_bank[:, :, :0:-1],
        ],
        axis=2,
    )
    u = jnp.einsum("tzk,ckm->tzcm", onehot, reversed_bank, precision=lax.Precision.HIGHEST)
    return u.reshape(trials, 2 * zsel, RADIX)


def bands(picks, template_bank):
    trials, zsel = picks.shape
    u = reversed_taps(picks, template_bank)
    wide = 2 * zsel * LANES
    shape = jax.ShapeDtypeStruct((trials, 2 * RADIX, wide), jnp.bfloat16)
    spec = pl.BlockSpec((1, 2 * RADIX, wide), lambda t: (t, 0, 0))
    return pl.pallas_call(
        functools.partial(bands_kernel, zsel),
        grid=(trials,),
        out_shape=[shape, shape],
        in_specs=[pl.BlockSpec((1, 2 * zsel, RADIX), lambda t: (t, 0, 0))],
        out_specs=[spec, spec],
        compiler_params=pltpu.CompilerParams(vmem_limit_bytes=LIMIT),
        cost_estimate=pl.CostEstimate(
            flops=trials * RADIX * RADIX * 20,
            bytes_accessed=trials * 2 * RADIX * wide * 4,
            transcendentals=0,
        ),
        name="bands",
    )(u)


def tables(samples, channels, width, taps):
    cols = samples // RADIX
    outs = cols // 2
    split_by = width // cols if width % cols == 0 else 1
    place = np.arange(RADIX)
    row_of = split_by * (place % (RADIX // split_by)) + place // (RADIX // split_by)
    freq = (np.arange(RADIX) - taps // 2) % RADIX
    b = np.arange(cols)
    scale = 1.0 / math.sqrt(samples * channels)
    angle = 2.0 * np.pi / RADIX * (row_of[:, None] * freq[None, :] % RADIX)
    first = np.concatenate([np.cos(angle), -np.sin(angle)], axis=1) * scale
    angle = 2.0 * np.pi / samples * (b[:, None] * freq[None, :] % samples)
    tw_cos, tw_sin = np.cos(angle), np.sin(angle)
    angle = 2.0 * np.pi / cols * (np.arange(outs)[:, None] * b[None, :] % cols)
    second = np.concatenate([np.cos(angle), np.sin(angle)], axis=1)

    def parts(value):
        value = value.astype(np.float32)
        high = value.astype(ml_dtypes.bfloat16)
        return high, (value - high.astype(np.float32)).astype(ml_dtypes.bfloat16)

    return (
        *parts(first),
        tw_cos.astype(np.float32),
        tw_sin.astype(np.float32),
        *parts(second),
    )


def dot3(a_high, a_low, b_high, b_low):
    def dot(a, b):
        return jnp.dot(a, b, preferred_element_type=jnp.float32)

    return dot(a_high, b_high) + (dot(a_high, b_low) + dot(a_low, b_high))


def powers_of(x, band_high, band_low, consts, zsel, half_taps, store):
    fh, fl, tc, ts, sh, sl = consts
    cols = tc.shape[0]
    outs = cols // 2
    x_high, x_low = split(x.T)
    first = dot3(x_high, x_low, fh[...], fl[...])
    re, im = first[:, :RADIX], first[:, RADIX:]
    mid_re = re * tc[...] + im * ts[...]
    mid_im = im * tc[...] - re * ts[...]
    re_high, re_low = split(mid_re)
    im_high, im_low = split(mid_im)

    def block(a, b):
        return jnp.concatenate(
            [jnp.concatenate([a, b], axis=1), jnp.concatenate([b, -a], axis=1)], axis=0
        )

    spec = dot3(sh[...], sl[...], block(re_high, im_high), block(re_low, im_low))
    row = lax.broadcasted_iota(jnp.int32, (outs, RADIX), 0)
    lane = lax.broadcasted_iota(jnp.int32, (outs, RADIX), 1)
    even, odd = [], []
    for part in (spec[:, :RADIX], spec[:, RADIX:]):
        down = jnp.where(row == 0, 0.0, pltpu.roll(part, 1, 0))
        up = jnp.where(row == outs - 1, 0.0, pltpu.roll(part, outs - 1, 0))
        here = jnp.where(lane < half_taps, down, part)
        after = jnp.where(lane < half_taps, part, up)
        even.append(here)
        odd += [here[:, LANES:], after[:, :LANES]]
    window = jnp.concatenate(
        [jnp.concatenate(even, axis=1), jnp.concatenate(odd, axis=1)], axis=0
    )
    w_high, w_low = split(window)
    got = dot3(w_high, w_low, band_high, band_low)
    for z in range(zsel):
        at = 2 * z * LANES
        real, imag = got[:, at : at + LANES], got[:, at + LANES : at + 2 * LANES]
        power = real * real + imag * imag
        for e in range(2):
            store(pl.ds(e * zsel + z, outs, 2 * zsel), power[e * outs : (e + 1) * outs])


def spectra_kernel(zsel, half_taps, aliased, *refs):
    x_ref, bh_ref, bl_ref = refs[:3]
    consts = refs[3:9]
    out_ref, done_ref = refs[10:] if aliased else refs[9:]
    done_ref[...] = jnp.zeros_like(done_ref)
    cols = consts[2].shape[0]
    x = x_ref[...]
    x = x.reshape(-1, x.shape[-1])
    if x.shape[1] != cols:
        x = jnp.concatenate(
            [x[:, i * cols : (i + 1) * cols] for i in range(x.shape[1] // cols)], axis=0
        )

    def store(rows, value):
        out_ref[0, rows, :] = value

    powers_of(x, bh_ref[0], bl_ref[0], consts, zsel, half_taps, store)


def spectra(x, band_high, band_low, consts, zsel, taps, trials, first_trial, so_far):
    cols = consts[2].shape[0]
    outs = cols // 2
    rows = 2 * outs * zsel
    if x.shape[-1] % cols == 0:
        here = x.shape[1]
        x_spec = pl.BlockSpec((x.shape[0], 1, SUBS, x.shape[-1]), lambda t: (0, t, 0, 0))
    else:
        here = x.shape[1]
        x = x.transpose(1, 0, 2, 3).reshape(here, RADIX, cols)
        x_spec = pl.BlockSpec((1, RADIX, cols), lambda t: (t, 0, 0))
    band_spec = pl.BlockSpec(
        (1,) + band_high.shape[1:], lambda t: (first_trial + t, 0, 0)
    )
    whole = [pl.BlockSpec(c.shape, lambda t: (0, 0)) for c in consts]
    aliased = so_far is not None
    more = [so_far] if aliased else []
    macs = here * (cols * RADIX * 2 * RADIX + outs * 2 * cols * 2 * RADIX + 2 * outs * 4 * RADIX * RADIX)
    return pl.pallas_call(
        functools.partial(spectra_kernel, zsel, taps // 2, aliased),
        grid=(here,),
        out_shape=[
            jax.ShapeDtypeStruct((trials, rows, LANES), jnp.float32),
            jax.ShapeDtypeStruct((SUBS, LANES), jnp.float32),
        ],
        in_specs=[x_spec, band_spec, band_spec, *whole]
        + [pl.BlockSpec(memory_space=pl.ANY)] * len(more),
        out_specs=[
            pl.BlockSpec((1, rows, LANES), lambda t: (first_trial + t, 0, 0)),
            pl.BlockSpec((SUBS, LANES), lambda t: (0, 0)),
        ],
        input_output_aliases={9: 0} if aliased else {},
        compiler_params=pltpu.CompilerParams(vmem_limit_bytes=LIMIT),
        cost_estimate=pl.CostEstimate(
            flops=6 * macs, bytes_accessed=here * 2 * 1024 * 1024, transcendentals=0
        ),
        name="spectra",
    )(x, band_high, band_low, *consts, *more)


def after_kernel(value_ref, done_ref, out_ref):
    del value_ref, done_ref, out_ref


def after(value, done):
    anywhere = pl.BlockSpec(memory_space=pl.ANY)
    return pl.pallas_call(
        after_kernel,
        out_shape=jax.ShapeDtypeStruct(value.shape, value.dtype),
        in_specs=[anywhere, anywhere],
        out_specs=anywhere,
        input_output_aliases={0: 0},
        name="after",
    )(value, done)


def finish(out, trials, samples, zsel):
    out = out.reshape(trials, samples // 2 // LANES, zsel, LANES).transpose(0, 2, 1, 3)
    return out.reshape(1, trials, zsel, samples // 2)


def rim_pack(sections):
    return LANES >> (sections * MAXD - 1).bit_length()


def fused_kernel(
    nb, nt, sections, trials, zsel, taps,
    picks_hbm, delay_hbm, wanted_hbm, bank_ref, sig_ref, *refs
):
    const_refs, refs = refs[:6], refs[6:]
    power, got, band_high, band_low, refs = refs[0], refs[1:3], refs[3], refs[4], refs[5:]
    consts, sent, refs = refs[:6], refs[6:8], refs[8:]
    raw, rim, rim_sent, buf_a, buf_b, stage, refs = *refs[:6], refs[6:]
    bank, reverse, refs = *refs[:2], refs[2:]
    picks_ref, delay_ref, wanted_ref, refs = *refs[:3], refs[3:]
    (
        one_send, one_recv, two_send, two_recv, rim_sems, stage_sem, load_sems,
    ) = refs

    everyone = nb * nt
    rows, _, span = buf_a.shape
    span = span - LANES
    blocks = CH_DEV // SUBS
    tiles = span // LANES
    early = range(tiles + 1)
    late = range(tiles + 1, 2 * tiles)
    pack = rim_pack(sections)
    share = LANES // pack
    mt, mb = lax.axis_index("tm"), lax.axis_index("band")
    me = mt * nb + mb

    def device(e):
        return {"tm": e // nb, "band": e % nb}

    barrier = pltpu.get_barrier_semaphore()

    @pl.loop(1, everyone)
    def _(d):
        pl.semaphore_signal(
            barrier, 1, device_id=device((me + d) % everyone), device_id_type=MESH
        )

    pl.semaphore_wait(barrier, everyone - 1)

    def slab(i, k):
        return sig_ref.at[:, k, :, pl.ds(i * LANES, LANES)]

    def landed(ref, sem):
        pltpu.make_async_copy(ref, ref, sem).wait()

    def first(i, d):
        return pltpu.make_async_remote_copy(
            slab(i, (mb + d) % nb),
            raw.at[pl.ds(mb * blocks, blocks), i],
            one_send,
            one_recv.at[i],
            device_id={"band": (mb + d) % nb},
            device_id_type=MESH,
        )

    def first_own(i):
        return pltpu.make_async_copy(
            slab(i, mb), raw.at[pl.ds(mb * blocks, blocks), i], one_recv.at[i]
        )

    def first_wait(i):
        landed(raw.at[:, i], one_recv.at[i])

    apart = sorted(range(1, nb), key=lambda d: -min(d, nb - d))
    for i in (*early, *late):
        for d in apart:
            first(i, d).start()
        first_own(i).start()
    loads = [
        pltpu.make_async_copy(a, b, load_sems.at[i])
        for i, (a, b) in enumerate(zip(
            (bank_ref, picks_hbm, delay_hbm, wanted_hbm, *const_refs),
            (bank, picks_ref, delay_ref, wanted_ref, *consts),
        ))
    ]
    for load in loads:
        load.start()

    for load in loads[:4]:
        load.wait()
    turn_row = lax.broadcasted_iota(jnp.int32, (taps, RADIX), 0)
    turn_lane = lax.broadcasted_iota(jnp.int32, (taps, RADIX), 1)
    turned_to = jnp.where((turn_row + turn_lane) % RADIX == 0, 1.0, 0.0).astype(jnp.float32)
    for part in range(2):
        reverse[part] = lax.dot_general(
            bank[part],
            turned_to,
            (((0,), (0,)), ((), ())),
            precision=lax.Precision.HIGHEST,
            preferred_element_type=jnp.float32,
        )

    lane = lax.broadcasted_iota(jnp.int32, (SUBS, LANES), 1)
    sub = lax.broadcasted_iota(jnp.int32, (SUBS, LANES), 0)

    def merge(src, section, r, dst, at, count):
        half = 1 << section
        base = r - r % (2 * half) + r % half - r % min(half, CH_DEV)
        a = base + picks_ref[0, section, r]
        b = base + half + picks_ref[1, section, r]
        d = delay_ref[section, r]
        turn = (LANES - d) & (LANES - 1)
        keep = lane < LANES - d
        turned = [
            pltpu.roll(src[b, :, i * LANES : (i + 1) * LANES], turn, 1) for i in range(tiles + 1)
        ]
        for i in range(count):
            later = turned[min(i + 1, tiles)]
            dst[at, :, i * LANES : (i + 1) * LANES] = src[
                a, :, i * LANES : (i + 1) * LANES
            ] + jnp.where(keep, turned[i], later)

    def tree_part(c):
        @pl.loop(0, nb * blocks)
        def _(q):
            for ch in range(SUBS):
                r = q * SUBS + ch
                rows_of = pl.ds(ch, SUBS, stride=SUBS)
                for i in range(tiles + 1 - c):
                    buf_a[r, :, i * LANES : (i + 1) * LANES] = raw[q, c * tiles + i, rows_of, :]
                if c == 1:
                    edges = pltpu.roll(rim[q // pack], (LANES - (q % pack) * share) % LANES, 1)
                    up = pltpu.roll(raw[q, 0, rows_of, :], SUBS - 1, 0)
                    edge = jnp.broadcast_to(edges[ch : ch + 1], (SUBS, LANES))
                    buf_a[r, :, span:] = jnp.where(sub == SUBS - 1, edge, up)

        src, dst = buf_a, buf_b
        for section in range(sections - 1):

            @pl.loop(0, rows, unroll=16)
            def _(r, src=src, dst=dst, section=section):
                merge(src, section, r, dst, r, tiles + 1)

            src, dst = dst, src

        @pl.loop(0, everyone)
        def _(e):
            start = (e % nb) * CH_DEV + (e // nb) * trials

            @pl.loop(0, trials, unroll=trials)
            def _(i):
                merge(src, sections - 1, start + i, stage.at[e], i, tiles)

        copy = pltpu.make_async_copy(stage, sent[c], stage_sem)
        copy.start()
        copy.wait()

    def part_of(c, t):
        return (pl.ds(t, 1), 1 + t) if c else (slice(None), 0)

    def second(c, t, e):
        which, at = part_of(c, t)
        return pltpu.make_async_remote_copy(
            sent[c].at[e, which],
            got[c].at[me, which],
            two_send.at[c],
            two_recv.at[at],
            device_id=device(e),
            device_id_type=MESH,
        )

    def send_second(c, t):
        @pl.loop(0, (nb - 1) * nt)
        def _(i):
            b = (mb + 1 + (i // nt + nb // 2 - 1) % (nb - 1)) % nb
            second(c, t, ((mt + i) % nt) * nb + b).start()

        @pl.loop(1, nt)
        def _(i):
            second(c, t, ((mt + i) % nt) * nb + mb).start()

        which, at = part_of(c, t)
        pltpu.make_async_copy(
            sent[c].at[me, which], got[c].at[me, which], two_recv.at[at]
        ).start()

    def wait_second(c, t):
        which, at = part_of(c, t)
        landed(got[c].at[:, which], two_recv.at[at])

    for i in early:
        first_wait(i)

    @pl.loop(0, nb * blocks // pack)
    def _(q):
        packed = raw[q * pack, 0, :SUBS, :]
        for p in range(1, pack):
            moved = pltpu.roll(raw[q * pack + p, 0, :SUBS, :], p * share, 1)
            packed = jnp.where(lane < p * share, packed, moved)
        rim_sent[q] = packed

    rim_copy = pltpu.make_async_remote_copy(
        rim_sent,
        rim,
        rim_sems.at[0],
        rim_sems.at[1],
        device_id=device((me + everyone - 1) % everyone),
        device_id_type=MESH,
    )

    @pl.when(me > 0)
    def _():
        rim_copy.start()

    @pl.when(me == everyone - 1)
    def _():
        rim[...] = jnp.zeros_like(rim)

    tree_part(0)
    send_second(0, 0)
    for i in late:
        first_wait(i)

    @pl.when(me < everyone - 1)
    def _():
        rim_copy.wait_recv()

    tree_part(1)
    for t in range(min(AHEAD, trials)):
        send_second(1, t)
    landed(raw.at[pl.ds(0, (nb - 1) * blocks)], one_send)

    @pl.when(me > 0)
    def _():
        rim_copy.wait_send()

    for load in loads[4:]:
        load.wait()
    wait_second(0, 0)

    def bands_of(t):
        def row(z, part):
            return reverse[part, pl.ds(wanted_ref[z, t], 1), :]

        fill_bands(row, zsel, band_high, band_low)

    last = trials - 1

    @pl.loop(0, last)
    def _(t):
        bands_of(t)
        wait_second(1, t)

        @pl.when(t + AHEAD < trials)
        def _():
            send_second(1, t + AHEAD)

        def store(where, value):
            power[t, where, :] = value

        x = assemble([got[c][:, t] for c in range(2)], consts)
        powers_of(x, band_high[...], band_low[...], consts, zsel, taps // 2, store)

    bands_of(last)
    wait_second(1, last)
    for c in range(2):
        landed(sent[c].at[pl.ds(0, everyone - 1)], two_send.at[c])


def assemble(parts, consts):
    cols = consts[2].shape[0]
    parts = [part.reshape(-1, part.shape[-1]) for part in parts]
    return jnp.concatenate(
        [part[:, i : i + cols] for part in parts for i in range(0, part.shape[1], cols)], axis=0
    )


def last_kernel(zsel, half_taps, *refs):
    done_ref, got, (band_high, band_low) = refs[0], refs[1:3], refs[3:5]
    consts, out_ref, power, move_sem, sem = refs[5:11], *refs[11:]
    count = done_ref.shape[0]
    move = pltpu.make_async_copy(done_ref, out_ref.at[pl.ds(0, count)], move_sem)
    move.start()
    x = assemble([ref[:, count] for ref in got], consts)

    def store(where, value):
        power[where, :] = value

    powers_of(x, band_high[...], band_low[...], consts, zsel, half_taps, store)
    final = pltpu.make_async_copy(power, out_ref.at[count], sem)
    final.start()
    move.wait()
    final.wait()


def fused(signal, picks, delays, template_bank, wanted, consts, zsel, taps, nb, nt):
    sections = picks.shape[1]
    channels = CH_DEV * nb
    everyone = nb * nt
    trials = CH_DEV // nt
    slab = signal.shape[1] // nb
    width = slab // SUBS
    span = width // 2
    blocks = CH_DEV // SUBS
    cols = consts[2].shape[0]
    outs = cols // 2
    rows = 2 * outs * zsel
    wide = 2 * zsel * LANES
    view = signal.reshape(blocks, SUBS, nb * SUBS, width).transpose(0, 2, 1, 3)
    view = view.reshape(blocks, nb, SUBS * SUBS, width)
    bank = template_bank.transpose(0, 2, 1)
    anywhere = pl.BlockSpec(memory_space=pl.ANY)
    dma = pltpu.SemaphoreType.DMA
    f32, bf16 = jnp.float32, jnp.bfloat16
    macs = cols * RADIX * 2 * RADIX + outs * 2 * cols * 2 * RADIX + 2 * outs * 4 * RADIX * RADIX
    exchanged = (everyone, trials, SUBS, span)
    kept = [
        pltpu.VMEM((trials - 1, rows, LANES), f32),
        *[pltpu.VMEM(exchanged, f32)] * 2,
        *[pltpu.VMEM((2 * RADIX, wide), bf16)] * 2,
        *[pltpu.VMEM(c.shape, c.dtype) for c in consts],
    ]
    vmem = pl.BlockSpec(memory_space=pltpu.VMEM)
    *handed, _, _ = pl.pallas_call(
        functools.partial(fused_kernel, nb, nt, sections, trials, zsel, taps),
        out_shape=kept + [jax.ShapeDtypeStruct(exchanged, f32)] * 2,
        in_specs=[anywhere] * 11,
        out_specs=[vmem] * len(kept) + [anywhere] * 2,
        scratch_shapes=[
            pltpu.VMEM((nb * blocks, width // LANES, SUBS * SUBS, LANES), f32),
            *[pltpu.VMEM((nb * blocks // rim_pack(sections), SUBS, LANES), f32)] * 2,
            pltpu.VMEM((channels, SUBS, span + LANES), f32),
            pltpu.VMEM((channels, SUBS, span + LANES), f32),
            pltpu.VMEM(exchanged, f32),
            pltpu.VMEM(bank.shape, f32),
            pltpu.VMEM(template_bank.shape[:2] + (RADIX,), f32),
            *[pltpu.SMEM(a.shape, jnp.int32) for a in (picks, delays, wanted.T)],
            dma,
            dma((width // LANES,)),
            dma((2,)),
            dma((1 + trials,)),
            dma((2,)),
            dma,
            dma((4 + len(consts),)),
        ],
        compiler_params=pltpu.CompilerParams(
            collective_id=0, has_side_effects=True, vmem_limit_bytes=FUSED_LIMIT
        ),
        cost_estimate=pl.CostEstimate(
            flops=6 * trials * macs, bytes_accessed=3 * signal.size * 4, transcendentals=0
        ),
        name="fused",
    )(picks, delays, wanted.T, bank, view, *consts)
    return pl.pallas_call(
        functools.partial(last_kernel, zsel, taps // 2),
        out_shape=jax.ShapeDtypeStruct((trials, rows, LANES), f32),
        in_specs=[vmem] * len(kept),
        out_specs=anywhere,
        scratch_shapes=[pltpu.VMEM((rows, LANES), f32), dma, dma],
        compiler_params=pltpu.CompilerParams(vmem_limit_bytes=LAST_LIMIT),
        cost_estimate=pl.CostEstimate(
            flops=6 * macs, bytes_accessed=signal.size * 4, transcendentals=0
        ),
        name="last",
    )(*handed)


def on_device(signal, tree_picks, tree_delays, template_bank, template_pick):
    band_count = lax.axis_size("band")
    time_count = lax.axis_size("tm")
    everyone = band_count * time_count
    sections = LOGCD + band_count.bit_length() - 1
    rim_depth = sections * MAXD
    channels = CH_DEV * band_count
    samples = signal.shape[1] * time_count
    slab = signal.shape[1] // band_count
    width = slab // SUBS
    trials = CH_DEV // time_count
    last = max(1, 3 * trials // 16)
    counts = [count for count in (trials - last, last) if count]
    zsel = template_pick.shape[2]
    taps = template_bank.shape[2]
    cols = samples // RADIX
    if width % (2 * cols) == 0 and trials % 2 == 0 and trials >= 4:
        consts = [jnp.asarray(c) for c in tables(samples, channels, width, taps)]
        out = fused(
            signal, tree_picks, tree_delays, template_bank, template_pick[0], consts, zsel, taps,
            band_count, time_count,
        )
        return finish(out, trials, samples, zsel)

    band_high, band_low = bands(template_pick[0], template_bank)

    half = (1 << np.arange(sections))[:, None]
    r = np.arange(channels)[None, :]
    base = r - r % (2 * half) + r % half - r % np.minimum(half, CH_DEV)
    low = tree_picks[0] + base.astype(np.int32)
    high = tree_picks[1] + (base + half).astype(np.int32)
    grid = np.arange(channels).reshape(band_count, time_count, trials).transpose(1, 0, 2)
    firsts = [sum(counts[:q]) for q in range(len(counts))]
    order = np.concatenate(
        [grid[:, :, first : first + count].reshape(-1) for first, count in zip(firsts, counts)]
    ).astype(np.int32)
    tables_of = (low, high, tree_delays, jnp.asarray(order))
    sizes = [everyone * count for count in counts]

    folded = signal.reshape(CH_DEV, band_count, SUBS, width)

    def exchanged(value):
        value = lax.all_to_all(value, "band", split_axis=0, concat_axis=0, tiled=True)
        return value.reshape(channels, SUBS, -1)

    def rim_of(x):
        rim = shifted(x[:, 0, :rim_depth], ("tm", "band"), -1)
        rim = jnp.pad(rim, ((0, 0), (0, LANES - rim_depth)))
        return jnp.broadcast_to(rim[:, None, :], (channels, SUBS, LANES))

    if width % (2 * LANES) == 0:
        span = width // 2
        cut = span + LANES
        x_a = exchanged(folded[..., :cut].transpose(1, 0, 2, 3))
        x_b = after(after(folded[..., cut:].transpose(1, 0, 2, 3), x_a), band_low)
        x_b = exchanged(x_b)
        pieces = tree([x_a], [0], None, tables_of, sizes, width, span, 0, [])
        pieces = tree(
            [x_a, x_b], [span, 0], rim_of(x_a), tables_of, sizes, width, span, 1, pieces
        )
    else:
        x = exchanged(folded.transpose(1, 0, 2, 3))
        pieces = tree([x], [0], rim_of(x), tables_of, sizes, width, width, 0, [])

    consts = [jnp.asarray(c) for c in tables(samples, channels, width, taps)]
    out = None
    for first, count, piece in zip(firsts, counts, pieces):
        piece = piece.reshape(everyone, count, SUBS, width)
        if out is not None:
            piece = after(piece, arrived)
        arrived = lax.all_to_all(piece, ("tm", "band"), split_axis=0, concat_axis=0, tiled=True)
        out, _ = spectra(
            arrived, band_high, band_low, consts, zsel, taps, trials, first, out
        )
    return finish(out, trials, samples, zsel)


def solution(mesh):
    in_specs = (P(("beams", "band"), "tm"), P(), P(), P(), P(("beams", "band"), "tm", None))
    out_specs = P(("beams", "band"), "tm", None, None)
    return jax.shard_map(
        on_device, mesh=mesh, in_specs=in_specs, out_specs=out_specs, check_vma=False
    )
```

```python
import functools
import math

import jax
import jax.numpy as jnp
import ml_dtypes
import numpy as np
from jax import lax
from jax.experimental import pallas as pl
from jax.experimental.pallas import tpu as pltpu
from jax.sharding import PartitionSpec as P

CH_DEV = 64
LOGCD = 6
MAXD = 4
LANES = 128
SUBS = 8
RADIX = 256
LIMIT = 56 * 1024 * 1024
FUSED_LIMIT = 41 * 1024 * 1024
LAST_LIMIT = 14 * 1024 * 1024
AHEAD = 6
MESH = pl.DeviceIdType.MESH


def shifted(value, axis, steps):
    count = lax.axis_size(axis)
    first, last = (max(0, -steps), min(count, count - steps))
    return lax.ppermute(value, axis, [(source, source + steps) for source in range(first, last)])


def tree_kernel(sections, sizes, parts, has_rim, *refs):
    low_ref, high_ref, delay_ref, row_ref = refs[:4]
    xs, refs = refs[4 : 4 + len(parts)], refs[4 + len(parts) :]
    if has_rim:
        rim_ref, refs = refs[0], refs[1:]
    buf_a, buf_b = refs[-2:]
    outs = refs[len(refs) - 2 - len(sizes) : -2]
    rows, _, span = buf_a.shape
    tiles = span // LANES - 1
    lane = lax.broadcasted_iota(jnp.int32, (SUBS, LANES), 1)
    sub = lax.broadcasted_iota(jnp.int32, (SUBS, LANES), 0)

    @pl.loop(0, rows, unroll=4)
    def _(r):
        at = 0
        for x_ref, first in zip(xs, parts):
            count = x_ref.shape[2] - first
            buf_a[r, :, at : at + count] = x_ref[r, :, first:]
            at += count
        if has_rim:
            up = pltpu.roll(xs[0][r, :, 0:LANES], SUBS - 1, 0)
            buf_a[r, :, at : at + LANES] = jnp.where(sub == SUBS - 1, rim_ref[r], up)

    def merge(src, section, r, dst, at, count):
        a = low_ref[section, r]
        b = high_ref[section, r]
        d = delay_ref[section, r]
        turn = (LANES - d) & (LANES - 1)
        keep = lane < LANES - d
        turned = [
            pltpu.roll(src[b, :, i * LANES : (i + 1) * LANES], turn, 1) for i in range(tiles + 1)
        ]
        for i in range(count):
            later = turned[min(i + 1, tiles)]
            dst[at, :, i * LANES : (i + 1) * LANES] = src[
                a, :, i * LANES : (i + 1) * LANES
            ] + jnp.where(keep, turned[i], later)

    src, dst = buf_a, buf_b
    for section in range(sections - 1):

        @pl.loop(0, rows, unroll=16)
        def _(r, src=src, dst=dst, section=section):
            merge(src, section, r, dst, r, tiles + 1)

        src, dst = dst, src
    start = 0
    for size, out in zip(sizes, outs):

        @pl.loop(0, size, unroll=16)
        def _(i, start=start, src=src, out=out):
            merge(src, sections - 1, row_ref[start + i], out, i, tiles)

        start += size


def tree(xs, parts, rim, tables_of, sizes, width, span, place, so_far):
    rows = xs[0].shape[0]
    sections = tables_of[0].shape[0]
    smem = pl.BlockSpec(memory_space=pltpu.SMEM)
    vmem = pl.BlockSpec(memory_space=pltpu.VMEM)
    has_rim = rim is not None
    inputs = [*tables_of, *xs] + ([rim] if has_rim else [])
    known = len(inputs)
    return pl.pallas_call(
        functools.partial(tree_kernel, sections, sizes, parts, has_rim),
        grid=(1,),
        out_shape=[jax.ShapeDtypeStruct((size, SUBS, width), jnp.float32) for size in sizes],
        in_specs=[smem] * 4
        + [vmem] * (known - 4)
        + [pl.BlockSpec(memory_space=pl.ANY)] * len(so_far),
        out_specs=[pl.BlockSpec((size, SUBS, span), lambda i: (0, 0, place)) for size in sizes],
        input_output_aliases={known + i: i for i in range(len(so_far))},
        scratch_shapes=[pltpu.VMEM((rows, SUBS, span + LANES), jnp.float32)] * 2,
        compiler_params=pltpu.CompilerParams(vmem_limit_bytes=LIMIT),
        cost_estimate=pl.CostEstimate(
            flops=rows * SUBS * span * sections * 4,
            bytes_accessed=rows * SUBS * span * 8,
            transcendentals=0,
        ),
        name="tree",
    )(*inputs, *so_far)


def split(value):
    high = value.astype(jnp.bfloat16)
    return high, (value - high.astype(jnp.float32)).astype(jnp.bfloat16)


def fill_bands(row_of, zsel, high_ref, low_ref):
    for z in range(zsel):
        pair = []
        for part in range(2):
            wide = jnp.broadcast_to(row_of(z, part), (RADIX, RADIX))
            band = pltpu.roll(wide, 0, 1, stride=1, stride_axis=0)[:, :LANES]
            pair.append(split(band))
        at = 2 * z * LANES
        for ref, real, imag in (
            (high_ref, pair[0][0], pair[1][0]),
            (low_ref, pair[0][1], pair[1][1]),
        ):
            ref[:RADIX, at : at + LANES] = real
            ref[RADIX:, at : at + LANES] = -imag
            ref[:RADIX, at + LANES : at + 2 * LANES] = imag
            ref[RADIX:, at + LANES : at + 2 * LANES] = real


def bands_kernel(zsel, u_ref, high_ref, low_ref):
    def row_of(z, part):
        return u_ref[0, 2 * z + part : 2 * z + part + 1, :]

    fill_bands(row_of, zsel, high_ref.at[0], low_ref.at[0])


def reversed_taps(picks, template_bank):
    trials, zsel = picks.shape
    taps = template_bank.shape[2]
    onehot = (picks[:, :, None] == jnp.arange(template_bank.shape[1], dtype=jnp.int32)).astype(
        jnp.float32
    )
    reversed_bank = jnp.concatenate(
        [
            template_bank[:, :, :1],
            jnp.zeros(template_bank.shape[:2] + (RADIX - taps,), jnp.float32),
            template_bank[:, :, :0:-1],
        ],
        axis=2,
    )
    u = jnp.einsum("tzk,ckm->tzcm", onehot, reversed_bank, precision=lax.Precision.HIGHEST)
    return u.reshape(trials, 2 * zsel, RADIX)


def bands(picks, template_bank):
    trials, zsel = picks.shape
    u = reversed_taps(picks, template_bank)
    wide = 2 * zsel * LANES
    shape = jax.ShapeDtypeStruct((trials, 2 * RADIX, wide), jnp.bfloat16)
    spec = pl.BlockSpec((1, 2 * RADIX, wide), lambda t: (t, 0, 0))
    return pl.pallas_call(
        functools.partial(bands_kernel, zsel),
        grid=(trials,),
        out_shape=[shape, shape],
        in_specs=[pl.BlockSpec((1, 2 * zsel, RADIX), lambda t: (t, 0, 0))],
        out_specs=[spec, spec],
        compiler_params=pltpu.CompilerParams(vmem_limit_bytes=LIMIT),
        cost_estimate=pl.CostEstimate(
            flops=trials * RADIX * RADIX * 20,
            bytes_accessed=trials * 2 * RADIX * wide * 4,
            transcendentals=0,
        ),
        name="bands",
    )(u)


def tables(samples, channels, width, taps):
    cols = samples // RADIX
    outs = cols // 2
    split_by = width // cols if width % cols == 0 else 1
    place = np.arange(RADIX)
    row_of = split_by * (place % (RADIX // split_by)) + place // (RADIX // split_by)
    freq = (np.arange(RADIX) - taps // 2) % RADIX
    b = np.arange(cols)
    scale = 1.0 / math.sqrt(samples * channels)
    angle = 2.0 * np.pi / RADIX * (row_of[:, None] * freq[None, :] % RADIX)
    first = np.concatenate([np.cos(angle), -np.sin(angle)], axis=1) * scale
    angle = 2.0 * np.pi / samples * (b[:, None] * freq[None, :] % samples)
    tw_cos, tw_sin = np.cos(angle), np.sin(angle)
    angle = 2.0 * np.pi / cols * (np.arange(outs)[:, None] * b[None, :] % cols)
    second = np.concatenate([np.cos(angle), np.sin(angle)], axis=1)

    def parts(value):
        value = value.astype(np.float32)
        high = value.astype(ml_dtypes.bfloat16)
        return high, (value - high.astype(np.float32)).astype(ml_dtypes.bfloat16)

    return (
        *parts(first),
        tw_cos.astype(np.float32),
        tw_sin.astype(np.float32),
        *parts(second),
    )


def dot3(a_high, a_low, b_high, b_low):
    def dot(a, b):
        return jnp.dot(a, b, preferred_element_type=jnp.float32)

    return dot(a_high, b_high) + (dot(a_high, b_low) + dot(a_low, b_high))


def powers_of(x, band_high, band_low, consts, zsel, half_taps, store):
    fh, fl, tc, ts, sh, sl = consts
    cols = tc.shape[0]
    outs = cols // 2
    x_high, x_low = split(x.T)
    first = dot3(x_high, x_low, fh[...], fl[...])
    re, im = first[:, :RADIX], first[:, RADIX:]
    mid_re = re * tc[...] + im * ts[...]
    mid_im = im * tc[...] - re * ts[...]
    re_high, re_low = split(mid_re)
    im_high, im_low = split(mid_im)

    def block(a, b):
        return jnp.concatenate(
            [jnp.concatenate([a, b], axis=1), jnp.concatenate([b, -a], axis=1)], axis=0
        )

    spec = dot3(sh[...], sl[...], block(re_high, im_high), block(re_low, im_low))
    row = lax.broadcasted_iota(jnp.int32, (outs, RADIX), 0)
    lane = lax.broadcasted_iota(jnp.int32, (outs, RADIX), 1)
    even, odd = [], []
    for part in (spec[:, :RADIX], spec[:, RADIX:]):
        down = jnp.where(row == 0, 0.0, pltpu.roll(part, 1, 0))
        up = jnp.where(row == outs - 1, 0.0, pltpu.roll(part, outs - 1, 0))
        here = jnp.where(lane < half_taps, down, part)
        after = jnp.where(lane < half_taps, part, up)
        even.append(here)
        odd += [here[:, LANES:], after[:, :LANES]]
    window = jnp.concatenate(
        [jnp.concatenate(even, axis=1), jnp.concatenate(odd, axis=1)], axis=0
    )
    w_high, w_low = split(window)
    got = dot3(w_high, w_low, band_high, band_low)
    for z in range(zsel):
        at = 2 * z * LANES
        real, imag = got[:, at : at + LANES], got[:, at + LANES : at + 2 * LANES]
        power = real * real + imag * imag
        for e in range(2):
            store(pl.ds(e * zsel + z, outs, 2 * zsel), power[e * outs : (e + 1) * outs])


def spectra_kernel(zsel, half_taps, aliased, *refs):
    x_ref, bh_ref, bl_ref = refs[:3]
    consts = refs[3:9]
    out_ref, done_ref = refs[10:] if aliased else refs[9:]
    done_ref[...] = jnp.zeros_like(done_ref)
    cols = consts[2].shape[0]
    x = x_ref[...]
    x = x.reshape(-1, x.shape[-1])
    if x.shape[1] != cols:
        x = jnp.concatenate(
            [x[:, i * cols : (i + 1) * cols] for i in range(x.shape[1] // cols)], axis=0
        )

    def store(rows, value):
        out_ref[0, rows, :] = value

    powers_of(x, bh_ref[0], bl_ref[0], consts, zsel, half_taps, store)


def spectra(x, band_high, band_low, consts, zsel, taps, trials, first_trial, so_far):
    cols = consts[2].shape[0]
    outs = cols // 2
    rows = 2 * outs * zsel
    if x.shape[-1] % cols == 0:
        here = x.shape[1]
        x_spec = pl.BlockSpec((x.shape[0], 1, SUBS, x.shape[-1]), lambda t: (0, t, 0, 0))
    else:
        here = x.shape[1]
        x = x.transpose(1, 0, 2, 3).reshape(here, RADIX, cols)
        x_spec = pl.BlockSpec((1, RADIX, cols), lambda t: (t, 0, 0))
    band_spec = pl.BlockSpec(
        (1,) + band_high.shape[1:], lambda t: (first_trial + t, 0, 0)
    )
    whole = [pl.BlockSpec(c.shape, lambda t: (0, 0)) for c in consts]
    aliased = so_far is not None
    more = [so_far] if aliased else []
    macs = here * (cols * RADIX * 2 * RADIX + outs * 2 * cols * 2 * RADIX + 2 * outs * 4 * RADIX * RADIX)
    return pl.pallas_call(
        functools.partial(spectra_kernel, zsel, taps // 2, aliased),
        grid=(here,),
        out_shape=[
            jax.ShapeDtypeStruct((trials, rows, LANES), jnp.float32),
            jax.ShapeDtypeStruct((SUBS, LANES), jnp.float32),
        ],
        in_specs=[x_spec, band_spec, band_spec, *whole]
        + [pl.BlockSpec(memory_space=pl.ANY)] * len(more),
        out_specs=[
            pl.BlockSpec((1, rows, LANES), lambda t: (first_trial + t, 0, 0)),
            pl.BlockSpec((SUBS, LANES), lambda t: (0, 0)),
        ],
        input_output_aliases={9: 0} if aliased else {},
        compiler_params=pltpu.CompilerParams(vmem_limit_bytes=LIMIT),
        cost_estimate=pl.CostEstimate(
            flops=6 * macs, bytes_accessed=here * 2 * 1024 * 1024, transcendentals=0
        ),
        name="spectra",
    )(x, band_high, band_low, *consts, *more)


def after_kernel(value_ref, done_ref, out_ref):
    del value_ref, done_ref, out_ref


def after(value, done):
    anywhere = pl.BlockSpec(memory_space=pl.ANY)
    return pl.pallas_call(
        after_kernel,
        out_shape=jax.ShapeDtypeStruct(value.shape, value.dtype),
        in_specs=[anywhere, anywhere],
        out_specs=anywhere,
        input_output_aliases={0: 0},
        name="after",
    )(value, done)


def finish(out, trials, samples, zsel):
    out = out.reshape(trials, samples // 2 // LANES, zsel, LANES).transpose(0, 2, 1, 3)
    return out.reshape(1, trials, zsel, samples // 2)


def rim_pack(sections):
    return LANES >> (sections * MAXD - 1).bit_length()


def fused_kernel(
    nb, nt, sections, trials, zsel, taps,
    picks_hbm, delay_hbm, wanted_hbm, bank_ref, sig_ref, *refs
):
    const_refs, refs = refs[:6], refs[6:]
    power, got, band_high, band_low, refs = refs[0], refs[1:3], refs[3], refs[4], refs[5:]
    consts, refs = refs[:6], refs[6:]
    raw, rim, rim_sent, buf_a, buf_b, refs = *refs[:5], refs[5:]
    sent, refs = refs[:2], refs[2:]
    bank, reverse, refs = *refs[:2], refs[2:]
    picks_ref, delay_ref, wanted_ref, refs = *refs[:3], refs[3:]
    (
        one_send, one_recv, two_send, two_recv, rim_sems, load_sems,
    ) = refs

    everyone = nb * nt
    rows, _, span = buf_a.shape
    span = span - LANES
    blocks = CH_DEV // SUBS
    tiles = span // LANES
    early = range(tiles + 1)
    late = range(tiles + 1, 2 * tiles)
    pack = rim_pack(sections)
    share = LANES // pack
    mt, mb = lax.axis_index("tm"), lax.axis_index("band")
    me = mt * nb + mb

    def device(e):
        return {"tm": e // nb, "band": e % nb}

    barrier = pltpu.get_barrier_semaphore()

    @pl.loop(1, everyone)
    def _(d):
        pl.semaphore_signal(
            barrier, 1, device_id=device((me + d) % everyone), device_id_type=MESH
        )

    def slab(i, k):
        return sig_ref.at[:, k, :, pl.ds(i * LANES, LANES)]

    def landed(ref, sem):
        pltpu.make_async_copy(ref, ref, sem).wait()

    def first(i, d):
        return pltpu.make_async_remote_copy(
            slab(i, (mb + d) % nb),
            raw.at[pl.ds(mb * blocks, blocks), i],
            one_send,
            one_recv.at[i],
            device_id={"band": (mb + d) % nb},
            device_id_type=MESH,
        )

    def first_own(i):
        return pltpu.make_async_copy(
            slab(i, mb), raw.at[pl.ds(mb * blocks, blocks), i], one_recv.at[i]
        )

    def first_wait(i):
        landed(raw.at[:, i], one_recv.at[i])

    loads = [
        pltpu.make_async_copy(a, b, load_sems.at[i])
        for i, (a, b) in enumerate(zip(
            (bank_ref, picks_hbm, delay_hbm, wanted_hbm, *const_refs),
            (bank, picks_ref, delay_ref, wanted_ref, *consts),
        ))
    ]
    for load in loads:
        load.start()

    for i in (*early, *late):
        first_own(i).start()
    pl.semaphore_wait(barrier, everyone - 1)

    apart = sorted(range(1, nb), key=lambda d: -min(d, nb - d))
    for i in (*early, *late):
        for d in apart:
            first(i, d).start()
    for load in loads[:4]:
        load.wait()
    turn_row = lax.broadcasted_iota(jnp.int32, (taps, RADIX), 0)
    turn_lane = lax.broadcasted_iota(jnp.int32, (taps, RADIX), 1)
    turned_to = jnp.where((turn_row + turn_lane) % RADIX == 0, 1.0, 0.0).astype(jnp.float32)
    for part in range(2):
        reverse[part] = lax.dot_general(
            bank[part],
            turned_to,
            (((0,), (0,)), ((), ())),
            precision=lax.Precision.HIGHEST,
            preferred_element_type=jnp.float32,
        )

    lane = lax.broadcasted_iota(jnp.int32, (SUBS, LANES), 1)
    sub = lax.broadcasted_iota(jnp.int32, (SUBS, LANES), 0)

    def merge(src, section, r, dst, at, count):
        half = 1 << section
        base = r - r % (2 * half) + r % half - r % min(half, CH_DEV)
        a = base + picks_ref[0, section, r]
        b = base + half + picks_ref[1, section, r]
        d = delay_ref[section, r]
        turn = (LANES - d) & (LANES - 1)
        keep = lane < LANES - d
        turned = [
            pltpu.roll(src[b, :, i * LANES : (i + 1) * LANES], turn, 1) for i in range(tiles + 1)
        ]
        for i in range(count):
            later = turned[min(i + 1, tiles)]
            dst[at, :, i * LANES : (i + 1) * LANES] = src[
                a, :, i * LANES : (i + 1) * LANES
            ] + jnp.where(keep, turned[i], later)

    def tree_part(c):
        @pl.loop(0, nb * blocks)
        def _(q):
            for ch in range(SUBS):
                r = q * SUBS + ch
                rows_of = pl.ds(ch, SUBS, stride=SUBS)
                for i in range(tiles + 1 - c):
                    buf_a[r, :, i * LANES : (i + 1) * LANES] = raw[q, c * tiles + i, rows_of, :]
                if c == 1:
                    edges = pltpu.roll(rim[q // pack], (LANES - (q % pack) * share) % LANES, 1)
                    up = pltpu.roll(raw[q, 0, rows_of, :], SUBS - 1, 0)
                    edge = jnp.broadcast_to(edges[ch : ch + 1], (SUBS, LANES))
                    buf_a[r, :, span:] = jnp.where(sub == SUBS - 1, edge, up)

        src, dst = buf_a, buf_b
        for section in range(sections - 1):

            @pl.loop(0, rows, unroll=16)
            def _(r, src=src, dst=dst, section=section):
                merge(src, section, r, dst, r, tiles + 1)

            src, dst = dst, src

        @pl.loop(0, everyone)
        def _(e):
            start = (e % nb) * CH_DEV + (e // nb) * trials

            @pl.loop(0, trials, unroll=trials)
            def _(i):
                merge(src, sections - 1, start + i, sent[c].at[e], i, tiles)

    def part_of(c, t):
        return (pl.ds(t, 1), 1 + t) if c else (slice(None), 0)

    def second(c, t, e):
        which, at = part_of(c, t)
        return pltpu.make_async_remote_copy(
            sent[c].at[e, which],
            got[c].at[me, which],
            two_send.at[c],
            two_recv.at[at],
            device_id=device(e),
            device_id_type=MESH,
        )

    def send_second(c, t):
        @pl.loop(0, (nb - 1) * nt)
        def _(i):
            b = (mb + 1 + (i // nt + nb // 2 - 1) % (nb - 1)) % nb
            second(c, t, ((mt + i) % nt) * nb + b).start()

        @pl.loop(1, nt)
        def _(i):
            second(c, t, ((mt + i) % nt) * nb + mb).start()

        which, at = part_of(c, t)
        pltpu.make_async_copy(
            sent[c].at[me, which], got[c].at[me, which], two_recv.at[at]
        ).start()

    def wait_second(c, t):
        which, at = part_of(c, t)
        landed(got[c].at[:, which], two_recv.at[at])

    for i in early:
        first_wait(i)

    @pl.loop(0, nb * blocks // pack)
    def _(q):
        packed = raw[q * pack, 0, :SUBS, :]
        for p in range(1, pack):
            moved = pltpu.roll(raw[q * pack + p, 0, :SUBS, :], p * share, 1)
            packed = jnp.where(lane < p * share, packed, moved)
        rim_sent[q] = packed

    rim_copy = pltpu.make_async_remote_copy(
        rim_sent,
        rim,
        rim_sems.at[0],
        rim_sems.at[1],
        device_id=device((me + everyone - 1) % everyone),
        device_id_type=MESH,
    )

    @pl.when(me > 0)
    def _():
        rim_copy.start()

    @pl.when(me == everyone - 1)
    def _():
        rim[...] = jnp.zeros_like(rim)

    tree_part(0)
    send_second(0, 0)
    for i in late:
        first_wait(i)

    @pl.when(me < everyone - 1)
    def _():
        rim_copy.wait_recv()

    tree_part(1)
    for t in range(min(AHEAD, trials)):
        send_second(1, t)
    landed(raw.at[pl.ds(0, (nb - 1) * blocks)], one_send)

    @pl.when(me > 0)
    def _():
        rim_copy.wait_send()

    for load in loads[4:]:
        load.wait()
    wait_second(0, 0)

    def bands_of(t):
        def row(z, part):
            return reverse[part, pl.ds(wanted_ref[z, t], 1), :]

        fill_bands(row, zsel, band_high, band_low)

    last = trials - 1

    @pl.loop(0, last)
    def _(t):
        bands_of(t)
        wait_second(1, t)

        @pl.when(t + AHEAD < trials)
        def _():
            send_second(1, t + AHEAD)

        def store(where, value):
            power[t, where, :] = value

        x = assemble([got[c][:, t] for c in range(2)], consts)
        powers_of(x, band_high[...], band_low[...], consts, zsel, taps // 2, store)

    bands_of(last)
    wait_second(1, last)
    for c in range(2):
        landed(sent[c].at[pl.ds(0, everyone - 1)], two_send.at[c])


def assemble(parts, consts):
    cols = consts[2].shape[0]
    parts = [part.reshape(-1, part.shape[-1]) for part in parts]
    return jnp.concatenate(
        [part[:, i : i + cols] for part in parts for i in range(0, part.shape[1], cols)], axis=0
    )


def last_kernel(zsel, half_taps, *refs):
    done_ref, got, (band_high, band_low) = refs[0], refs[1:3], refs[3:5]
    consts, out_ref, power, move_sem, sem = refs[5:11], *refs[11:]
    count = done_ref.shape[0]
    move = pltpu.make_async_copy(done_ref, out_ref.at[pl.ds(0, count)], move_sem)
    move.start()
    x = assemble([ref[:, count] for ref in got], consts)

    def store(where, value):
        power[where, :] = value

    powers_of(x, band_high[...], band_low[...], consts, zsel, half_taps, store)
    final = pltpu.make_async_copy(power, out_ref.at[count], sem)
    final.start()
    move.wait()
    final.wait()


def fused(signal, picks, delays, template_bank, wanted, consts, zsel, taps, nb, nt):
    sections = picks.shape[1]
    channels = CH_DEV * nb
    everyone = nb * nt
    trials = CH_DEV // nt
    slab = signal.shape[1] // nb
    width = slab // SUBS
    span = width // 2
    blocks = CH_DEV // SUBS
    cols = consts[2].shape[0]
    outs = cols // 2
    rows = 2 * outs * zsel
    wide = 2 * zsel * LANES
    view = signal.reshape(blocks, SUBS, nb * SUBS, width).transpose(0, 2, 1, 3)
    view = view.reshape(blocks, nb, SUBS * SUBS, width)
    bank = template_bank.transpose(0, 2, 1)
    anywhere = pl.BlockSpec(memory_space=pl.ANY)
    dma = pltpu.SemaphoreType.DMA
    f32, bf16 = jnp.float32, jnp.bfloat16
    macs = cols * RADIX * 2 * RADIX + outs * 2 * cols * 2 * RADIX + 2 * outs * 4 * RADIX * RADIX
    exchanged = (everyone, trials, SUBS, span)
    kept = [
        pltpu.VMEM((trials - 1, rows, LANES), f32),
        *[pltpu.VMEM(exchanged, f32)] * 2,
        *[pltpu.VMEM((2 * RADIX, wide), bf16)] * 2,
        *[pltpu.VMEM(c.shape, c.dtype) for c in consts],
    ]
    vmem = pl.BlockSpec(memory_space=pltpu.VMEM)
    handed = pl.pallas_call(
        functools.partial(fused_kernel, nb, nt, sections, trials, zsel, taps),
        out_shape=kept,
        in_specs=[anywhere] * 11,
        out_specs=[vmem] * len(kept),
        scratch_shapes=[
            pltpu.VMEM((nb * blocks, width // LANES, SUBS * SUBS, LANES), f32),
            *[pltpu.VMEM((nb * blocks // rim_pack(sections), SUBS, LANES), f32)] * 2,
            pltpu.VMEM((channels, SUBS, span + LANES), f32),
            pltpu.VMEM((channels, SUBS, span + LANES), f32),
            *[pltpu.VMEM(exchanged, f32)] * 2,
            pltpu.VMEM(bank.shape, f32),
            pltpu.VMEM(template_bank.shape[:2] + (RADIX,), f32),
            *[pltpu.SMEM(a.shape, jnp.int32) for a in (picks, delays, wanted.T)],
            dma,
            dma((width // LANES,)),
            dma((2,)),
            dma((1 + trials,)),
            dma((2,)),
            dma((4 + len(consts),)),
        ],
        compiler_params=pltpu.CompilerParams(
            collective_id=0, has_side_effects=True, vmem_limit_bytes=FUSED_LIMIT
        ),
        cost_estimate=pl.CostEstimate(
            flops=6 * trials * macs, bytes_accessed=3 * signal.size * 4, transcendentals=0
        ),
        name="fused",
    )(picks, delays, wanted.T, bank, view, *consts)
    return pl.pallas_call(
        functools.partial(last_kernel, zsel, taps // 2),
        out_shape=jax.ShapeDtypeStruct((trials, rows, LANES), f32),
        in_specs=[vmem] * len(kept),
        out_specs=anywhere,
        scratch_shapes=[pltpu.VMEM((rows, LANES), f32), dma, dma],
        compiler_params=pltpu.CompilerParams(vmem_limit_bytes=LAST_LIMIT),
        cost_estimate=pl.CostEstimate(
            flops=6 * macs, bytes_accessed=signal.size * 4, transcendentals=0
        ),
        name="last",
    )(*handed)


def on_device(signal, tree_picks, tree_delays, template_bank, template_pick):
    band_count = lax.axis_size("band")
    time_count = lax.axis_size("tm")
    everyone = band_count * time_count
    sections = LOGCD + band_count.bit_length() - 1
    rim_depth = sections * MAXD
    channels = CH_DEV * band_count
    samples = signal.shape[1] * time_count
    slab = signal.shape[1] // band_count
    width = slab // SUBS
    trials = CH_DEV // time_count
    last = max(1, 3 * trials // 16)
    counts = [count for count in (trials - last, last) if count]
    zsel = template_pick.shape[2]
    taps = template_bank.shape[2]
    cols = samples // RADIX
    if width % (2 * cols) == 0 and trials % 2 == 0 and trials >= 4:
        consts = [jnp.asarray(c) for c in tables(samples, channels, width, taps)]
        out = fused(
            signal, tree_picks, tree_delays, template_bank, template_pick[0], consts, zsel, taps,
            band_count, time_count,
        )
        return finish(out, trials, samples, zsel)

    band_high, band_low = bands(template_pick[0], template_bank)

    half = (1 << np.arange(sections))[:, None]
    r = np.arange(channels)[None, :]
    base = r - r % (2 * half) + r % half - r % np.minimum(half, CH_DEV)
    low = tree_picks[0] + base.astype(np.int32)
    high = tree_picks[1] + (base + half).astype(np.int32)
    grid = np.arange(channels).reshape(band_count, time_count, trials).transpose(1, 0, 2)
    firsts = [sum(counts[:q]) for q in range(len(counts))]
    order = np.concatenate(
        [grid[:, :, first : first + count].reshape(-1) for first, count in zip(firsts, counts)]
    ).astype(np.int32)
    tables_of = (low, high, tree_delays, jnp.asarray(order))
    sizes = [everyone * count for count in counts]

    folded = signal.reshape(CH_DEV, band_count, SUBS, width)

    def exchanged(value):
        value = lax.all_to_all(value, "band", split_axis=0, concat_axis=0, tiled=True)
        return value.reshape(channels, SUBS, -1)

    def rim_of(x):
        rim = shifted(x[:, 0, :rim_depth], ("tm", "band"), -1)
        rim = jnp.pad(rim, ((0, 0), (0, LANES - rim_depth)))
        return jnp.broadcast_to(rim[:, None, :], (channels, SUBS, LANES))

    if width % (2 * LANES) == 0:
        span = width // 2
        cut = span + LANES
        x_a = exchanged(folded[..., :cut].transpose(1, 0, 2, 3))
        x_b = after(after(folded[..., cut:].transpose(1, 0, 2, 3), x_a), band_low)
        x_b = exchanged(x_b)
        pieces = tree([x_a], [0], None, tables_of, sizes, width, span, 0, [])
        pieces = tree(
            [x_a, x_b], [span, 0], rim_of(x_a), tables_of, sizes, width, span, 1, pieces
        )
    else:
        x = exchanged(folded.transpose(1, 0, 2, 3))
        pieces = tree([x], [0], rim_of(x), tables_of, sizes, width, width, 0, [])

    consts = [jnp.asarray(c) for c in tables(samples, channels, width, taps)]
    out = None
    for first, count, piece in zip(firsts, counts, pieces):
        piece = piece.reshape(everyone, count, SUBS, width)
        if out is not None:
            piece = after(piece, arrived)
        arrived = lax.all_to_all(piece, ("tm", "band"), split_axis=0, concat_axis=0, tiled=True)
        out, _ = spectra(
            arrived, band_high, band_low, consts, zsel, taps, trials, first, out
        )
    return finish(out, trials, samples, zsel)


def solution(mesh):
    in_specs = (P(("beams", "band"), "tm"), P(), P(), P(), P(("beams", "band"), "tm", None))
    out_specs = P(("beams", "band"), "tm", None, None)
    return jax.shard_map(
        on_device, mesh=mesh, in_specs=in_specs, out_specs=out_specs, check_vma=False
    )
```

```python
import functools
import math

import jax
import jax.numpy as jnp
import ml_dtypes
import numpy as np
from jax import lax
from jax.experimental import pallas as pl
from jax.experimental.pallas import tpu as pltpu
from jax.sharding import PartitionSpec as P

CH_DEV = 64
LOGCD = 6
MAXD = 4
LANES = 128
SUBS = 8
RADIX = 256
LIMIT = 56 * 1024 * 1024
FUSED_LIMIT = 38 * 1024 * 1024
LAST_LIMIT = 14 * 1024 * 1024
AHEAD = 6
MESH = pl.DeviceIdType.MESH


def shifted(value, axis, steps):
    count = lax.axis_size(axis)
    first, last = (max(0, -steps), min(count, count - steps))
    return lax.ppermute(value, axis, [(source, source + steps) for source in range(first, last)])


def tree_kernel(sections, sizes, parts, has_rim, *refs):
    low_ref, high_ref, delay_ref, row_ref = refs[:4]
    xs, refs = refs[4 : 4 + len(parts)], refs[4 + len(parts) :]
    if has_rim:
        rim_ref, refs = refs[0], refs[1:]
    buf_a, buf_b = refs[-2:]
    outs = refs[len(refs) - 2 - len(sizes) : -2]
    rows, _, span = buf_a.shape
    tiles = span // LANES - 1
    lane = lax.broadcasted_iota(jnp.int32, (SUBS, LANES), 1)
    sub = lax.broadcasted_iota(jnp.int32, (SUBS, LANES), 0)

    @pl.loop(0, rows, unroll=4)
    def _(r):
        at = 0
        for x_ref, first in zip(xs, parts):
            count = x_ref.shape[2] - first
            buf_a[r, :, at : at + count] = x_ref[r, :, first:]
            at += count
        if has_rim:
            up = pltpu.roll(xs[0][r, :, 0:LANES], SUBS - 1, 0)
            buf_a[r, :, at : at + LANES] = jnp.where(sub == SUBS - 1, rim_ref[r], up)

    def merge(src, section, r, dst, at, count):
        a = low_ref[section, r]
        b = high_ref[section, r]
        d = delay_ref[section, r]
        turn = (LANES - d) & (LANES - 1)
        keep = lane < LANES - d
        turned = [
            pltpu.roll(src[b, :, i * LANES : (i + 1) * LANES], turn, 1) for i in range(tiles + 1)
        ]
        for i in range(count):
            later = turned[min(i + 1, tiles)]
            dst[at, :, i * LANES : (i + 1) * LANES] = src[
                a, :, i * LANES : (i + 1) * LANES
            ] + jnp.where(keep, turned[i], later)

    src, dst = buf_a, buf_b
    for section in range(sections - 1):

        @pl.loop(0, rows, unroll=16)
        def _(r, src=src, dst=dst, section=section):
            merge(src, section, r, dst, r, tiles + 1)

        src, dst = dst, src
    start = 0
    for size, out in zip(sizes, outs):

        @pl.loop(0, size, unroll=16)
        def _(i, start=start, src=src, out=out):
            merge(src, sections - 1, row_ref[start + i], out, i, tiles)

        start += size


def tree(xs, parts, rim, tables_of, sizes, width, span, place, so_far):
    rows = xs[0].shape[0]
    sections = tables_of[0].shape[0]
    smem = pl.BlockSpec(memory_space=pltpu.SMEM)
    vmem = pl.BlockSpec(memory_space=pltpu.VMEM)
    has_rim = rim is not None
    inputs = [*tables_of, *xs] + ([rim] if has_rim else [])
    known = len(inputs)
    return pl.pallas_call(
        functools.partial(tree_kernel, sections, sizes, parts, has_rim),
        grid=(1,),
        out_shape=[jax.ShapeDtypeStruct((size, SUBS, width), jnp.float32) for size in sizes],
        in_specs=[smem] * 4
        + [vmem] * (known - 4)
        + [pl.BlockSpec(memory_space=pl.ANY)] * len(so_far),
        out_specs=[pl.BlockSpec((size, SUBS, span), lambda i: (0, 0, place)) for size in sizes],
        input_output_aliases={known + i: i for i in range(len(so_far))},
        scratch_shapes=[pltpu.VMEM((rows, SUBS, span + LANES), jnp.float32)] * 2,
        compiler_params=pltpu.CompilerParams(vmem_limit_bytes=LIMIT),
        cost_estimate=pl.CostEstimate(
            flops=rows * SUBS * span * sections * 4,
            bytes_accessed=rows * SUBS * span * 8,
            transcendentals=0,
        ),
        name="tree",
    )(*inputs, *so_far)


def split(value):
    high = value.astype(jnp.bfloat16)
    return high, (value - high.astype(jnp.float32)).astype(jnp.bfloat16)


def fill_bands(row_of, zsel, high_ref, low_ref):
    for z in range(zsel):
        pair = []
        for part in range(2):
            wide = jnp.broadcast_to(row_of(z, part), (RADIX, RADIX))
            band = pltpu.roll(wide, 0, 1, stride=1, stride_axis=0)[:, :LANES]
            pair.append(split(band))
        at = 2 * z * LANES
        for ref, real, imag in (
            (high_ref, pair[0][0], pair[1][0]),
            (low_ref, pair[0][1], pair[1][1]),
        ):
            ref[:RADIX, at : at + LANES] = real
            ref[RADIX:, at : at + LANES] = -imag
            ref[:RADIX, at + LANES : at + 2 * LANES] = imag
            ref[RADIX:, at + LANES : at + 2 * LANES] = real


def bands_kernel(zsel, u_ref, high_ref, low_ref):
    def row_of(z, part):
        return u_ref[0, 2 * z + part : 2 * z + part + 1, :]

    fill_bands(row_of, zsel, high_ref.at[0], low_ref.at[0])


def reversed_taps(picks, template_bank):
    trials, zsel = picks.shape
    taps = template_bank.shape[2]
    onehot = (picks[:, :, None] == jnp.arange(template_bank.shape[1], dtype=jnp.int32)).astype(
        jnp.float32
    )
    reversed_bank = jnp.concatenate(
        [
            template_bank[:, :, :1],
            jnp.zeros(template_bank.shape[:2] + (RADIX - taps,), jnp.float32),
            template_bank[:, :, :0:-1],
        ],
        axis=2,
    )
    u = jnp.einsum("tzk,ckm->tzcm", onehot, reversed_bank, precision=lax.Precision.HIGHEST)
    return u.reshape(trials, 2 * zsel, RADIX)


def bands(picks, template_bank):
    trials, zsel = picks.shape
    u = reversed_taps(picks, template_bank)
    wide = 2 * zsel * LANES
    shape = jax.ShapeDtypeStruct((trials, 2 * RADIX, wide), jnp.bfloat16)
    spec = pl.BlockSpec((1, 2 * RADIX, wide), lambda t: (t, 0, 0))
    return pl.pallas_call(
        functools.partial(bands_kernel, zsel),
        grid=(trials,),
        out_shape=[shape, shape],
        in_specs=[pl.BlockSpec((1, 2 * zsel, RADIX), lambda t: (t, 0, 0))],
        out_specs=[spec, spec],
        compiler_params=pltpu.CompilerParams(vmem_limit_bytes=LIMIT),
        cost_estimate=pl.CostEstimate(
            flops=trials * RADIX * RADIX * 20,
            bytes_accessed=trials * 2 * RADIX * wide * 4,
            transcendentals=0,
        ),
        name="bands",
    )(u)


def tables(samples, channels, width, taps):
    cols = samples // RADIX
    outs = cols // 2
    split_by = width // cols if width % cols == 0 else 1
    place = np.arange(RADIX)
    row_of = split_by * (place % (RADIX // split_by)) + place // (RADIX // split_by)
    freq = (np.arange(RADIX) - taps // 2) % RADIX
    b = np.arange(cols)
    scale = 1.0 / math.sqrt(samples * channels)
    angle = 2.0 * np.pi / RADIX * (row_of[:, None] * freq[None, :] % RADIX)
    first = np.concatenate([np.cos(angle), -np.sin(angle)], axis=1) * scale
    angle = 2.0 * np.pi / samples * (b[:, None] * freq[None, :] % samples)
    tw_cos, tw_sin = np.cos(angle), np.sin(angle)
    angle = 2.0 * np.pi / cols * (np.arange(outs)[:, None] * b[None, :] % cols)
    second = np.concatenate([np.cos(angle), np.sin(angle)], axis=1)

    def parts(value):
        value = value.astype(np.float32)
        high = value.astype(ml_dtypes.bfloat16)
        return high, (value - high.astype(np.float32)).astype(ml_dtypes.bfloat16)

    return (
        *parts(first),
        tw_cos.astype(np.float32),
        tw_sin.astype(np.float32),
        *parts(second),
    )


def dot3(a_high, a_low, b_high, b_low):
    def dot(a, b):
        return jnp.dot(a, b, preferred_element_type=jnp.float32)

    return dot(a_high, b_high) + (dot(a_high, b_low) + dot(a_low, b_high))


def powers_of(x, band_high, band_low, consts, zsel, half_taps, store):
    fh, fl, tc, ts, sh, sl = consts
    cols = tc.shape[0]
    outs = cols // 2
    x_high, x_low = split(x.T)
    first = dot3(x_high, x_low, fh[...], fl[...])
    re, im = first[:, :RADIX], first[:, RADIX:]
    mid_re = re * tc[...] + im * ts[...]
    mid_im = im * tc[...] - re * ts[...]
    re_high, re_low = split(mid_re)
    im_high, im_low = split(mid_im)

    def block(a, b):
        return jnp.concatenate(
            [jnp.concatenate([a, b], axis=1), jnp.concatenate([b, -a], axis=1)], axis=0
        )

    spec = dot3(sh[...], sl[...], block(re_high, im_high), block(re_low, im_low))
    row = lax.broadcasted_iota(jnp.int32, (outs, RADIX), 0)
    lane = lax.broadcasted_iota(jnp.int32, (outs, RADIX), 1)
    even, odd = [], []
    for part in (spec[:, :RADIX], spec[:, RADIX:]):
        down = jnp.where(row == 0, 0.0, pltpu.roll(part, 1, 0))
        up = jnp.where(row == outs - 1, 0.0, pltpu.roll(part, outs - 1, 0))
        here = jnp.where(lane < half_taps, down, part)
        after = jnp.where(lane < half_taps, part, up)
        even.append(here)
        odd += [here[:, LANES:], after[:, :LANES]]
    window = jnp.concatenate(
        [jnp.concatenate(even, axis=1), jnp.concatenate(odd, axis=1)], axis=0
    )
    w_high, w_low = split(window)
    got = dot3(w_high, w_low, band_high, band_low)
    for z in range(zsel):
        at = 2 * z * LANES
        real, imag = got[:, at : at + LANES], got[:, at + LANES : at + 2 * LANES]
        power = real * real + imag * imag
        for e in range(2):
            store(pl.ds(e * zsel + z, outs, 2 * zsel), power[e * outs : (e + 1) * outs])


def spectra_kernel(zsel, half_taps, aliased, *refs):
    x_ref, bh_ref, bl_ref = refs[:3]
    consts = refs[3:9]
    out_ref, done_ref = refs[10:] if aliased else refs[9:]
    done_ref[...] = jnp.zeros_like(done_ref)
    cols = consts[2].shape[0]
    x = x_ref[...]
    x = x.reshape(-1, x.shape[-1])
    if x.shape[1] != cols:
        x = jnp.concatenate(
            [x[:, i * cols : (i + 1) * cols] for i in range(x.shape[1] // cols)], axis=0
        )

    def store(rows, value):
        out_ref[0, rows, :] = value

    powers_of(x, bh_ref[0], bl_ref[0], consts, zsel, half_taps, store)


def spectra(x, band_high, band_low, consts, zsel, taps, trials, first_trial, so_far):
    cols = consts[2].shape[0]
    outs = cols // 2
    rows = 2 * outs * zsel
    if x.shape[-1] % cols == 0:
        here = x.shape[1]
        x_spec = pl.BlockSpec((x.shape[0], 1, SUBS, x.shape[-1]), lambda t: (0, t, 0, 0))
    else:
        here = x.shape[1]
        x = x.transpose(1, 0, 2, 3).reshape(here, RADIX, cols)
        x_spec = pl.BlockSpec((1, RADIX, cols), lambda t: (t, 0, 0))
    band_spec = pl.BlockSpec(
        (1,) + band_high.shape[1:], lambda t: (first_trial + t, 0, 0)
    )
    whole = [pl.BlockSpec(c.shape, lambda t: (0, 0)) for c in consts]
    aliased = so_far is not None
    more = [so_far] if aliased else []
    macs = here * (cols * RADIX * 2 * RADIX + outs * 2 * cols * 2 * RADIX + 2 * outs * 4 * RADIX * RADIX)
    return pl.pallas_call(
        functools.partial(spectra_kernel, zsel, taps // 2, aliased),
        grid=(here,),
        out_shape=[
            jax.ShapeDtypeStruct((trials, rows, LANES), jnp.float32),
            jax.ShapeDtypeStruct((SUBS, LANES), jnp.float32),
        ],
        in_specs=[x_spec, band_spec, band_spec, *whole]
        + [pl.BlockSpec(memory_space=pl.ANY)] * len(more),
        out_specs=[
            pl.BlockSpec((1, rows, LANES), lambda t: (first_trial + t, 0, 0)),
            pl.BlockSpec((SUBS, LANES), lambda t: (0, 0)),
        ],
        input_output_aliases={9: 0} if aliased else {},
        compiler_params=pltpu.CompilerParams(vmem_limit_bytes=LIMIT),
        cost_estimate=pl.CostEstimate(
            flops=6 * macs, bytes_accessed=here * 2 * 1024 * 1024, transcendentals=0
        ),
        name="spectra",
    )(x, band_high, band_low, *consts, *more)


def after_kernel(value_ref, done_ref, out_ref):
    del value_ref, done_ref, out_ref


def after(value, done):
    anywhere = pl.BlockSpec(memory_space=pl.ANY)
    return pl.pallas_call(
        after_kernel,
        out_shape=jax.ShapeDtypeStruct(value.shape, value.dtype),
        in_specs=[anywhere, anywhere],
        out_specs=anywhere,
        input_output_aliases={0: 0},
        name="after",
    )(value, done)


def finish(out, trials, samples, zsel):
    out = out.reshape(trials, samples // 2 // LANES, zsel, LANES).transpose(0, 2, 1, 3)
    return out.reshape(1, trials, zsel, samples // 2)


def rim_pack(sections):
    return LANES >> (sections * MAXD - 1).bit_length()


def fused_kernel(
    nb, nt, sections, trials, zsel, taps,
    picks_hbm, delay_hbm, wanted_hbm, bank_ref, sig_ref, *refs
):
    const_refs, refs = refs[:6], refs[6:]
    power, got, band_high, band_low, refs = refs[0], refs[1:3], refs[3], refs[4], refs[5:]
    consts, sent, refs = refs[:6], refs[6:8], refs[8:]
    raw, rim, rim_sent, buf_a, buf_b, stage, refs = *refs[:6], refs[6:]
    bank, reverse, refs = *refs[:2], refs[2:]
    picks_ref, delay_ref, wanted_ref, refs = *refs[:3], refs[3:]
    (
        one_send, one_recv, two_send, two_recv, rim_sems, stage_sem, load_sems,
    ) = refs

    everyone = nb * nt
    rows, _, span = buf_a.shape
    span = span - LANES
    blocks = CH_DEV // SUBS
    tiles = span // LANES
    early = range(tiles + 1)
    late = range(tiles + 1, 2 * tiles)
    pack = rim_pack(sections)
    share = LANES // pack
    mt, mb = lax.axis_index("tm"), lax.axis_index("band")
    me = mt * nb + mb

    def device(e):
        return {"tm": e // nb, "band": e % nb}

    barrier = pltpu.get_barrier_semaphore()

    @pl.loop(1, everyone)
    def _(d):
        pl.semaphore_signal(
            barrier, 1, device_id=device((me + d) % everyone), device_id_type=MESH
        )

    pl.semaphore_wait(barrier, everyone - 1)

    def slab(i, k):
        return sig_ref.at[:, k, :, pl.ds(i * LANES, LANES)]

    def landed(ref, sem):
        pltpu.make_async_copy(ref, ref, sem).wait()

    def first(i, d):
        return pltpu.make_async_remote_copy(
            slab(i, (mb + d) % nb),
            raw.at[pl.ds(mb * blocks, blocks), i],
            one_send,
            one_recv.at[i],
            device_id={"band": (mb + d) % nb},
            device_id_type=MESH,
        )

    def first_own(i):
        return pltpu.make_async_copy(
            slab(i, mb), raw.at[pl.ds(mb * blocks, blocks), i], one_recv.at[i]
        )

    def first_wait(i):
        landed(raw.at[:, i], one_recv.at[i])

    apart = sorted(range(1, nb), key=lambda d: -min(d, nb - d))
    for i in (*early, *late):
        for d in apart:
            first(i, d).start()
        first_own(i).start()
    loads = [
        pltpu.make_async_copy(a, b, load_sems.at[i])
        for i, (a, b) in enumerate(zip(
            (bank_ref, picks_hbm, delay_hbm, wanted_hbm, *const_refs),
            (bank, picks_ref, delay_ref, wanted_ref, *consts),
        ))
    ]
    for load in loads:
        load.start()

    for load in loads[:4]:
        load.wait()
    turn_row = lax.broadcasted_iota(jnp.int32, (taps, RADIX), 0)
    turn_lane = lax.broadcasted_iota(jnp.int32, (taps, RADIX), 1)
    turned_to = jnp.where((turn_row + turn_lane) % RADIX == 0, 1.0, 0.0).astype(jnp.float32)
    for part in range(2):
        reverse[part] = lax.dot_general(
            bank[part],
            turned_to,
            (((0,), (0,)), ((), ())),
            precision=lax.Precision.HIGHEST,
            preferred_element_type=jnp.float32,
        )

    lane = lax.broadcasted_iota(jnp.int32, (SUBS, LANES), 1)
    sub = lax.broadcasted_iota(jnp.int32, (SUBS, LANES), 0)

    def merge(src, section, r, dst, at, count):
        half = 1 << section
        base = r - r % (2 * half) + r % half - r % min(half, CH_DEV)
        a = base + picks_ref[0, section, r]
        b = base + half + picks_ref[1, section, r]
        d = delay_ref[section, r]
        turn = (LANES - d) & (LANES - 1)
        keep = lane < LANES - d
        turned = [
            pltpu.roll(src[b, :, i * LANES : (i + 1) * LANES], turn, 1) for i in range(tiles + 1)
        ]
        for i in range(count):
            later = turned[min(i + 1, tiles)]
            dst[at, :, i * LANES : (i + 1) * LANES] = src[
                a, :, i * LANES : (i + 1) * LANES
            ] + jnp.where(keep, turned[i], later)

    def tree_part(c):
        @pl.loop(0, nb * blocks)
        def _(q):
            for ch in range(SUBS):
                r = q * SUBS + ch
                rows_of = pl.ds(ch, SUBS, stride=SUBS)
                for i in range(tiles + 1 - c):
                    buf_a[r, :, i * LANES : (i + 1) * LANES] = raw[q, c * tiles + i, rows_of, :]
                if c == 1:
                    edges = pltpu.roll(rim[q // pack], (LANES - (q % pack) * share) % LANES, 1)
                    up = pltpu.roll(raw[q, 0, rows_of, :], SUBS - 1, 0)
                    edge = jnp.broadcast_to(edges[ch : ch + 1], (SUBS, LANES))
                    buf_a[r, :, span:] = jnp.where(sub == SUBS - 1, edge, up)

        src, dst = buf_a, buf_b
        for section in range(sections - 1):

            @pl.loop(0, rows, unroll=16)
            def _(r, src=src, dst=dst, section=section):
                merge(src, section, r, dst, r, tiles + 1)

            src, dst = dst, src

        @pl.loop(0, everyone)
        def _(e):
            start = (e % nb) * CH_DEV + (e // nb) * trials

            @pl.loop(0, trials, unroll=trials)
            def _(i):
                merge(src, sections - 1, start + i, stage.at[e], i, tiles)

        copy = pltpu.make_async_copy(stage, sent[c], stage_sem)
        copy.start()
        copy.wait()

    def part_of(c, t):
        return (pl.ds(t, 1), 1 + t) if c else (slice(None), 0)

    def second(c, t, e):
        which, at = part_of(c, t)
        return pltpu.make_async_remote_copy(
            sent[c].at[e, which],
            got[c].at[me, which],
            two_send.at[c],
            two_recv.at[at],
            device_id=device(e),
            device_id_type=MESH,
        )

    def send_second(c, t):
        @pl.loop(0, (nb - 1) * nt)
        def _(i):
            b = (mb + 1 + (i // nt + nb // 2 - 1) % (nb - 1)) % nb
            second(c, t, ((mt + i) % nt) * nb + b).start()

        @pl.loop(1, nt)
        def _(i):
            second(c, t, ((mt + i) % nt) * nb + mb).start()

        which, at = part_of(c, t)
        pltpu.make_async_copy(
            sent[c].at[me, which], got[c].at[me, which], two_recv.at[at]
        ).start()

    def wait_second(c, t):
        which, at = part_of(c, t)
        landed(got[c].at[:, which], two_recv.at[at])

    first_wait(0)

    @pl.loop(0, nb * blocks // pack)
    def _(q):
        packed = raw[q * pack, 0, :SUBS, :]
        for p in range(1, pack):
            moved = pltpu.roll(raw[q * pack + p, 0, :SUBS, :], p * share, 1)
            packed = jnp.where(lane < p * share, packed, moved)
        rim_sent[q] = packed

    rim_copy = pltpu.make_async_remote_copy(
        rim_sent,
        rim,
        rim_sems.at[0],
        rim_sems.at[1],
        device_id=device((me + everyone - 1) % everyone),
        device_id_type=MESH,
    )

    @pl.when(me > 0)
    def _():
        rim_copy.start()

    for i in early[1:]:
        first_wait(i)

    @pl.when(me == everyone - 1)
    def _():
        rim[...] = jnp.zeros_like(rim)

    tree_part(0)
    send_second(0, 0)
    for i in late:
        first_wait(i)

    @pl.when(me < everyone - 1)
    def _():
        rim_copy.wait_recv()

    tree_part(1)
    for t in range(min(AHEAD, trials)):
        send_second(1, t)
    landed(raw.at[pl.ds(0, (nb - 1) * blocks)], one_send)

    @pl.when(me > 0)
    def _():
        rim_copy.wait_send()

    for load in loads[4:]:
        load.wait()
    wait_second(0, 0)

    def bands_of(t):
        def row(z, part):
            return reverse[part, pl.ds(wanted_ref[z, t], 1), :]

        fill_bands(row, zsel, band_high, band_low)

    last = trials - 1

    @pl.loop(0, last)
    def _(t):
        bands_of(t)
        wait_second(1, t)

        @pl.when(t + AHEAD < trials)
        def _():
            send_second(1, t + AHEAD)

        def store(where, value):
            power[t, where, :] = value

        x = assemble([got[c][:, t] for c in range(2)], consts)
        powers_of(x, band_high[...], band_low[...], consts, zsel, taps // 2, store)

    bands_of(last)
    wait_second(1, last)
    for c in range(2):
        landed(sent[c].at[pl.ds(0, everyone - 1)], two_send.at[c])


def assemble(parts, consts):
    cols = consts[2].shape[0]
    parts = [part.reshape(-1, part.shape[-1]) for part in parts]
    return jnp.concatenate(
        [part[:, i : i + cols] for part in parts for i in range(0, part.shape[1], cols)], axis=0
    )


def last_kernel(zsel, half_taps, *refs):
    done_ref, got, (band_high, band_low) = refs[0], refs[1:3], refs[3:5]
    consts, out_ref, power, move_sem, sem = refs[5:11], *refs[11:]
    count = done_ref.shape[0]
    move = pltpu.make_async_copy(done_ref, out_ref.at[pl.ds(0, count)], move_sem)
    move.start()
    x = assemble([ref[:, count] for ref in got], consts)

    def store(where, value):
        power[where, :] = value

    powers_of(x, band_high[...], band_low[...], consts, zsel, half_taps, store)
    final = pltpu.make_async_copy(power, out_ref.at[count], sem)
    final.start()
    move.wait()
    final.wait()


def fused(signal, picks, delays, template_bank, wanted, consts, zsel, taps, nb, nt):
    sections = picks.shape[1]
    channels = CH_DEV * nb
    everyone = nb * nt
    trials = CH_DEV // nt
    slab = signal.shape[1] // nb
    width = slab // SUBS
    span = width // 2
    blocks = CH_DEV // SUBS
    cols = consts[2].shape[0]
    outs = cols // 2
    rows = 2 * outs * zsel
    wide = 2 * zsel * LANES
    view = signal.reshape(blocks, SUBS, nb * SUBS, width).transpose(0, 2, 1, 3)
    view = view.reshape(blocks, nb, SUBS * SUBS, width)
    bank = template_bank.transpose(0, 2, 1)
    anywhere = pl.BlockSpec(memory_space=pl.ANY)
    dma = pltpu.SemaphoreType.DMA
    f32, bf16 = jnp.float32, jnp.bfloat16
    macs = cols * RADIX * 2 * RADIX + outs * 2 * cols * 2 * RADIX + 2 * outs * 4 * RADIX * RADIX
    exchanged = (everyone, trials, SUBS, span)
    kept = [
        pltpu.VMEM((trials - 1, rows, LANES), f32),
        *[pltpu.VMEM(exchanged, f32)] * 2,
        *[pltpu.VMEM((2 * RADIX, wide), bf16)] * 2,
        *[pltpu.VMEM(c.shape, c.dtype) for c in consts],
    ]
    vmem = pl.BlockSpec(memory_space=pltpu.VMEM)
    *handed, _, _ = pl.pallas_call(
        functools.partial(fused_kernel, nb, nt, sections, trials, zsel, taps),
        out_shape=kept + [jax.ShapeDtypeStruct(exchanged, f32)] * 2,
        in_specs=[anywhere] * 11,
        out_specs=[vmem] * len(kept) + [anywhere] * 2,
        scratch_shapes=[
            pltpu.VMEM((nb * blocks, width // LANES, SUBS * SUBS, LANES), f32),
            *[pltpu.VMEM((nb * blocks // rim_pack(sections), SUBS, LANES), f32)] * 2,
            pltpu.VMEM((channels, SUBS, span + LANES), f32),
            pltpu.VMEM((channels, SUBS, span + LANES), f32),
            pltpu.VMEM(exchanged, f32),
            pltpu.VMEM(bank.shape, f32),
            pltpu.VMEM(template_bank.shape[:2] + (RADIX,), f32),
            *[pltpu.SMEM(a.shape, jnp.int32) for a in (picks, delays, wanted.T)],
            dma,
            dma((width // LANES,)),
            dma((2,)),
            dma((1 + trials,)),
            dma((2,)),
            dma,
            dma((4 + len(consts),)),
        ],
        compiler_params=pltpu.CompilerParams(
            collective_id=0, has_side_effects=True, vmem_limit_bytes=FUSED_LIMIT
        ),
        cost_estimate=pl.CostEstimate(
            flops=6 * trials * macs, bytes_accessed=3 * signal.size * 4, transcendentals=0
        ),
        name="fused",
    )(picks, delays, wanted.T, bank, view, *consts)
    return pl.pallas_call(
        functools.partial(last_kernel, zsel, taps // 2),
        out_shape=jax.ShapeDtypeStruct((trials, rows, LANES), f32),
        in_specs=[vmem] * len(kept),
        out_specs=anywhere,
        scratch_shapes=[pltpu.VMEM((rows, LANES), f32), dma, dma],
        compiler_params=pltpu.CompilerParams(vmem_limit_bytes=LAST_LIMIT),
        cost_estimate=pl.CostEstimate(
            flops=6 * macs, bytes_accessed=signal.size * 4, transcendentals=0
        ),
        name="last",
    )(*handed)


def on_device(signal, tree_picks, tree_delays, template_bank, template_pick):
    band_count = lax.axis_size("band")
    time_count = lax.axis_size("tm")
    everyone = band_count * time_count
    sections = LOGCD + band_count.bit_length() - 1
    rim_depth = sections * MAXD
    channels = CH_DEV * band_count
    samples = signal.shape[1] * time_count
    slab = signal.shape[1] // band_count
    width = slab // SUBS
    trials = CH_DEV // time_count
    last = max(1, 3 * trials // 16)
    counts = [count for count in (trials - last, last) if count]
    zsel = template_pick.shape[2]
    taps = template_bank.shape[2]
    cols = samples // RADIX
    if width % (2 * cols) == 0 and trials % 2 == 0 and trials >= 4:
        consts = [jnp.asarray(c) for c in tables(samples, channels, width, taps)]
        out = fused(
            signal, tree_picks, tree_delays, template_bank, template_pick[0], consts, zsel, taps,
            band_count, time_count,
        )
        return finish(out, trials, samples, zsel)

    band_high, band_low = bands(template_pick[0], template_bank)

    half = (1 << np.arange(sections))[:, None]
    r = np.arange(channels)[None, :]
    base = r - r % (2 * half) + r % half - r % np.minimum(half, CH_DEV)
    low = tree_picks[0] + base.astype(np.int32)
    high = tree_picks[1] + (base + half).astype(np.int32)
    grid = np.arange(channels).reshape(band_count, time_count, trials).transpose(1, 0, 2)
    firsts = [sum(counts[:q]) for q in range(len(counts))]
    order = np.concatenate(
        [grid[:, :, first : first + count].reshape(-1) for first, count in zip(firsts, counts)]
    ).astype(np.int32)
    tables_of = (low, high, tree_delays, jnp.asarray(order))
    sizes = [everyone * count for count in counts]

    folded = signal.reshape(CH_DEV, band_count, SUBS, width)

    def exchanged(value):
        value = lax.all_to_all(value, "band", split_axis=0, concat_axis=0, tiled=True)
        return value.reshape(channels, SUBS, -1)

    def rim_of(x):
        rim = shifted(x[:, 0, :rim_depth], ("tm", "band"), -1)
        rim = jnp.pad(rim, ((0, 0), (0, LANES - rim_depth)))
        return jnp.broadcast_to(rim[:, None, :], (channels, SUBS, LANES))

    if width % (2 * LANES) == 0:
        span = width // 2
        cut = span + LANES
        x_a = exchanged(folded[..., :cut].transpose(1, 0, 2, 3))
        x_b = after(after(folded[..., cut:].transpose(1, 0, 2, 3), x_a), band_low)
        x_b = exchanged(x_b)
        pieces = tree([x_a], [0], None, tables_of, sizes, width, span, 0, [])
        pieces = tree(
            [x_a, x_b], [span, 0], rim_of(x_a), tables_of, sizes, width, span, 1, pieces
        )
    else:
        x = exchanged(folded.transpose(1, 0, 2, 3))
        pieces = tree([x], [0], rim_of(x), tables_of, sizes, width, width, 0, [])

    consts = [jnp.asarray(c) for c in tables(samples, channels, width, taps)]
    out = None
    for first, count, piece in zip(firsts, counts, pieces):
        piece = piece.reshape(everyone, count, SUBS, width)
        if out is not None:
            piece = after(piece, arrived)
        arrived = lax.all_to_all(piece, ("tm", "band"), split_axis=0, concat_axis=0, tiled=True)
        out, _ = spectra(
            arrived, band_high, band_low, consts, zsel, taps, trials, first, out
        )
    return finish(out, trials, samples, zsel)


def solution(mesh):
    in_specs = (P(("beams", "band"), "tm"), P(), P(), P(), P(("beams", "band"), "tm", None))
    out_specs = P(("beams", "band"), "tm", None, None)
    return jax.shard_map(
        on_device, mesh=mesh, in_specs=in_specs, out_specs=out_specs, check_vma=False
    )
```
